128 devices in a mesh: section: 2 (over core), ctx: 16 (over z, x), fsdp: 4 (over y).
Axes of the slice: x: 4, y: 4, z: 4, core: 2. Of those that a mesh axis runs over, the one named last changes fastest.
Arguments:
- tokens: bfloat16 [8, 1024, 768], P('fsdp', 'ctx'), may hold values from -6 to 6
- cotangent: float32 [8, 1024, 768], P('fsdp', 'ctx'), may hold values from -6 to 6
- block_order: int32 [32], replicated, may hold values from 0 to 31, as said below
- first_gain: bfloat16 [2, 768], P('section', 'fsdp'), may hold values from 0.5 to 1.5
- first_shift: bfloat16 [2, 768], P('section', 'fsdp'), may hold values from -1.25 to 1.25
- w_query: bfloat16 [2, 768, 768], P('section', 'fsdp'), may hold values from -0.21875 to 0.21875
- b_query: bfloat16 [2, 768], P('section', 'fsdp'), may hold values from -1.25 to 1.25
- w_key: bfloat16 [2, 768, 768], P('section', 'fsdp'), may hold values from -0.21875 to 0.21875
- w_value: bfloat16 [2, 768, 768], P('section', 'fsdp'), may hold values from -0.21875 to 0.21875
- b_value: bfloat16 [2, 768], P('section', 'fsdp'), may hold values from -1.25 to 1.25
- w_out: bfloat16 [2, 768, 768], P('section', 'fsdp'), may hold values from -3.5 to 3.5
- b_out: bfloat16 [2, 768], P('section', 'fsdp'), may hold values from -1.25 to 1.25
- second_gain: bfloat16 [2, 768], P('section', 'fsdp'), may hold values from 0.5 to 1.5
- second_shift: bfloat16 [2, 768], P('section', 'fsdp'), may hold values from -1.25 to 1.25
- w_expand: bfloat16 [2, 768, 3072], P('section', 'fsdp'), may hold values from -0.21875 to 0.21875
- b_expand: bfloat16 [2, 3072], P('section', 'fsdp'), may hold values from -1.25 to 1.25
- w_reduce: bfloat16 [2, 3072, 768], P('section', 'fsdp'), may hold values from -0.21875 to 0.21875
- b_reduce: bfloat16 [2, 768], P('section', 'fsdp'), may hold values from -1.25 to 1.25
Outputs:
- layer_outputs: bfloat16 [2, 8, 1024, 768], P('section', 'fsdp', 'ctx')
- input_grads: float32 [2, 8, 1024, 768], P('section', 'fsdp', 'ctx')
- grad_first_gain: float32 [2, 768], P('section', 'fsdp')
- grad_first_shift: float32 [2, 768], P('section', 'fsdp')
- grad_w_query: float32 [2, 768, 768], P('section', 'fsdp')
- grad_b_query: float32 [2, 768], P('section', 'fsdp')
- grad_w_key: float32 [2, 768, 768], P('section', 'fsdp')
- grad_w_value: float32 [2, 768, 768], P('section', 'fsdp')
- grad_b_value: float32 [2, 768], P('section', 'fsdp')
- grad_w_out: float32 [2, 768, 768], P('section', 'fsdp')
- grad_b_out: float32 [2, 768], P('section', 'fsdp')
- grad_second_gain: float32 [2, 768], P('section', 'fsdp')
- grad_second_shift: float32 [2, 768], P('section', 'fsdp')
- grad_w_expand: float32 [2, 768, 3072], P('section', 'fsdp')
- grad_b_expand: float32 [2, 3072], P('section', 'fsdp')
- grad_w_reduce: float32 [2, 3072, 768], P('section', 'fsdp')
- grad_b_reduce: float32 [2, 768], P('section', 'fsdp')
The draws below stay inside these ranges and needn't reach their ends.
Inputs may be any that keep to these rules, and one draw needn't show every extreme that they name: `block_order`: a permutation of 0 to 31 in which entries 2c and 2c + 1 are b and 31 - b for some b, for every c.
All inputs are finite; a program needn't handle non-finite values.
Results may differ from the reference program's by a relative error of at most 0.025.
Values may be sent and summed in bfloat16 or wider, within the bound.
A program may use at most 192 MiB of HBM per device.

```python
import jax
import jax.numpy as jnp
from jax import lax

D = 768
H = 12
HEAD = 64
FF = 3072
SEQ_LEN = 1024
SEQS = 8
BLOCKS = 32
BLOCK = 32


def draw_block_order(key, part):
    key = jax.random.fold_in(key, 7)
    pair_key, flip_key = jax.random.split(key)
    half = BLOCKS // 2
    pairs = jax.random.permutation(pair_key, half).astype(jnp.int32)
    flips = jax.random.randint(flip_key, (half,), 0, 2).astype(jnp.int32)
    first = jnp.where(flips == 1, BLOCKS - 1 - pairs, pairs)
    second = BLOCKS - 1 - first
    return jnp.stack([first, second], axis=1).reshape(BLOCKS).astype(jnp.int32)


def shard_levels(stream_key, shape, pieces, low, high):
    def one(position, parts):
        steps = jax.random.uniform(jax.random.fold_in(jax.random.fold_in(stream_key, 6), position), (parts,), jnp.float32, low / len(pieces), high / len(pieces))
        return jnp.repeat(jnp.exp(steps), shape[position] // parts).reshape((-1,) + (1,) * (len(shape) - position - 1))

    loudness = one(*pieces[0])
    for cut in pieces[1:]:
        loudness = loudness * one(*cut)
    return loudness


def scatter_about(key, extent, deviation, limit, shards=(), held_as=jnp.bfloat16):
    drawn = jax.random.normal(key, extent, jnp.float32) * deviation
    if len(shards) > 0:
        drawn = shard_levels(key, extent, shards, -0.22, 0.18) * drawn
    return jnp.clip(drawn, min=-limit, max=limit).astype(held_as)


def setup_inputs(seed: int = 0) -> dict:
    key_list = jax.random.split(jax.random.key(seed), 19)
    tokens = scatter_about(key_list[0], (SEQS, SEQ_LEN, D), 1.0, 6.0, ((0, 4), (1, 16)))
    cotangent = scatter_about(key_list[1], (SEQS, SEQ_LEN, D), 1.0, 6.0, ((0, 4), (1, 16)), jnp.float32)
    block_order = draw_block_order(jax.random.fold_in(key_list[18], 71), 0)
    first_gain = jnp.clip(1.0 + 0.1 * jax.random.normal(key_list[3], (2, D), jnp.float32), 0.5, 1.5).astype(jnp.bfloat16)
    first_shift = scatter_about(key_list[4], (2, D), 0.2, 1.25, ((0, 2), (1, 4)))
    w_query = scatter_about(key_list[5], (2, D, D), D ** -0.5, 0.21875, ((0, 2), (1, 4)))
    b_query = scatter_about(key_list[6], (2, D), 0.2, 1.25, ((0, 2), (1, 4)))
    w_key = scatter_about(key_list[7], (2, D, D), D ** -0.5, 0.21875, ((0, 2), (1, 4)))
    w_value = scatter_about(key_list[8], (2, D, D), D ** -0.5, 0.21875, ((0, 2), (1, 4)))
    b_value = scatter_about(key_list[9], (2, D), 0.2, 1.25, ((0, 2), (1, 4)))
    w_out = scatter_about(key_list[10], (2, D, D), (max(1, 4 * D // SEQ_LEN)) ** -0.5, 3.5, ((0, 2), (1, 4)))
    b_out = scatter_about(key_list[11], (2, D), 0.2, 1.25, ((0, 2), (1, 4)))
    second_gain = jnp.clip(1.0 + 0.1 * jax.random.normal(key_list[12], (2, D), jnp.float32), 0.5, 1.5).astype(jnp.bfloat16)
    second_shift = scatter_about(key_list[13], (2, D), 0.2, 1.25, ((0, 2), (1, 4)))
    w_expand = scatter_about(key_list[14], (2, D, FF), D ** -0.5, 0.21875, ((0, 2), (1, 4)))
    b_expand = scatter_about(key_list[15], (2, FF), 0.2, 1.25, ((0, 2), (1, 4)))
    w_reduce = scatter_about(key_list[16], (2, FF, D), (FF // 4) ** -0.5, 0.21875, ((0, 2), (1, 4)))
    b_reduce = scatter_about(key_list[17], (2, D), 0.2, 1.25, ((0, 2), (1, 4)))
    return {"tokens": tokens, "cotangent": cotangent, "block_order": block_order, "first_gain": first_gain, "first_shift": first_shift, "w_query": w_query, "b_query": b_query, "w_key": w_key, "w_value": w_value, "b_value": b_value, "w_out": w_out, "b_out": b_out, "second_gain": second_gain, "second_shift": second_shift, "w_expand": w_expand, "b_expand": b_expand, "w_reduce": w_reduce, "b_reduce": b_reduce}


@jax.custom_vjp
def low(v):
    return lax.optimization_barrier(v.astype(jnp.bfloat16)).astype(jnp.float32)

@jax.custom_vjp
def low_back(v):
    return v

def low_keep(v):
    return (low(v), None)

def low_pass(kept, grad):
    return (grad,)

def back_keep(v):
    return (v, None)

def back_low(kept, grad):
    return (low(grad),)
low.defvjp(low_keep, low_pass)
low_back.defvjp(back_keep, back_low)
EPSILON = 1e-05
HIGHEST = lax.Precision.HIGHEST

def layer_norm(values, gain, shift):
    average = lax.optimization_barrier(jnp.mean(values, axis=-1, keepdims=True))
    centered = values - average
    variance = lax.optimization_barrier(jnp.mean(centered * centered, axis=-1, keepdims=True))
    return centered * lax.rsqrt(variance + EPSILON) * gain + shift

def product(left, right):
    return jnp.dot(left, right, precision=HIGHEST)

def attend_block(query, keys, values, query_pos, key_pos):
    scores = low_back(jnp.einsum('qhd,khd->hqk', query, keys, precision=HIGHEST))
    allowed = key_pos[None, None, :] <= query_pos[None, :, None]
    scores = jnp.where(allowed, scores, -1e+30)
    highest = lax.optimization_barrier(jnp.max(scores, axis=-1, keepdims=True))
    raised = jnp.exp(scores - highest)
    probs = low(raised / lax.optimization_barrier(jnp.sum(raised, axis=-1, keepdims=True)))
    return jnp.einsum('hqk,khd->qhd', probs, values, precision=HIGHEST)

def attend_sequence(query, keys, values, positions):
    rows = min(512, SEQ_LEN)
    query_blocks = query.reshape(SEQ_LEN // rows, rows, H, HEAD)
    position_blocks = positions.reshape(SEQ_LEN // rows, rows)
    key_heads = keys.reshape(SEQ_LEN, H, HEAD)
    value_heads = values.reshape(SEQ_LEN, H, HEAD)
    step_fn = jax.checkpoint(lambda pair: attend_block(pair[0], key_heads, value_heads, pair[1], positions))
    mixed = lax.map(step_fn, (query_blocks, position_blocks))
    return mixed.reshape(SEQ_LEN, D)

def layer(inputs, params, positions):
    first_gain, first_shift, w_query, b_query, w_key, w_value, b_value, w_out, b_out, second_gain, second_shift, w_expand, b_expand, w_reduce, b_reduce = params
    normed = low(layer_norm(inputs, first_gain, first_shift))
    query = low(low_back((product(normed, w_query) + b_query) * 0.125))
    keys = low(low_back(product(normed, w_key)))
    values = low(low_back(product(normed, w_value) + b_value))
    mixed = lax.map(lambda triple: attend_sequence(triple[0], triple[1], triple[2], positions), (query, keys, values))
    mixed = low(low_back(mixed))
    hidden = inputs + low_back(product(mixed, w_out) + b_out)
    normed_two = low(layer_norm(hidden, second_gain, second_shift))
    before = low_back(product(normed_two, w_expand) + b_expand)
    active = low(jax.nn.gelu(before))
    return hidden + low_back(product(active, w_reduce) + b_reduce)

def reference(tokens, cotangent, block_order, first_gain, first_shift, w_query, b_query, w_key, w_value, b_value, w_out, b_out, second_gain, second_shift, w_expand, b_expand, w_reduce, b_reduce):
    positions = (jnp.repeat(block_order, BLOCK) * BLOCK + jnp.tile(jnp.arange(BLOCK, dtype=jnp.int32), BLOCKS)).astype(jnp.int32)
    weights = [first_gain, first_shift, w_query, b_query, w_key, w_value, b_value, w_out, b_out, second_gain, second_shift, w_expand, b_expand, w_reduce, b_reduce]
    floats = [piece.astype(jnp.float32) for piece in weights]
    params_zero = [piece[0] for piece in floats]
    params_one = [piece[1] for piece in floats]
    inputs = tokens.astype(jnp.float32)
    joint = jnp.zeros_like(inputs)

    def run(start, joined, layer_zero, layer_one):
        first = layer(start, layer_zero, positions)
        passed = low_back(low(first)) + joined
        second = layer(passed, layer_one, positions)
        return (first, second)
    (first, second), pullback = jax.vjp(run, inputs, joint, params_zero, params_one)
    grad_start, grad_joint, grads_zero, grads_one = pullback((jnp.zeros_like(first), cotangent.astype(jnp.float32)))
    stacked = [jnp.stack([earlier, later]) for earlier, later in zip(grads_zero, grads_one)]
    layer_outputs = jnp.stack([first, second]).astype(jnp.bfloat16)
    input_grads = jnp.stack([grad_start, grad_joint])
    return (layer_outputs, input_grads, stacked[0], stacked[1], stacked[2], stacked[3], stacked[4], stacked[5], stacked[6], stacked[7], stacked[8], stacked[9], stacked[10], stacked[11], stacked[12], stacked[13], stacked[14])
```

```python
import functools

import jax
import jax.numpy as jnp
from jax import lax
from jax.experimental import pallas as pl
from jax.experimental.pallas import tpu as pltpu
from jax.sharding import PartitionSpec as P

HEAD = 64
EPSILON = 1e-05
F32 = jnp.float32
BF16 = jnp.bfloat16
MESH = pl.DeviceIdType.MESH
GELU_SCALE = 0.7978845608028654
GELU_CUBE = 0.044715


def mm(left, right):
    return jnp.dot(left, right, preferred_element_type=F32)


def mm_nt(left, right):
    return lax.dot_general(left, right, (((1,), (1,)), ((), ())), preferred_element_type=F32)


def mm_tn(left, right):
    return lax.dot_general(left, right, (((0,), (0,)), ((), ())), preferred_element_type=F32)


def normalize(values):
    average = jnp.mean(values, axis=-1, keepdims=True)
    centered = values - average
    variance = jnp.mean(centered * centered, axis=-1, keepdims=True)
    factor = lax.rsqrt(variance + EPSILON)
    return centered * factor, factor


def norm_back(grad, normal, factor, gain):
    scaled = grad * gain
    return factor * (
        scaled
        - jnp.mean(scaled, axis=-1, keepdims=True)
        - normal * jnp.mean(scaled * normal, axis=-1, keepdims=True)
    )


def column_sums(values):
    return jnp.sum(values.astype(F32), axis=0, keepdims=True)


def kernel(
    N, S, R, D, F,
    tok, cot, wqkv_in, wout_in, wexp_in, wred_in, vecs_in, biases, qpos, kpos,
    out_y, out_dx, out_wqkv, out_wout, out_wexp, out_wred, out_small,
    u_in, cot_in, gp_in, y_low, dx_buf, dx_low, vecs,
    w3, wexp, n1, n2, g_all, ga_all, gb_all, active, slope,
    q_all, kv, probs, mixed, gm_all, dq_all, dk_all, dv_all, dkv_send, dkv_recv,
    part_send, part_recv, own, hidden, grad,
    ff1s, ff1r, ff2, ff3, aq1s, aq1r, aq2, aq3, ao1s, ao1r, ao2, ao3,
    sm_y, sm_x, sm_z, sm_own,
    ssem, rsem, lsem,
):
    T = S * R
    DH = D // N
    heads = DH // HEAD
    s = lax.axis_index("section")
    c = lax.axis_index("ctx")
    y = lax.axis_index("fsdp")
    x = lax.rem(c, N)
    z = lax.div(c, N)
    straight = y == z
    order = tuple(sorted(range(1, N), key=lambda d: min(d, N - d)))

    def near(v, d):
        return lax.rem(v + d, N)

    counter = [0]

    def block_of(count=N):
        counter[0] += count
        return counter[0] - count

    drains = []

    def start(src, dst, send, recv, device):
        copy = pltpu.make_async_remote_copy(
            src_ref=src, dst_ref=dst, send_sem=ssem.at[send], recv_sem=rsem.at[recv],
            device_id=device, device_id_type=MESH,
        )
        copy.start()
        drains.append((None, copy))

    def start_if(condition, src, dst, send, recv, device):
        copy = pltpu.make_async_remote_copy(
            src_ref=src, dst_ref=dst, send_sem=ssem.at[send], recv_sem=rsem.at[recv],
            device_id=device, device_id_type=MESH,
        )
        pl.when(condition)(lambda: copy.start())
        drains.append((condition, copy))

    def landed(dst, recv):
        pltpu.make_async_remote_copy(
            src_ref=dst, dst_ref=dst, send_sem=ssem.at[0], recv_sem=rsem.at[recv],
            device_id={"section": 1 - s}, device_id_type=MESH,
        ).wait_recv()

    def along(axis, index):
        if axis == "y":
            return {"fsdp": index}
        if axis == "x":
            return {"ctx": z * N + index}
        return {"ctx": index * N + x}

    place = {"x": x, "y": y, "z": z}

    def spread(axis, ref, base):
        me = place[axis]
        for d in order:
            start(ref.at[me], ref.at[me], base + d, base + me, along(axis, near(me, d)))

    def arrived(axis, ref, base, d):
        source = near(place[axis], d)
        landed(ref.at[source], base + source)

    def deal(axis, src, dst, base, d):
        me = place[axis]
        other = near(me, d)
        start(src.at[other], dst.at[me], base + d, base + me, along(axis, other))

    barrier = pltpu.get_barrier_semaphore()
    met = 0
    for dx in range(N):
        for dy in range(N):
            if dx or dy:
                pl.semaphore_signal(
                    barrier, inc=1, device_id={"ctx": z * N + near(x, dx), "fsdp": near(y, dy)},
                    device_id_type=MESH,
                )
                met += 1
    for dz in range(1, N):
        pl.semaphore_signal(
            barrier, inc=1, device_id={"ctx": near(z, dz) * N + x}, device_id_type=MESH
        )
        met += 1
    pl.semaphore_signal(barrier, inc=1, device_id={"section": 1 - s}, device_id_type=MESH)
    met += 1
    partner = {"ctx": y * N + x, "fsdp": z}

    @pl.when(jnp.logical_not(straight))
    def _():
        pl.semaphore_signal(barrier, inc=1, device_id=partner, device_id_type=MESH)
        pl.semaphore_wait(barrier, met + 1)

    @pl.when(straight)
    def _():
        pl.semaphore_wait(barrier, met)

    turned = jnp.logical_not(straight)

    k_u, k_cot, k_gp, k_y, k_dx = (block_of(1) for _ in range(5))
    start_if(jnp.logical_and(s == 0, turned), tok, u_in, k_u, k_u, partner)

    @pl.when(jnp.logical_and(s == 0, straight))
    def _():
        u_in[...] = tok[...]

    k_vecs = block_of()
    vecs[y] = vecs_in[...]
    spread("y", vecs, k_vecs)
    k_w3 = block_of()
    own_w3 = pltpu.make_async_copy(wqkv_in.at[y], w3.at[y], lsem.at[0])
    own_w3.start()
    for d in order:
        deal("y", wqkv_in, w3, k_w3, d)
    k_wexp = block_of()
    own_wexp = pltpu.make_async_copy(
        wexp_in.at[:, pl.ds(pl.multiple_of(y * F, 128), F)], wexp.at[y], lsem.at[1]
    )
    own_wexp.start()
    for d in order:
        other = near(y, d)
        start(
            wexp_in.at[:, pl.ds(pl.multiple_of(other * F, 128), F)], wexp.at[y],
            k_wexp + d, k_wexp + y, along("y", other),
        )
    start_if(jnp.logical_and(s == 1, turned), cot, cot_in, k_cot, k_cot, partner)

    @pl.when(jnp.logical_and(s == 1, straight))
    def _():
        cot_in[...] = cot[...]

    for d in order:
        arrived("y", vecs, k_vecs, d)
    params = vecs[0]
    for other in range(1, N):
        params = params + vecs[other]
    gain1, shift1, gain2, shift2, b_out, b_reduce = (params[i : i + 1] for i in range(6))
    b_query = biases[0:1, 0:DH]
    b_value = biases[1:2, 0:DH]
    b_expand = biases[2:3, 0:F]

    @pl.when(jnp.logical_or(s == 1, turned))
    def _():
        landed(u_in, k_u)

    start_values = u_in[...].reshape(T, D).astype(F32)
    normal, _ = normalize(start_values)
    n1[y] = (normal * gain1 + shift1).astype(BF16)
    k_n1 = block_of()
    spread("y", n1, k_n1)

    own_w3.wait()
    for d in order:
        arrived("y", w3, k_w3, d)
    for d in (0,) + order:
        b = near(y, d)
        if d:
            arrived("y", n1, k_n1, d)
        rows = n1[b]
        kv[x, 0, b] = mm(rows, w3[:, 1].reshape(D, DH)).astype(BF16).reshape(S, R, DH)
        kv[x, 1, b] = (mm(rows, w3[:, 2].reshape(D, DH)) + b_value).astype(BF16).reshape(S, R, DH)
        q_all[b] = (
            ((mm(rows, w3[:, 0].reshape(D, DH)) + b_query) * 0.125).astype(BF16).reshape(S, R, DH)
        )
    k_kv = block_of()
    spread("x", kv, k_kv)

    lanes = lax.broadcasted_iota(jnp.int32, (1, DH), 1)
    in_head = [
        jnp.logical_and(lanes >= h * HEAD, lanes < (h + 1) * HEAD) for h in range(heads)
    ]

    def only(h, values):
        return jnp.where(in_head[h], values.astype(F32), 0.0)

    for d in order:
        arrived("x", kv, k_kv, d)

    @pl.loop(0, S)
    def _(i):
        query = q_all[:, i].reshape(N * R, DH)
        keys = kv[:, 0, :, i].reshape(N * N * R, DH)
        values = kv[:, 1, :, i].reshape(N * N * R, DH)
        allowed = kpos[...] <= qpos[...]
        total = jnp.zeros((N * R, DH), F32)
        for h in range(heads):
            scores = mm_nt(only(h, query).astype(BF16), keys)
            scores = jnp.where(allowed, scores, -1e30)
            raised = jnp.exp(scores - jnp.max(scores, axis=-1, keepdims=True))
            part = raised / jnp.sum(raised, axis=-1, keepdims=True)
            probs[i * heads + h] = part
            total = total + only(h, mm(part.astype(BF16), values))
        mixed[:, i] = total.astype(BF16).reshape(N, R, DH)

    def scatter(number, base, block, dealt):
        for d in dealt:
            b = near(y, d)
            term = block(b, d)
            if d:
                part_send[number, b] = term.astype(BF16)
                deal("y", part_send.at[number], part_recv.at[number], base, d)
            else:
                own[...] = term

    def collected(number, base):
        total = own[...]
        for d in order:
            arrived("y", part_recv.at[number], base, d)
            total = total + part_recv[number, near(y, d)].astype(F32)
        return total

    k_po = block_of()
    scatter(
        0, k_po, lambda b, d: mm(mixed[b].reshape(T, DH), wout_in[...]), order[::-1] + (0,)
    )
    state = start_values + (collected(0, k_po) + b_out)
    hidden[...] = state
    normal, _ = normalize(state)
    n2[y] = (normal * gain2 + shift2).astype(BF16)
    k_n2 = block_of()
    spread("y", n2, k_n2)

    own_wexp.wait()
    for d in order:
        arrived("y", wexp, k_wexp, d)

    def feed(b, d):
        if d:
            arrived("y", n2, k_n2, d)
        before = mm(n2[b], wexp[...].reshape(D, F)) + b_expand
        square = before * before
        bent = jnp.tanh(GELU_SCALE * (before + GELU_CUBE * (square * before)))
        half = 0.5 * (1.0 + bent)
        low = (before * half).astype(BF16)
        active[b] = low
        slope[b] = half + 0.5 * before * (1.0 - bent * bent) * (
            GELU_SCALE * (1.0 + 3.0 * GELU_CUBE * square)
        )
        return mm(low, wred_in[...])

    k_ff = block_of()
    scatter(1, k_ff, feed, (0,) + order)
    result = hidden[...] + (collected(1, k_ff) + b_reduce)
    y_low[...] = result.astype(BF16).reshape(S, R, D)
    start_if(s == 0, y_low, u_in, k_u, k_u, {"section": 1})
    start_if(turned, y_low, out_y, k_y, k_y, partner)
    own_y = pltpu.make_async_copy(y_low, out_y, lsem.at[2])
    pl.when(straight)(lambda: own_y.start())

    @pl.when(jnp.logical_and(s == 1, turned))
    def _():
        landed(cot_in, k_cot)

    @pl.when(s == 1)
    def _():
        grad[...] = cot_in[...].reshape(T, D)

    @pl.when(s == 0)
    def _():
        landed(gp_in, k_gp)
        grad[...] = gp_in[...].astype(F32)

    branch = grad[...].astype(BF16)
    g_all[y] = branch
    k_g = block_of()
    spread("y", g_all, k_g)
    sm_own[...] = jnp.zeros_like(sm_own)
    sm_own[5:6] = column_sums(branch)

    def feed_back(b, d):
        if d:
            arrived("y", g_all, k_g, d)
        low = (mm_nt(g_all[b], wred_in[...]) * slope[b]).astype(BF16)
        gb_all[b] = low
        return mm_nt(low, wexp[...].reshape(D, F))

    k_gf = block_of()
    scatter(2, k_gf, feed_back, (0,) + order)

    g_rows = g_all[...].reshape(N * T, D)
    gb_rows = gb_all[...].reshape(N * T, F)
    sm_own[10:11] = column_sums(gb_rows)
    ff1s[:, 1] = mm_tn(active[...].reshape(N * T, F), g_rows).astype(BF16).reshape(N, F // N, D)
    ff1s[:, 0] = mm_tn(n2[...].reshape(N * T, D), gb_rows).astype(BF16).reshape(N, DH, F)
    k_ff1 = block_of()
    for d in order:
        deal("x", ff1s, ff1r, k_ff1, d)

    grad_two = collected(2, k_gf)
    normal, factor = normalize(hidden[...])
    sm_own[2:3] = column_sums(grad_two * normal)
    sm_own[3:4] = column_sums(grad_two)
    grad_hidden = grad[...] + norm_back(grad_two, normal, factor, gain2)
    grad[...] = grad_hidden
    low = grad_hidden.astype(BF16)
    ga_all[y] = low
    k_ga = block_of()
    spread("y", ga_all, k_ga)
    sm_own[4:5] = column_sums(low)

    for d in (0,) + order:
        if d:
            arrived("y", ga_all, k_ga, d)
        b = near(y, d)
        gm_all[b] = mm_nt(ga_all[b], wout_in[...]).astype(BF16).reshape(S, R, DH)

    @pl.loop(0, S)
    def _(i):
        query = q_all[:, i].reshape(N * R, DH)
        keys = kv[:, 0, :, i].reshape(N * N * R, DH)
        values = kv[:, 1, :, i].reshape(N * N * R, DH)
        grad_mixed = gm_all[:, i].reshape(N * R, DH)
        dq = jnp.zeros((N * R, DH), F32)
        dk = jnp.zeros((N * N * R, DH), F32)
        dv = jnp.zeros((N * N * R, DH), F32)
        for h in range(heads):
            part = probs[i * heads + h]
            mixed_head = only(h, grad_mixed).astype(BF16)
            grad_probs = mm_nt(mixed_head, values)
            inner = jnp.sum(part * grad_probs, axis=-1, keepdims=True)
            grad_scores = (part * (grad_probs - inner)).astype(BF16)
            dq = dq + only(h, mm(grad_scores, keys))
            dk = dk + mm_tn(grad_scores, only(h, query).astype(BF16))
            dv = dv + mm_tn(part.astype(BF16), mixed_head)
        dq_all[:, i] = (dq.astype(BF16).astype(F32) * 0.125).astype(BF16).reshape(N, R, DH)
        dkv_send[:, 0, :, i] = dk.astype(BF16).reshape(N, N, R, DH)
        dkv_send[:, 1, :, i] = dv.astype(BF16).reshape(N, N, R, DH)

    k_dkv = block_of()
    for d in order:
        deal("x", dkv_send, dkv_recv, k_dkv, d)

    def summed(axis, sent, received, base):
        me = place[axis]
        total = sent[me].astype(F32)
        for d in order:
            arrived(axis, received, base, d)
            total = total + received[near(me, d)].astype(F32)
        return total

    def in_order(ref, base):
        for d in order:
            arrived("z", ref, base, d)
        total = ref[0].astype(F32)
        for other in range(1, N):
            total = total + ref[other].astype(F32)
        return total

    ao1s[...] = (
        mm_tn(mixed[...].reshape(N * T, DH), ga_all[...].reshape(N * T, D))
        .astype(BF16)
        .reshape(N, DH // N, D)
    )
    k_ao1 = block_of()
    for d in order:
        deal("x", ao1s, ao1r, k_ao1, d)
    ff2[z] = summed("x", ff1s, ff1r, k_ff1).astype(BF16)
    k_ff2 = block_of()
    spread("z", ff2, k_ff2)

    total = dkv_send[x].astype(F32)
    for d in order:
        arrived("x", dkv_recv, k_dkv, d)
        total = total + dkv_recv[near(x, d)].astype(F32)
    dk_all[...] = total[0].astype(BF16)
    dv_all[...] = total[1].astype(BF16)

    def project_back(b, d):
        return (
            mm_nt(dq_all[b].reshape(T, DH), w3[:, 0].reshape(D, DH))
            + mm_nt(dk_all[b].reshape(T, DH), w3[:, 1].reshape(D, DH))
            + mm_nt(dv_all[b].reshape(T, DH), w3[:, 2].reshape(D, DH))
        )

    k_gn = block_of()
    scatter(3, k_gn, project_back, order[::-1] + (0,))
    n1_rows = n1[...].reshape(N * T, D)
    for j, ref in enumerate((dq_all, dk_all, dv_all)):
        rows = ref[...].reshape(N * T, DH)
        if j == 0:
            sm_own[8:9, 0:DH] = column_sums(rows)
        if j == 2:
            sm_own[9:10, 0:DH] = column_sums(rows)
        aq1s[:, j] = mm_tn(n1_rows, rows).astype(BF16).reshape(N, DH, DH)
    k_aq1 = block_of()
    for d in order:
        deal("x", aq1s, aq1r, k_aq1, d)

    grad_normed = collected(3, k_gn)
    normal, factor = normalize(u_in[...].reshape(T, D).astype(F32))
    sm_own[0:1] = column_sums(grad_normed * normal)
    sm_own[1:2] = column_sums(grad_normed)
    grad_input = grad[...] + norm_back(grad_normed, normal, factor, gain1)
    dx_low[...] = grad_input.astype(BF16)
    start_if(s == 1, dx_low, gp_in, k_gp, k_gp, {"section": 0})
    dx_buf[...] = grad_input.reshape(S, R, D)
    start_if(turned, dx_buf, out_dx, k_dx, k_dx, partner)
    own_dx = pltpu.make_async_copy(dx_buf, out_dx, lsem.at[3])
    pl.when(straight)(lambda: own_dx.start())

    sm_y[y] = sm_own[0:8]
    k_smy = block_of()
    spread("y", sm_y, k_smy)

    k_wexp_out = block_of()
    k_wred_out = block_of()
    k_wqkv_out = block_of()
    k_wout_out = block_of()
    k_sends = [block_of() for _ in range(4)]
    locals_ = []

    def hand_rows(src, dst_of, base, send_base, slot):
        for d in order:
            other = near(x, d)
            start(src, dst_of(x), send_base + d, base + x, along("x", other))
        copy = pltpu.make_async_copy(src, dst_of(x), lsem.at[slot])
        copy.start()
        locals_.append((None, copy))

    def hand_across(src, dst_of, base, send_base, slot):
        home = y == x
        for d in range(N):
            other = near(x, d)
            device = {"ctx": z * N + other, "fsdp": x}
            if d:
                start(src, dst_of(y), send_base + d, base + y, device)
            else:
                start_if(jnp.logical_not(home), src, dst_of(y), send_base + d, base + y, device)
        copy = pltpu.make_async_copy(src, dst_of(y), lsem.at[slot])
        pl.when(home)(lambda: copy.start())
        locals_.append((home, copy))

    def wexp_slot(i):
        return out_wexp.at[:, pl.ds(pl.multiple_of(i * F, 128), F)]

    def wred_slot(i):
        return out_wred.at[i]

    def wqkv_slot(i):
        return out_wqkv.at[i]

    def wout_slot(i):
        return out_wout.at[i]

    ff3[...] = in_order(ff2, k_ff2).astype(BF16)
    hand_across(ff3.at[0], wexp_slot, k_wexp_out, k_sends[0], 4)
    hand_rows(ff3.at[1], wred_slot, k_wred_out, k_sends[1], 5)

    aq2[z] = summed("x", aq1s, aq1r, k_aq1).astype(BF16)
    k_aq2 = block_of()
    spread("z", aq2, k_aq2)
    ao2[z] = summed("x", ao1s, ao1r, k_ao1).astype(BF16)
    k_ao2 = block_of()
    spread("z", ao2, k_ao2)

    for d in order:
        arrived("y", sm_y, k_smy, d)
    rows = sm_y[0]
    for other in range(1, N):
        rows = rows + sm_y[other]
    sm_x[x, 0:8] = rows
    sm_x[x, 8:16] = sm_own[8:16]
    k_smx = block_of()
    spread("x", sm_x, k_smx)

    aq3[...] = in_order(aq2, k_aq2).astype(BF16)
    hand_across(aq3, wqkv_slot, k_wqkv_out, k_sends[2], 6)
    ao3[...] = in_order(ao2, k_ao2).astype(BF16)
    hand_rows(ao3, wout_slot, k_wout_out, k_sends[3], 7)

    for d in order:
        arrived("x", sm_x, k_smx, d)
    rows = sm_x[0]
    for other in range(1, N):
        rows = rows + sm_x[other]
    sm_z[z] = rows
    k_smz = block_of()
    spread("z", sm_z, k_smz)
    for d in order:
        arrived("z", sm_z, k_smz, d)
    rows = sm_z[0]
    for other in range(1, N):
        rows = rows + sm_z[other]
    out_small[...] = rows

    for d in order:
        landed(wred_slot(near(x, d)), k_wred_out + near(x, d))
        landed(wout_slot(near(x, d)), k_wout_out + near(x, d))
    for d in range(N):
        source = near(y, d)
        if d:
            landed(wexp_slot(source), k_wexp_out + source)
            landed(wqkv_slot(source), k_wqkv_out + source)
        else:
            @pl.when(x != y)
            def _():
                landed(wexp_slot(source), k_wexp_out + source)
                landed(wqkv_slot(source), k_wqkv_out + source)

    @pl.when(turned)
    def _():
        landed(out_y, k_y)
        landed(out_dx, k_dx)

    @pl.when(straight)
    def _():
        own_y.wait()
        own_dx.wait()

    for condition, copy in locals_:
        if condition is None:
            copy.wait()
        else:
            pl.when(condition)(functools.partial(copy.wait))
    for condition, copy in drains:
        if condition is None:
            copy.wait_send()
        else:
            pl.when(condition)(functools.partial(copy.wait_send))
    assert counter[0] <= SEMS


SEMS = 128


def shards(
    tokens, cotangent, block_order, first_gain, first_shift, w_query, b_query, w_key, w_value,
    b_value, w_out, b_out, second_gain, second_shift, w_expand, b_expand, w_reduce, b_reduce,
):
    N = lax.axis_size("fsdp")
    S, R, D = tokens.shape
    F = w_reduce.shape[1]
    DH = D // N
    T = S * R
    heads = DH // HEAD
    c = lax.axis_index("ctx")
    y = lax.axis_index("fsdp")
    x = lax.rem(c, N)
    block = R // 2

    places = block_order.reshape(N, N, 2, 1) * block + jnp.arange(block, dtype=jnp.int32)
    places = places.transpose(1, 0, 2, 3).reshape(N, N * R)
    qpos = lax.dynamic_index_in_dim(places, x, 0, keepdims=False).reshape(N * R, 1)
    kpos = places.reshape(1, N * N * R)

    wqkv = jnp.stack([w_query[0], w_key[0], w_value[0]])
    wqkv = wqkv.reshape(3, DH, N, DH).transpose(2, 0, 1, 3)
    six = jnp.concatenate(
        [first_gain, first_shift, second_gain, second_shift, b_out, b_reduce], axis=0
    ).astype(F32)
    vecs = lax.dynamic_update_slice(jnp.zeros((8, D), F32), six, (0, y * DH))
    biases = jnp.zeros((8, max(D, F)), F32)
    biases = biases.at[0:1, 0:DH].set(b_query.astype(F32))
    biases = biases.at[1:2, 0:DH].set(b_value.astype(F32))
    biases = biases.at[2:3, 0:F].set(b_expand.astype(F32))

    def shape(dims, dtype):
        return jax.ShapeDtypeStruct(dims, dtype)

    vmem = pl.BlockSpec(memory_space=pltpu.VMEM)
    hbm = pl.BlockSpec(memory_space=pl.ANY)
    V = pltpu.VMEM
    rows = (N, S, R, DH)
    outs = pl.pallas_call(
        functools.partial(kernel, N, S, R, D, F),
        out_shape=(
            shape((S, R, D), BF16),
            shape((S, R, D), F32),
            shape((N, 3, DH, DH), BF16),
            shape((N, DH // N, D), BF16),
            shape((DH, N * F), BF16),
            shape((N, F // N, D), BF16),
            shape((16, D), F32),
        ),
        in_specs=[vmem, vmem, hbm, vmem, hbm, vmem, vmem, vmem, vmem, vmem],
        out_specs=(hbm, hbm, hbm, hbm, hbm, hbm, vmem),
        scratch_shapes=[
            V((S, R, D), BF16), V((S, R, D), F32), V((T, D), BF16),
            V((S, R, D), BF16), V((S, R, D), F32), V((T, D), BF16), V((N, 8, D), F32),
            V((N, 3, DH, DH), BF16), V((N, DH, F), BF16),
            V((N, T, D), BF16), V((N, T, D), BF16), V((N, T, D), BF16), V((N, T, D), BF16),
            V((N, T, F), BF16), V((N, T, F), BF16), V((N, T, F), F32),
            V(rows, BF16), V((N, 2) + rows, BF16), V((S * heads, N * R, N * N * R), F32),
            V(rows, BF16), V(rows, BF16), V(rows, BF16), V(rows, BF16), V(rows, BF16),
            V((N, 2) + rows, BF16), V((N, 2) + rows, BF16),
            V((4, N, T, D), BF16), V((4, N, T, D), BF16), V((T, D), F32), V((T, D), F32),
            V((T, D), F32),
            V((N, 2, DH, D), BF16), V((N, 2, DH, D), BF16), V((N, 2, DH, D), BF16),
            V((2, DH, D), BF16),
            V((N, 3, DH, DH), BF16), V((N, 3, DH, DH), BF16), V((N, 3, DH, DH), BF16),
            V((3, DH, DH), BF16),
            V((N, DH // N, D), BF16), V((N, DH // N, D), BF16), V((N, DH // N, D), BF16),
            V((DH // N, D), BF16),
            V((N, 8, D), F32), V((N, 16, D), F32), V((N, 16, D), F32), V((16, D), F32),
            pltpu.SemaphoreType.DMA((SEMS,)),
            pltpu.SemaphoreType.DMA((SEMS,)),
            pltpu.SemaphoreType.DMA((8,)),
        ],
        compiler_params=pltpu.CompilerParams(
            collective_id=0, has_side_effects=True, vmem_limit_bytes=60 * 1024 * 1024
        ),
        name="layers",
    )(
        tokens, cotangent, wqkv, w_out[0], w_expand[0], w_reduce[0], vecs, biases, qpos, kpos
    )
    out_y, out_dx, g_qkv, g_out, g_exp, g_red, small = outs
    g_qkv = g_qkv.transpose(1, 2, 0, 3).reshape(3, DH, D).astype(F32)
    mine = lax.dynamic_slice(small, (0, y * DH), (6, DH))
    return (
        out_y[None],
        out_dx[None],
        mine[0:1],
        mine[1:2],
        g_qkv[0:1],
        small[8:9, 0:DH],
        g_qkv[1:2],
        g_qkv[2:3],
        small[9:10, 0:DH],
        g_out.reshape(1, DH, D).astype(F32),
        mine[4:5],
        mine[2:3],
        mine[3:4],
        g_exp.astype(F32)[None],
        small[10:11, 0:F],
        g_red.reshape(1, F, D).astype(F32),
        mine[5:6],
    )


def solution(mesh):
    vector = P("section", "fsdp")
    matrix = P("section", "fsdp", None)
    return jax.shard_map(
        shards,
        mesh=mesh,
        in_specs=(
            P("fsdp", "ctx", None), P("fsdp", "ctx", None), P(),
            vector, vector, matrix, vector, matrix, matrix, vector, matrix, vector, vector, vector,
            matrix, vector, matrix, vector,
        ),
        out_specs=(
            P("section", "fsdp", "ctx", None), P("section", "fsdp", "ctx", None),
            vector, vector, matrix, vector, matrix, matrix, vector, matrix, vector, vector, vector,
            matrix, vector, matrix, vector,
        ),
        check_vma=False,
    )
```

```python
import functools

import jax
import jax.numpy as jnp
from jax import lax
from jax.experimental import pallas as pl
from jax.experimental.pallas import tpu as pltpu
from jax.sharding import PartitionSpec as P

HEAD = 64
EPSILON = 1e-05
F32 = jnp.float32
BF16 = jnp.bfloat16
MESH = pl.DeviceIdType.MESH
GELU_SCALE = 0.7978845608028654
GELU_CUBE = 0.044715
SEMS = 256


def mm(left, right):
    return jnp.dot(left, right, preferred_element_type=F32)


def mm_nt(left, right):
    return lax.dot_general(left, right, (((1,), (1,)), ((), ())), preferred_element_type=F32)


def mm_tn(left, right):
    return lax.dot_general(left, right, (((0,), (0,)), ((), ())), preferred_element_type=F32)


def normalize(values):
    average = jnp.mean(values, axis=-1, keepdims=True)
    centered = values - average
    variance = jnp.mean(centered * centered, axis=-1, keepdims=True)
    factor = lax.rsqrt(variance + EPSILON)
    return centered * factor, factor


def norm_back(grad, normal, factor, gain):
    scaled = grad * gain
    return factor * (
        scaled
        - jnp.mean(scaled, axis=-1, keepdims=True)
        - normal * jnp.mean(scaled * normal, axis=-1, keepdims=True)
    )


def column_sums(values):
    return jnp.sum(values.astype(F32), axis=0, keepdims=True)


def kernel(
    N, S, R, D, F,
    tok, cot, order_in, gain1_in, shift1_in, wq_in, bq_in, wk_in, wv_in, bv_in, wout_in, bout_in,
    gain2_in, shift2_in, wexp_in, bexp_in, wred_in, bred_in,
    out_y, out_dx, out_kv, out_q, out_out, out_wexp, out_wred, out_small,
    u_in, cot_in, gp_in, y_low, dx_buf, dx_low, pack, vecs, kpos, qpos,
    w_send, w_all, wexp, wred, wout, n1, n2, g_all, ga_all, gb_all, active, slope,
    q_all, kv, probs, mixed, gm_all, dq_all, dkv_all, acc_q, acc_kv, dkv_send, dkv_recv,
    part_send, part_recv, hidden, grad,
    ff_s, ff_r, ff_sum, qo_s, qo_r, qo_sum, kv_s, kv_r, kv_sum,
    sm_y, sm_c, sm_own,
    ssem, rsem, lsem, go,
):
    NN = N * N
    M = N * R
    DH = D // N
    W = 2 * DH // 3
    WQ, WKV = 2 * W, 3 * W
    heads = DH // HEAD
    s = lax.axis_index("section")
    c = lax.axis_index("ctx")
    y = lax.axis_index("fsdp")
    x = lax.rem(c, N)
    z = lax.div(c, N)
    straight = y == z
    turned = y != z
    order = tuple(sorted(range(1, N), key=lambda d: min(d, N - d)))
    streams = range(S)
    sibling = {"section": 1 - s}
    partner = {"ctx": y * N + x, "fsdp": z}

    def near(v, d):
        return lax.rem(v + d, N)

    def near_ctx(d):
        return lax.rem(c + d, NN)

    counter = [0]

    def block_of(count=N):
        counter[0] += count
        assert counter[0] <= SEMS
        return counter[0] - count

    drains = []

    def remote(src, dst, send, recv, device):
        return pltpu.make_async_remote_copy(
            src_ref=src, dst_ref=dst, send_sem=ssem.at[send], recv_sem=rsem.at[recv],
            device_id=device, device_id_type=MESH,
        )

    def start(src, dst, send, recv, device):
        copy = remote(src, dst, send, recv, device)
        copy.start()
        drains.append(copy.wait_send)

    def start_if(condition, src, dst, send, recv, device):
        copy = remote(src, dst, send, recv, device)
        pl.when(condition)(lambda: copy.start())
        drains.append(lambda: pl.when(condition)(lambda: copy.wait_send()))

    def start_each(count, make):
        @pl.loop(1, count)
        def _(d):
            make(d).start()

        def drain():
            @pl.loop(1, count)
            def _(d):
                make(d).wait_send()

        drains.append(drain)

    def landed(dst, recv):
        remote(dst, dst, 0, recv, sibling).wait_recv()

    def local_if(condition, src, dst, slot):
        copy = pltpu.make_async_copy(src, dst, lsem.at[slot])
        pl.when(condition)(lambda: copy.start())
        return lambda: pl.when(condition)(lambda: copy.wait())

    def local(src, dst, slot):
        copy = pltpu.make_async_copy(src, dst, lsem.at[slot])
        copy.start()
        return copy.wait

    def along(axis, index):
        if axis == "y":
            return {"fsdp": index}
        return {"ctx": z * N + index}

    place = {"x": x, "y": y}

    def spread(axis, ref, base):
        me = place[axis]
        for d in order:
            start(ref.at[me], ref.at[me], base + d, base + me, along(axis, near(me, d)))

    def arrived(axis, ref, base):
        for d in order:
            source = near(place[axis], d)
            landed(ref.at[source], base + source)

    def deal(axis, src, dst, base):
        me = place[axis]
        for d in order:
            other = near(me, d)
            start(src.at[other], dst.at[me], base + d, base + me, along(axis, other))

    barrier = pltpu.get_barrier_semaphore()

    @pl.loop(1, NN * N)
    def _(d):
        index = lax.rem(c * N + y + d, NN * N)
        pl.semaphore_signal(
            barrier, inc=1, device_id={"ctx": lax.div(index, N), "fsdp": lax.rem(index, N)},
            device_id_type=MESH,
        )

    pl.semaphore_signal(barrier, inc=1, device_id=sibling, device_id_type=MESH)
    wait_wred = local(wred_in, wred, 0)
    wait_wout = local(wout_in, wout.at[pl.ds(WQ - DH, DH)], 1)
    pl.semaphore_wait(barrier, NN * N)

    k_u = block_of(S)
    k_gp = block_of(S)
    k_cot, k_y, k_dx = (block_of(1) for _ in range(3))
    wait_u = []
    for i in streams:
        start_if(
            jnp.logical_and(s == 0, turned), tok.at[i], u_in.at[i], k_u + i, k_u + i, partner
        )
        wait_u.append(
            local_if(jnp.logical_and(s == 0, straight), tok.at[i], u_in.at[i], 2 + i)
        )

    pack[...] = jnp.zeros_like(pack)
    for j, ref in enumerate((gain1_in, shift1_in, gain2_in, shift2_in, bout_in, bred_in)):
        pack[j : j + 1] = ref[...].astype(F32)
    put = (
        lax.broadcasted_iota(jnp.int32, (DH, D), 0) + y * DH
        == lax.broadcasted_iota(jnp.int32, (DH, D), 1)
    )
    vecs[y] = mm(pack[...].astype(BF16), jnp.where(put, 1.0, 0.0).astype(BF16))[0:8]
    k_vecs = block_of()
    spread("y", vecs, k_vecs)

    def picker(width, shift, first):
        row = lax.broadcasted_iota(jnp.int32, (WQ, width), 0)
        col = lax.broadcasted_iota(jnp.int32, (WQ, width), 1)
        inside = jnp.logical_and(col >= first, col < first + DH)
        return jnp.where(
            jnp.logical_and(row - shift == col - first, inside), 1.0, 0.0
        ).astype(BF16)

    for b in range(N):
        lane = b * DH // W * W
        cut = slice(lane, lane + WQ)
        shift = b * DH - lane
        w_send[b, :, 0:WKV] = (
            mm(wk_in[:, cut], picker(WKV, shift, 0)) + mm(wv_in[:, cut], picker(WKV, shift, DH))
        ).astype(BF16)
        w_send[b, :, WKV : WKV + WQ] = mm(wq_in[:, cut], picker(WQ, shift, 0)).astype(BF16)
    w_all[y] = w_send[y]

    @pl.when(s == 1)
    def _():
        pl.semaphore_wait(go, 1)

    k_w = block_of()
    deal("y", w_send, w_all, k_w)

    blocks = 2 * NN
    half = R // 2
    slot = lax.broadcasted_iota(jnp.int32, (1, blocks * half), 1)
    found = jnp.zeros_like(slot)
    for b in range(blocks):
        xb, yb, side = b // (2 * N), b // 2 % N, b % 2
        found = jnp.where(slot >= b * half, order_in[2 * (yb * N + xb) + side] * half - b * half, found)
    kpos[...] = found + slot
    slot = lax.broadcasted_iota(jnp.int32, (M, 1), 0)
    found = jnp.zeros_like(slot)
    for b in range(2 * N):
        found = jnp.where(
            slot >= b * half, order_in[2 * ((b // 2) * N + x) + b % 2] * half - b * half, found
        )
    qpos[...] = found + slot

    arrived("y", vecs, k_vecs)
    params = vecs[0]
    for other in range(1, N):
        params = params + vecs[other]
    gain1, shift1, gain2, shift2, b_out, b_reduce = (params[j : j + 1] for j in range(6))
    lanes = lax.broadcasted_iota(jnp.int32, (1, WQ), 1)

    k_n1 = [block_of() for _ in streams]
    for i in streams:
        @pl.when(jnp.logical_or(s == 1, turned))
        def _():
            landed(u_in.at[i], k_u + i)

        wait_u[i]()
        normal, _ = normalize(u_in[i].astype(F32))
        n1[i, y] = (normal * gain1 + shift1).astype(BF16)
        spread("y", n1.at[i], k_n1[i])

    k_wexp = block_of()

    def wexp_cut(b):
        return wexp_in.at[:, pl.ds(pl.multiple_of(b * F, 128), F)]

    wait_wexp = local(wexp_cut(y), wexp.at[y], 4)
    for d in order:
        other = near(y, d)
        start(wexp_cut(other), wexp.at[y], k_wexp + d, k_wexp + y, along("y", other))
    start_if(jnp.logical_and(s == 1, turned), cot, cot_in, k_cot, k_cot, partner)
    wait_cot = local_if(jnp.logical_and(s == 1, straight), cot, cot_in, 5)

    k_kv = [block_of() for _ in streams]
    arrived("y", w_all, k_w)
    for i in streams:
        arrived("y", n1.at[i], k_n1[i])
        rows = n1[i].reshape(M, D)
        made = mm(rows, w_all[:, :, 0:WKV].reshape(D, WKV))
        made_low = made[:, 0 : 2 * DH]
        kv[i, x] = made_low.astype(BF16)
        kv[i, x, :, W:WKV] = (
            made[:, W:WKV] + bias_at(bv_in, W, WQ, DH)
        ).astype(BF16)
        spread("x", kv.at[i], k_kv[i])
        query = mm(rows, w_all[:, :, WKV : WKV + WQ].reshape(D, WQ)) + bias_at(bq_in, 0, WQ, 0)
        q_all[i] = (query * 0.125).astype(BF16)

    @pl.when(s == 0)
    def _():
        pl.semaphore_signal(go, inc=1, device_id=sibling, device_id_type=MESH)

    def only(h, values, first):
        inside = jnp.logical_and(lanes >= first + h * HEAD, lanes < first + (h + 1) * HEAD)
        return jnp.where(inside, values.astype(F32), 0.0)

    def scatter(number, i, term, base):
        part_send[number, i] = term.astype(BF16).reshape(N, R, D)
        deal("y", part_send.at[number, i], part_recv.at[number, i], base)

    def collected(number, i, base):
        total = part_send[number, i, y].astype(F32)
        arrived("y", part_recv.at[number, i], base)
        for d in order:
            total = total + part_recv[number, i, near(y, d)].astype(F32)
        return total

    wout[0 : WQ - DH] = jnp.zeros((WQ - DH, D), BF16)
    wait_wout()
    k_po = [block_of() for _ in streams]
    for i in streams:
        arrived("x", kv.at[i], k_kv[i])
        allowed = kpos[...] <= qpos[...]
        acc_q[...] = jnp.zeros_like(acc_q)

        @pl.loop(0, heads)
        def _(h):
            keys = kv[i, :, :, 0:WQ].reshape(N * M, WQ)
            values = kv[i, :, :, W:WKV].reshape(N * M, WQ)
            scores = mm_nt(only(h, q_all[i], 0).astype(BF16), keys)
            scores = jnp.where(allowed, scores, -1e30)
            raised = jnp.exp(scores - jnp.max(scores, axis=-1, keepdims=True))
            part = raised / jnp.sum(raised, axis=-1, keepdims=True)
            probs[i * heads + h] = part
            acc_q[...] += only(h, mm(part.astype(BF16), values), WQ - DH)

        low = acc_q[...].astype(BF16)
        mixed[i] = low
        scatter(0, i, mm(low, wout[...]), k_po[i])

    k_n2 = [block_of() for _ in streams]
    for i in streams:
        state = u_in[i].astype(F32) + (collected(0, i, k_po[i]) + b_out)
        hidden[i] = state
        normal, _ = normalize(state)
        n2[i, y] = (normal * gain2 + shift2).astype(BF16)
        spread("y", n2.at[i], k_n2[i])

    wait_wexp()
    wait_wred()
    arrived("y", wexp, k_wexp)
    k_ff = [block_of() for _ in streams]
    for i in streams:
        arrived("y", n2.at[i], k_n2[i])
        before = mm(n2[i].reshape(M, D), wexp[...].reshape(D, F)) + bexp_in[...].astype(F32)
        square = before * before
        bent = jnp.tanh(GELU_SCALE * (before + GELU_CUBE * (square * before)))
        side = 0.5 * (1.0 + bent)
        low = (before * side).astype(BF16)
        active[i] = low
        slope[i] = side + 0.5 * before * (1.0 - bent * bent) * (
            GELU_SCALE * (1.0 + 3.0 * GELU_CUBE * square)
        )
        scatter(1, i, mm(low, wred[...]), k_ff[i])

    for i in streams:
        result = hidden[i] + (collected(1, i, k_ff[i]) + b_reduce)
        y_low[i] = result.astype(BF16)
        start_if(s == 0, y_low.at[i], u_in.at[i], k_u + i, k_u + i, sibling)

    @pl.when(jnp.logical_and(s == 1, turned))
    def _():
        landed(cot_in, k_cot)

    wait_cot()
    sm_own[...] = jnp.zeros_like(sm_own)
    k_g = [block_of() for _ in streams]
    for i in streams:
        @pl.when(s == 1)
        def _():
            grad[i] = cot_in[i]

        @pl.when(s == 0)
        def _():
            landed(gp_in.at[i], k_gp + i)
            grad[i] = gp_in[i].astype(F32)

        low = grad[i].astype(BF16)
        g_all[i, y] = low
        spread("y", g_all.at[i], k_g[i])
        sm_own[5:6] += column_sums(low)

    start_if(turned, y_low, out_y, k_y, k_y, partner)
    wait_y = local_if(straight, y_low, out_y, 6)

    k_gf = [block_of() for _ in streams]
    for i in streams:
        arrived("y", g_all.at[i], k_g[i])
        low = (mm_nt(g_all[i].reshape(M, D), wred[...]) * slope[i]).astype(BF16)
        gb_all[i] = low
        scatter(2, i, mm_nt(low, wexp[...].reshape(D, F)), k_gf[i])

    def turn(index):
        return lax.rem(lax.rem(index, N) + lax.div(index, N), N)

    def piece(index):
        return turn(index) * N + lax.div(index, N)

    mine = piece(c)

    def pool(src, dst, base):
        dst[c] = src[mine]

        def make(d):
            other = near_ctx(d)
            return remote(src.at[piece(other)], dst.at[c], base + d, base + c, {"ctx": other})

        start_each(NN, make)

    def pooled(dst, base):
        @pl.loop(1, NN)
        def _(d):
            landed(dst.at[near_ctx(d)], base + near_ctx(d))

        total = dst[0].astype(F32)
        for other in range(1, NN):
            total = total + dst[other].astype(F32)
        return total

    g_rows = g_all[...].reshape(S * M, D)
    gb_rows = gb_all[...].reshape(S * M, F)
    sm_own[10:11] = column_sums(gb_rows)
    ff_s[:, 1] = mm_tn(active[...].reshape(S * M, F), g_rows).astype(BF16).reshape(NN, F // NN, D)
    ff_s[:, 0] = mm_tn(n2[...].reshape(S * M, D), gb_rows).astype(BF16).reshape(NN, D // NN, F)
    k_ffp = block_of(NN)
    pool(ff_s, ff_r, k_ffp)

    k_ga = [block_of() for _ in streams]
    for i in streams:
        grad_two = collected(2, i, k_gf[i])
        normal, factor = normalize(hidden[i])
        grad_hidden = grad[i] + norm_back(grad_two, normal, factor, gain2)
        grad[i] = grad_hidden
        low = grad_hidden.astype(BF16)
        ga_all[i, y] = low
        spread("y", ga_all.at[i], k_ga[i])
        sm_own[2:3] += column_sums(grad_two * normal)
        sm_own[3:4] += column_sums(grad_two)
        sm_own[4:5] += column_sums(low)

    k_dkv = [block_of() for _ in streams]
    for i in streams:
        arrived("y", ga_all.at[i], k_ga[i])
        gm_all[i] = mm_nt(ga_all[i].reshape(M, D), wout[...]).astype(BF16)
        acc_q[...] = jnp.zeros_like(acc_q)
        acc_kv[...] = jnp.zeros_like(acc_kv)

        @pl.loop(0, heads)
        def _(h):
            keys = kv[i, :, :, 0:WQ].reshape(N * M, WQ)
            values = kv[i, :, :, W:WKV].reshape(N * M, WQ)
            part = probs[i * heads + h]
            mixed_head = only(h, gm_all[i], WQ - DH).astype(BF16)
            grad_probs = mm_nt(mixed_head, values)
            inner = jnp.sum(part * grad_probs, axis=-1, keepdims=True)
            grad_scores = (part * (grad_probs - inner)).astype(BF16)
            acc_q[...] += only(h, mm(grad_scores, keys), 0)
            acc_kv[:, 0:WQ] += mm_tn(grad_scores, only(h, q_all[i], 0).astype(BF16))
            acc_kv[:, W:WKV] += mm_tn(part.astype(BF16), mixed_head)

        dkv_send[i] = acc_kv[...].astype(BF16).reshape(N, M, WKV)
        deal("x", dkv_send.at[i], dkv_recv.at[i], k_dkv[i])
        dq_all[i] = (acc_q[...].astype(BF16).astype(F32) * 0.125).astype(BF16)

    n1_rows = n1[...].reshape(S * M, D)
    dq_rows = dq_all[...].reshape(S * M, WQ)
    sm_own[8:9, 0:DH] = column_sums(dq_rows)[:, 0:DH]
    grad_q = mm_tn(n1_rows, dq_rows)
    grad_o = mm_tn(ga_all[...].reshape(S * M, D), mixed[...].reshape(S * M, WQ))
    qo_s[:, :, 0:W] = grad_q[:, 0:W].astype(BF16).reshape(NN, D // NN, W)
    qo_s[:, :, W:WQ] = (grad_q[:, W:WQ] + grad_o[:, 0:W]).astype(BF16).reshape(NN, D // NN, W)
    qo_s[:, :, WQ:WKV] = grad_o[:, W:WQ].astype(BF16).reshape(NN, D // NN, W)
    k_qop = block_of(NN)
    pool(qo_s, qo_r, k_qop)

    home = turn(c) == y
    finals = []
    late = []

    def hand_rows(src, dst, slot):
        base = block_of(NN)

        def make(d):
            return remote(src, dst(mine), base + d, base + c, {"ctx": near_ctx(d)})

        start_each(NN, make)
        late.append(local(src, dst(mine), slot))

        def finish():
            @pl.loop(1, NN)
            def _(d):
                landed(dst(piece(near_ctx(d))), base + near_ctx(d))

        finals.append(finish)

    def hand_across(src, dst, slot):
        base = block_of(NN)
        owner = turn(c)

        def make(d):
            return remote(
                src, dst(z, y), base + d, base + z * N + y,
                {"ctx": near_ctx(d), "fsdp": owner},
            )

        start_each(NN, make)
        start_if(
            jnp.logical_not(home), src, dst(z, y), base, base + z * N + y,
            {"ctx": c, "fsdp": owner},
        )
        late.append(local_if(home, src, dst(z, y), slot))

        def finish():
            @pl.loop(0, NN)
            def _(index):
                sub = lax.div(index, N)
                source = lax.rem(index, N)
                own = jnp.logical_and(jnp.logical_and(home, sub == z), source == y)

                @pl.when(jnp.logical_not(own))
                def _():
                    landed(dst(sub, source), base + index)

        finals.append(finish)

    def lane_block(ref, width):
        return lambda sub, source: ref.at[
            sub, :, pl.ds(pl.multiple_of(source * width, 128), width)
        ]

    ff_sum[...] = pooled(ff_r, k_ffp).astype(BF16)
    hand_across(ff_sum.at[0], lane_block(out_wexp, F), 7)
    hand_rows(ff_sum.at[1], lambda index: out_wred.at[index], 8)

    k_gn = [block_of() for _ in streams]
    for i in streams:
        total = dkv_send[i, x].astype(F32)
        arrived("x", dkv_recv.at[i], k_dkv[i])
        for d in order:
            total = total + dkv_recv[i, near(x, d)].astype(F32)
        low = total.astype(BF16)
        dkv_all[i] = low
        scatter(
            3, i,
            mm_nt(dq_all[i], w_all[:, :, WKV : WKV + WQ].reshape(D, WQ))
            + mm_nt(low, w_all[:, :, 0:WKV].reshape(D, WKV)),
            k_gn[i],
        )

    dkv_rows = dkv_all[...].reshape(S * M, WKV)
    sm_own[9:10, 0:WKV] = column_sums(dkv_rows)
    kv_s[...] = mm_tn(n1_rows, dkv_rows).astype(BF16).reshape(NN, D // NN, WKV)
    k_kvp = block_of(NN)
    pool(kv_s, kv_r, k_kvp)

    for i in streams:
        grad_normed = collected(3, i, k_gn[i])
        normal, factor = normalize(u_in[i].astype(F32))
        grad_input = grad[i] + norm_back(grad_normed, normal, factor, gain1)
        dx_low[i] = grad_input.astype(BF16)
        start_if(s == 1, dx_low.at[i], gp_in.at[i], k_gp + i, k_gp + i, sibling)
        dx_buf[i] = grad_input
        sm_own[0:1] += column_sums(grad_normed * normal)
        sm_own[1:2] += column_sums(grad_normed)

    sm_y[y] = sm_own[0:8]
    k_smy = block_of()
    spread("y", sm_y, k_smy)
    start_if(turned, dx_buf, out_dx, k_dx, k_dx, partner)
    wait_dx = local_if(straight, dx_buf, out_dx, 9)

    qo_sum[...] = pooled(qo_r, k_qop).astype(BF16)
    hand_across(qo_sum.at[:, 0:WQ], lane_block(out_q, WQ), 10)
    hand_rows(qo_sum.at[:, W:WKV], lambda index: out_out.at[index], 11)

    arrived("y", sm_y, k_smy)
    rows = sm_y[0]
    for other in range(1, N):
        rows = rows + sm_y[other]
    sm_c[c, 0:8] = rows
    sm_c[c, 8:16] = sm_own[8:16]
    k_smc = block_of(NN)
    start_each(
        NN,
        lambda d: remote(sm_c.at[c], sm_c.at[c], k_smc + d, k_smc + c, {"ctx": near_ctx(d)}),
    )

    kv_sum[...] = pooled(kv_r, k_kvp).astype(BF16)
    hand_across(kv_sum, lane_block(out_kv, WKV), 12)

    @pl.loop(1, NN)
    def _(d):
        landed(sm_c.at[near_ctx(d)], k_smc + near_ctx(d))

    rows = sm_c[0]
    for other in range(1, NN):
        rows = rows + sm_c[other]
    out_small[...] = rows

    for finish in finals:
        finish()

    @pl.when(turned)
    def _():
        landed(out_y, k_y)
        landed(out_dx, k_dx)

    for wait in [wait_y, wait_dx] + late:
        wait()
    for drain in drains:
        drain()


def bias_at(ref, lane, width, first):
    size = ref.shape[1]
    row = lax.broadcasted_iota(jnp.int32, (size, width), 0)
    col = lax.broadcasted_iota(jnp.int32, (size, width), 1)
    put = jnp.where(row + first == col + lane, 1.0, 0.0).astype(BF16)
    wide = jnp.broadcast_to(ref[...].astype(F32), (16, size)).astype(BF16)
    return mm(wide, put)[0:1]


def shards(
    tokens, cotangent, block_order, first_gain, first_shift, w_query, b_query, w_key, w_value,
    b_value, w_out, b_out, second_gain, second_shift, w_expand, b_expand, w_reduce, b_reduce,
):
    N = lax.axis_size("fsdp")
    S, R, D = tokens.shape
    F = w_reduce.shape[1]
    DH = D // N
    W = 2 * DH // 3
    WQ, WKV = 2 * W, 3 * W
    NN, M = N * N, N * R
    heads = DH // HEAD
    y = lax.axis_index("fsdp")

    def shape(dims, dtype):
        return jax.ShapeDtypeStruct(dims, dtype)

    vmem = pl.BlockSpec(memory_space=pltpu.VMEM)
    smem = pl.BlockSpec(memory_space=pltpu.SMEM)
    hbm = pl.BlockSpec(memory_space=pl.ANY)
    V = pltpu.VMEM
    slab = V((S, N, R, D), BF16)
    outs = pl.pallas_call(
        functools.partial(kernel, N, S, R, D, F),
        out_shape=(
            shape((S, R, D), BF16),
            shape((S, R, D), F32),
            shape((N, D // NN, N * WKV), BF16),
            shape((N, D // NN, N * WQ), BF16),
            shape((NN, D // NN, WQ), BF16),
            shape((N, D // NN, N * F), BF16),
            shape((NN, F // NN, D), BF16),
            shape((16, D), F32),
        ),
        in_specs=[
            hbm, hbm, smem, vmem, vmem, vmem, vmem, vmem, vmem, vmem, hbm, vmem, vmem, vmem, hbm,
            vmem, hbm, vmem,
        ],
        out_specs=(hbm, hbm, hbm, hbm, hbm, hbm, hbm, vmem),
        scratch_shapes=[
            V((S, R, D), BF16), V((S, R, D), F32), V((S, R, D), BF16), V((S, R, D), BF16),
            V((S, R, D), F32), V((S, R, D), BF16), V((16, DH), F32), V((N, 8, D), F32),
            V((1, N * M), jnp.int32), V((M, 1), jnp.int32),
            V((N, DH, WKV + WQ), BF16), V((N, DH, WKV + WQ), BF16), V((N, DH, F), BF16),
            V((F, D), BF16), V((WQ, D), BF16),
            slab, slab, slab, slab,
            V((S, M, F), BF16), V((S, M, F), BF16), V((S, M, F), F32),
            V((S, M, WQ), BF16), V((S, N, M, WKV), BF16), V((S * heads, M, N * M), F32),
            V((S, M, WQ), BF16), V((S, M, WQ), BF16), V((S, M, WQ), BF16), V((S, M, WKV), BF16),
            V((M, WQ), F32), V((N * M, WKV), F32),
            V((S, N, M, WKV), BF16), V((S, N, M, WKV), BF16),
            V((4, S, N, R, D), BF16), V((4, S, N, R, D), BF16), V((S, R, D), F32),
            V((S, R, D), F32),
            V((NN, 2, D // NN, D), BF16), V((NN, 2, D // NN, D), BF16), V((2, D // NN, D), BF16),
            V((NN, D // NN, WKV), BF16), V((NN, D // NN, WKV), BF16), V((D // NN, WKV), BF16),
            V((NN, D // NN, WKV), BF16), V((NN, D // NN, WKV), BF16), V((D // NN, WKV), BF16),
            V((N, 8, D), F32), V((NN, 16, D), F32), V((16, D), F32),
            pltpu.SemaphoreType.DMA((SEMS,)),
            pltpu.SemaphoreType.DMA((SEMS,)),
            pltpu.SemaphoreType.DMA((16,)),
            pltpu.SemaphoreType.REGULAR,
        ],
        compiler_params=pltpu.CompilerParams(
            collective_id=0, has_side_effects=True, vmem_limit_bytes=60 * 1024 * 1024
        ),
        name="layers",
    )(
        tokens, cotangent, block_order, first_gain, first_shift, w_query[0], b_query, w_key[0],
        w_value[0], b_value, w_out[0], b_out, second_gain, second_shift, w_expand[0], b_expand,
        w_reduce[0], b_reduce,
    )
    out_y, out_dx, g_kv, g_q, g_out, g_exp, g_red, small = outs
    g_kv = g_kv.reshape(DH, N, WKV)
    g_q = g_q.reshape(DH, N, WQ)

    def whole(part):
        return part.astype(F32).reshape(1, DH, D)

    mine = lax.dynamic_slice(small, (0, y * DH), (6, DH))
    return (
        out_y[None],
        out_dx[None],
        mine[0:1],
        mine[1:2],
        whole(g_q[:, :, 0:DH]),
        small[8:9, 0:DH],
        whole(g_kv[:, :, 0:DH]),
        whole(g_kv[:, :, DH:WKV]),
        small[9:10, DH:WKV],
        g_out.reshape(D, WQ)[:, WQ - DH :].T.astype(F32)[None],
        mine[4:5],
        mine[2:3],
        mine[3:4],
        g_exp.reshape(1, DH, N * F).astype(F32),
        small[10:11, 0:F],
        g_red.reshape(1, F, D).astype(F32),
        mine[5:6],
    )


def solution(mesh):
    vector = P("section", "fsdp")
    matrix = P("section", "fsdp", None)
    return jax.shard_map(
        shards,
        mesh=mesh,
        in_specs=(
            P("fsdp", "ctx", None), P("fsdp", "ctx", None), P(),
            vector, vector, matrix, vector, matrix, matrix, vector, matrix, vector, vector, vector,
            matrix, vector, matrix, vector,
        ),
        out_specs=(
            P("section", "fsdp", "ctx", None), P("section", "fsdp", "ctx", None),
            vector, vector, matrix, vector, matrix, matrix, vector, matrix, vector, vector, vector,
            matrix, vector, matrix, vector,
        ),
        check_vma=False,
    )
```

```python
import functools

import jax
import jax.numpy as jnp
from jax import lax
from jax.experimental import pallas as pl
from jax.experimental.pallas import tpu as pltpu
from jax.sharding import PartitionSpec as P

HEAD = 64
EPSILON = 1e-05
F32 = jnp.float32
BF16 = jnp.bfloat16
MESH = pl.DeviceIdType.MESH
GELU_SCALE = 0.7978845608028654
GELU_CUBE = 0.044715
SEMS = 448


def mm(left, right):
    return jnp.dot(left, right, preferred_element_type=F32)


def mm_nt(left, right):
    return lax.dot_general(left, right, (((1,), (1,)), ((), ())), preferred_element_type=F32)


def mm_tn(left, right):
    return lax.dot_general(left, right, (((0,), (0,)), ((), ())), preferred_element_type=F32)


def normalize(values):
    average = jnp.mean(values, axis=-1, keepdims=True)
    centered = values - average
    variance = jnp.mean(centered * centered, axis=-1, keepdims=True)
    factor = lax.rsqrt(variance + EPSILON)
    return centered * factor, factor


def norm_back(grad, normal, factor, gain):
    scaled = grad * gain
    return factor * (
        scaled
        - jnp.mean(scaled, axis=-1, keepdims=True)
        - normal * jnp.mean(scaled * normal, axis=-1, keepdims=True)
    )


def column_sums(values):
    return jnp.sum(values.astype(F32), axis=0, keepdims=True)


def kernel(
    N, J, Q, D, F,
    tok, cot, order_in, rows_in, bexp_in, wq_in, wk_in, wv_in, wout_in, wexp_in, wred_in,
    out_y, out_dx, out_kv, out_q, out_out, out_wexp, out_wred, out_small,
    u_in, cot_in, gp_in, y_low, dx_buf, dx_low, vecs, kpos, qpos,
    wq, wk, wv, w_send, w_all, wexp, wred, wout, n1, n2, g_all, ga_all, gb_all, active, slope,
    q_all, kv, probs, mixed, gm_all, dq_all, dkv_all, dkv_send, dkv_recv,
    part_send, part_recv, hidden, grad,
    ff_s, ff_r, ff_sum, qo_s, qo_r, qo_sum, kv_s, kv_r, kv_sum,
    sm_y, sm_c, sm_own, sm_ly, sm_lc, sm_last,
    ssem, rsem, lsem, go,
):
    NN = N * N
    M = N * Q
    S = J // 2
    DH = D // N
    W = 2 * DH // 3
    WQ, WKV = 2 * W, 3 * W
    heads = DH // HEAD
    s = lax.axis_index("section")
    c = lax.axis_index("ctx")
    y = lax.axis_index("fsdp")
    x = lax.rem(c, N)
    z = lax.div(c, N)
    straight = y == z
    turned = y != z
    order = tuple(sorted(range(1, N), key=lambda d: -min(d, N - d)))
    streams = range(J)
    sibling = {"section": 1 - s}
    partner = {"ctx": y * N + x, "fsdp": z}

    def near(v, d):
        return lax.rem(v + d, N)

    def near_ctx(d):
        return lax.rem(c + d, NN)

    counter = [0]

    def block_of(count=N):
        counter[0] += count
        assert counter[0] <= SEMS
        return counter[0] - count

    drains = []

    def remote(src, dst, send, recv, device):
        return pltpu.make_async_remote_copy(
            src_ref=src, dst_ref=dst, send_sem=ssem.at[send], recv_sem=rsem.at[recv],
            device_id=device, device_id_type=MESH,
        )

    def start(src, dst, send, recv, device):
        copy = remote(src, dst, send, recv, device)
        copy.start()
        drains.append(copy.wait_send)

    def start_if(condition, src, dst, send, recv, device):
        copy = remote(src, dst, send, recv, device)
        pl.when(condition)(lambda: copy.start())
        drains.append(lambda: pl.when(condition)(lambda: copy.wait_send()))

    def start_each(count, make):
        @pl.loop(1, count)
        def _(d):
            make(d).start()

        def drain():
            @pl.loop(1, count)
            def _(d):
                make(d).wait_send()

        drains.append(drain)

    def landed(dst, recv):
        remote(dst, dst, 0, recv, sibling).wait_recv()

    def local_if(condition, src, dst, slot):
        copy = pltpu.make_async_copy(src, dst, lsem.at[slot])
        pl.when(condition)(lambda: copy.start())
        return lambda: pl.when(condition)(lambda: copy.wait())

    def local(src, dst, slot):
        copy = pltpu.make_async_copy(src, dst, lsem.at[slot])
        copy.start()
        return copy.wait

    def along(axis, index):
        if axis == "y":
            return {"fsdp": index}
        return {"ctx": z * N + index}

    place = {"x": x, "y": y}

    def spread(axis, ref, base, *rest):
        me = place[axis]
        for d in order:
            start(
                ref.at[(me,) + rest], ref.at[(me,) + rest], base + d, base + me,
                along(axis, near(me, d)),
            )

    def arrived(axis, ref, base, *rest):
        for d in order:
            source = near(place[axis], d)
            landed(ref.at[(source,) + rest], base + source)

    def deal(axis, src, dst, base):
        me = place[axis]
        for d in order:
            other = near(me, d)
            start(src.at[other], dst.at[me], base + d, base + me, along(axis, other))

    barrier = pltpu.get_barrier_semaphore()

    @pl.loop(1, NN * N)
    def _(d):
        index = lax.rem(c * N + y + d, NN * N)
        pl.semaphore_signal(
            barrier, inc=1, device_id={"ctx": lax.div(index, N), "fsdp": lax.rem(index, N)},
            device_id_type=MESH,
        )

    pl.semaphore_signal(barrier, inc=1, device_id=sibling, device_id_type=MESH)
    wait_cuts = [local(a, b, 13 + j) for j, (a, b) in enumerate(((wq_in, wq), (wk_in, wk), (wv_in, wv)))]
    wait_wred = local(wred_in, wred, 0)
    wait_wout = local(wout_in, wout.at[pl.ds(WQ - DH, DH)], 1)

    put = (
        lax.broadcasted_iota(jnp.int32, (DH, D), 0) + y * DH
        == lax.broadcasted_iota(jnp.int32, (DH, D), 1)
    )
    vecs[y] = mm(rows_in[...].astype(BF16), jnp.where(put, 1.0, 0.0).astype(BF16))[0:8]

    def picker(width, shift, first):
        row = lax.broadcasted_iota(jnp.int32, (WQ, width), 0)
        col = lax.broadcasted_iota(jnp.int32, (WQ, width), 1)
        inside = jnp.logical_and(col >= first, col < first + DH)
        return jnp.where(
            jnp.logical_and(row - shift == col - first, inside), 1.0, 0.0
        ).astype(BF16)

    for wait in wait_cuts:
        wait()
    for b in range(N):
        lane = b * DH // W * W
        cut = slice(lane, lane + WQ)
        shift = b * DH - lane
        w_send[b, :, 0:WKV] = (
            mm(wk[:, cut], picker(WKV, shift, 0)) + mm(wv[:, cut], picker(WKV, shift, DH))
        ).astype(BF16)
        w_send[b, :, WKV : WKV + WQ] = mm(wq[:, cut], picker(WQ, shift, 0)).astype(BF16)
    w_all[y] = w_send[y]
    pl.semaphore_wait(barrier, NN * N)

    k_u = block_of(J)
    k_gp = block_of(J)
    k_cot, k_y, k_dx = (block_of(1) for _ in range(3))
    k_vecs = block_of()
    spread("y", vecs, k_vecs)
    wait_u = []
    for j in streams:
        start_if(
            jnp.logical_and(s == 0, turned), tok.at[j], u_in.at[j], k_u + j, k_u + j, partner
        )
        wait_u.append(
            local_if(jnp.logical_and(s == 0, straight), tok.at[j], u_in.at[j], 16 + j)
        )

    @pl.when(s == 1)
    def _():
        pl.semaphore_wait(go, 1)

    k_w = block_of()
    deal("y", w_send, w_all, k_w)

    slot = lax.broadcasted_iota(jnp.int32, (1, 2 * N * M), 1)
    found = jnp.zeros_like(slot)
    for b in range(2 * NN):
        stored = 2 * (b % N * N + b // (2 * N)) + b // N % 2
        found = jnp.where(slot >= b * Q, order_in[stored] * Q - b * Q, found)
    kpos[...] = found + slot
    slot = lax.broadcasted_iota(jnp.int32, (2 * M, 1), 0)
    found = jnp.zeros_like(slot)
    for b in range(2 * N):
        found = jnp.where(
            slot >= b * Q, order_in[2 * (b % N * N + x) + b // N] * Q - b * Q, found
        )
    qpos[...] = found + slot

    arrived("y", vecs, k_vecs)
    params = vecs[0]
    for other in range(1, N):
        params = params + vecs[other]
    gain1, shift1, gain2, shift2, b_out, b_reduce = (params[r : r + 1] for r in range(6))
    lanes = lax.broadcasted_iota(jnp.int32, (1, WQ), 1)

    k_n1 = [block_of() for _ in streams]
    for j in streams:
        @pl.when(jnp.logical_or(s == 1, turned))
        def _():
            landed(u_in.at[j], k_u + j)

        wait_u[j]()
        normal, _ = normalize(u_in[j].astype(F32))
        n1[j, y] = (normal * gain1 + shift1).astype(BF16)
        spread("y", n1.at[j], k_n1[j])

    k_wexp = block_of()

    def wexp_cut(b):
        return wexp_in.at[:, pl.ds(pl.multiple_of(b * F, 128), F)]

    wait_wexp = local(wexp_cut(y), wexp.at[y], 4)
    for d in order:
        other = near(y, d)
        start(wexp_cut(other), wexp.at[y], k_wexp + d, k_wexp + y, along("y", other))
    start_if(jnp.logical_and(s == 1, turned), cot, cot_in, k_cot, k_cot, partner)
    wait_cot = local_if(jnp.logical_and(s == 1, straight), cot, cot_in, 5)

    k_kv = [block_of() for _ in streams]
    arrived("y", w_all, k_w)
    b_value = bias_at(rows_in[7:8], W, WQ, DH)
    b_query = bias_at(rows_in[6:7], 0, WQ, 0)
    for j in streams:
        arrived("y", n1.at[j], k_n1[j])
        rows = n1[j].reshape(M, D)
        made = mm(rows, w_all[:, :, 0:WKV].reshape(D, WKV))
        kv[j // 2, x, j % 2, :, 0:W] = made[:, 0:W].astype(BF16)
        kv[j // 2, x, j % 2, :, W:WKV] = (made[:, W:WKV] + b_value).astype(BF16)
        spread("x", kv.at[j // 2], k_kv[j], j % 2)
        query = mm(rows, w_all[:, :, WKV : WKV + WQ].reshape(D, WQ)) + b_query
        q_all[j] = (query * 0.125).astype(BF16)

    @pl.when(s == 0)
    def _():
        pl.semaphore_signal(go, inc=1, device_id=sibling, device_id_type=MESH)

    def only(h, values, first):
        inside = jnp.logical_and(lanes >= first + h * HEAD, lanes < first + (h + 1) * HEAD)
        return jnp.where(inside, values.astype(F32), 0.0)

    def scatter(number, j, term, base):
        part_send[number, j] = term.astype(BF16).reshape(N, Q, D)
        deal("y", part_send.at[number, j], part_recv.at[number, j], base)

    def collected(number, j, base):
        total = part_send[number, j, y].astype(F32)
        arrived("y", part_recv.at[number, j], base)
        for d in order:
            total = total + part_recv[number, j, near(y, d)].astype(F32)
        return total

    def pair(ref, i):
        return ref[2 * i : 2 * i + 2].reshape(2 * M, WQ)

    wout[0 : WQ - DH] = jnp.zeros((WQ - DH, D), BF16)
    wait_wout()
    k_po = [block_of() for _ in streams]
    for i in range(S):
        for side in range(2):
            arrived("x", kv.at[i], k_kv[2 * i + side], side)
        allowed = kpos[...] <= qpos[...]
        keys = kv[i, :, :, :, 0:WQ].reshape(2 * N * M, WQ)
        values = kv[i, :, :, :, W:WKV].reshape(2 * N * M, WQ)
        total = jnp.zeros((2 * M, WQ), F32)
        for h in range(heads):
            scores = mm_nt(only(h, pair(q_all, i), 0).astype(BF16), keys)
            scores = jnp.where(allowed, scores, -1e30)
            raised = jnp.exp(scores - jnp.max(scores, axis=-1, keepdims=True))
            part = raised / jnp.sum(raised, axis=-1, keepdims=True)
            probs[i * heads + h] = part
            total = total + only(h, mm(part.astype(BF16), values), WQ - DH)
        low = total.astype(BF16)
        mixed[2 * i : 2 * i + 2] = low.reshape(2, M, WQ)
        term = mm(low, wout[...])
        for side in range(2):
            scatter(0, 2 * i + side, term[side * M : (side + 1) * M], k_po[2 * i + side])

    k_n2 = [block_of() for _ in streams]
    for j in streams:
        state = u_in[j].astype(F32) + (collected(0, j, k_po[j]) + b_out)
        hidden[j] = state
        normal, _ = normalize(state)
        n2[j, y] = (normal * gain2 + shift2).astype(BF16)
        spread("y", n2.at[j], k_n2[j])

    wait_wexp()
    wait_wred()
    arrived("y", wexp, k_wexp)
    k_ff = [block_of() for _ in streams]
    for j in streams:
        arrived("y", n2.at[j], k_n2[j])
        before = mm(n2[j].reshape(M, D), wexp[...].reshape(D, F)) + bexp_in[...].astype(F32)
        square = before * before
        bent = jnp.tanh(GELU_SCALE * (before + GELU_CUBE * (square * before)))
        side = 0.5 * (1.0 + bent)
        low = (before * side).astype(BF16)
        active[j] = low
        slope[j] = side + 0.5 * before * (1.0 - bent * bent) * (
            GELU_SCALE * (1.0 + 3.0 * GELU_CUBE * square)
        )
        scatter(1, j, mm(low, wred[...]), k_ff[j])

    for j in streams:
        result = hidden[j] + (collected(1, j, k_ff[j]) + b_reduce)
        y_low[j] = result.astype(BF16)
        start_if(s == 0, y_low.at[j], u_in.at[j], k_u + j, k_u + j, sibling)

    @pl.when(jnp.logical_and(s == 1, turned))
    def _():
        landed(cot_in, k_cot)

    wait_cot()
    sm_own[...] = jnp.zeros_like(sm_own)
    sm_last[...] = jnp.zeros_like(sm_last)
    k_g = [block_of() for _ in streams]
    for j in streams:
        @pl.when(s == 1)
        def _():
            grad[j] = cot_in[j]

        @pl.when(s == 0)
        def _():
            landed(gp_in.at[j], k_gp + j)
            grad[j] = gp_in[j].astype(F32)

        low = grad[j].astype(BF16)
        g_all[j, y] = low
        spread("y", g_all.at[j], k_g[j])
        sm_own[5:6] += column_sums(low)

    start_if(turned, y_low, out_y, k_y, k_y, partner)
    wait_y = local_if(straight, y_low, out_y, 6)

    k_gf = [block_of() for _ in streams]
    for j in streams:
        arrived("y", g_all.at[j], k_g[j])
        low = (mm_nt(g_all[j].reshape(M, D), wred[...]) * slope[j]).astype(BF16)
        gb_all[j] = low
        scatter(2, j, mm_nt(low, wexp[...].reshape(D, F)), k_gf[j])

    def turn(index):
        return lax.rem(lax.rem(index, N) + lax.div(index, N), N)

    def piece(index):
        return turn(index) * N + lax.div(index, N)

    mine = piece(c)

    def pool(src, dst, base):
        dst[c] = src[mine]

        def make(d):
            other = near_ctx(d)
            return remote(src.at[piece(other)], dst.at[c], base + d, base + c, {"ctx": other})

        start_each(NN, make)

    def pooled(dst, base):
        @pl.loop(1, NN)
        def _(d):
            landed(dst.at[near_ctx(d)], base + near_ctx(d))

        total = dst[0].astype(F32)
        for other in range(1, NN):
            total = total + dst[other].astype(F32)
        return total

    g_rows = g_all[...].reshape(J * M, D)
    gb_rows = gb_all[...].reshape(J * M, F)
    sm_own[10:11] = column_sums(gb_rows)
    ff_s[:, 1] = mm_tn(active[...].reshape(J * M, F), g_rows).astype(BF16).reshape(NN, F // NN, D)
    ff_s[:, 0] = mm_tn(n2[...].reshape(J * M, D), gb_rows).astype(BF16).reshape(NN, D // NN, F)
    k_ffp = block_of(NN)
    pool(ff_s, ff_r, k_ffp)

    k_ga = [block_of() for _ in streams]
    for j in streams:
        grad_two = collected(2, j, k_gf[j])
        normal, factor = normalize(hidden[j])
        grad_hidden = grad[j] + norm_back(grad_two, normal, factor, gain2)
        grad[j] = grad_hidden
        low = grad_hidden.astype(BF16)
        ga_all[j, y] = low
        spread("y", ga_all.at[j], k_ga[j])
        sm_own[2:3] += column_sums(grad_two * normal)
        sm_own[3:4] += column_sums(grad_two)
        sm_own[4:5] += column_sums(low)

    k_dkv = [block_of() for _ in range(S)]
    for i in range(S):
        for j in (2 * i, 2 * i + 1):
            arrived("y", ga_all.at[j], k_ga[j])
            gm_all[j] = mm_nt(ga_all[j].reshape(M, D), wout[...]).astype(BF16)
        keys = kv[i, :, :, :, 0:WQ].reshape(2 * N * M, WQ)
        values = kv[i, :, :, :, W:WKV].reshape(2 * N * M, WQ)
        total = jnp.zeros((2 * M, WQ), F32)
        total_k = jnp.zeros((2 * N * M, WQ), F32)
        total_v = jnp.zeros((2 * N * M, WQ), F32)
        for h in range(heads):
            part = probs[i * heads + h]
            mixed_head = only(h, pair(gm_all, i), WQ - DH).astype(BF16)
            grad_probs = mm_nt(mixed_head, values)
            inner = jnp.sum(part * grad_probs, axis=-1, keepdims=True)
            grad_scores = (part * (grad_probs - inner)).astype(BF16)
            total = total + only(h, mm(grad_scores, keys), 0)
            total_k = total_k + mm_tn(grad_scores, only(h, pair(q_all, i), 0).astype(BF16))
            total_v = total_v + mm_tn(part.astype(BF16), mixed_head)
        shared = total_k[:, W:WQ] + total_v[:, 0:W]
        for lane, terms in ((0, total_k[:, 0:W]), (W, shared), (WQ, total_v[:, W:WQ])):
            dkv_send[i, :, :, :, lane : lane + W] = terms.astype(BF16).reshape(N, 2, M, W)
        deal("x", dkv_send.at[i], dkv_recv.at[i], k_dkv[i])
        low = (total.astype(BF16).astype(F32) * 0.125).astype(BF16)
        dq_all[2 * i : 2 * i + 2] = low.reshape(2, M, WQ)

    n1_rows = n1[...].reshape(J * M, D)
    dq_rows = dq_all[...].reshape(J * M, WQ)
    sm_own[8:9, 0:DH] = column_sums(dq_rows)[:, 0:DH]
    grad_q = mm_tn(n1_rows, dq_rows)
    grad_o = mm_tn(ga_all[...].reshape(J * M, D), mixed[...].reshape(J * M, WQ))
    qo_s[:, :, 0:W] = grad_q[:, 0:W].astype(BF16).reshape(NN, D // NN, W)
    qo_s[:, :, W:WQ] = (grad_q[:, W:WQ] + grad_o[:, 0:W]).astype(BF16).reshape(NN, D // NN, W)
    qo_s[:, :, WQ:WKV] = grad_o[:, W:WQ].astype(BF16).reshape(NN, D // NN, W)
    k_qop = block_of(NN)
    pool(qo_s, qo_r, k_qop)

    home = turn(c) == y
    finals = []
    late = []

    def hand_rows(src, dst, slot):
        base = block_of(NN)

        def make(d):
            return remote(src, dst(mine), base + d, base + c, {"ctx": near_ctx(d)})

        start_each(NN, make)
        late.append(local(src, dst(mine), slot))

        def finish():
            @pl.loop(1, NN)
            def _(d):
                landed(dst(piece(near_ctx(d))), base + near_ctx(d))

        finals.append(finish)

    def hand_across(src, dst, slot):
        base = block_of(NN)
        owner = turn(c)

        def make(d):
            return remote(
                src, dst(z, y), base + d, base + z * N + y,
                {"ctx": near_ctx(d), "fsdp": owner},
            )

        start_each(NN, make)
        start_if(
            jnp.logical_not(home), src, dst(z, y), base, base + z * N + y,
            {"ctx": c, "fsdp": owner},
        )
        late.append(local_if(home, src, dst(z, y), slot))

        def finish():
            @pl.loop(0, NN)
            def _(index):
                sub = lax.div(index, N)
                source = lax.rem(index, N)
                own = jnp.logical_and(jnp.logical_and(home, sub == z), source == y)

                @pl.when(jnp.logical_not(own))
                def _():
                    landed(dst(sub, source), base + index)

        finals.append(finish)

    def lane_block(ref, width):
        return lambda sub, source: ref.at[
            sub, :, pl.ds(pl.multiple_of(source * width, 128), width)
        ]

    k_gn = [block_of() for _ in streams]
    for j in streams:
        i, side = j // 2, j % 2
        if side == 0:
            arrived("x", dkv_recv.at[i], k_dkv[i])
        total = dkv_send[i, x, side].astype(F32)
        for d in order:
            total = total + dkv_recv[i, near(x, d), side].astype(F32)
        low = total.astype(BF16)
        dkv_all[j] = low
        scatter(
            3, j,
            mm_nt(dq_all[j], w_all[:, :, WKV : WKV + WQ].reshape(D, WQ))
            + mm_nt(low, w_all[:, :, 0:WKV].reshape(D, WKV)),
            k_gn[j],
        )

    dkv_rows = dkv_all[...].reshape(J * M, WKV)
    sm_own[9:10, 0:WKV] = column_sums(dkv_rows)
    kv_s[...] = mm_tn(n1_rows, dkv_rows).astype(BF16).reshape(NN, D // NN, WKV)
    k_kvp = block_of(NN)
    pool(kv_s, kv_r, k_kvp)

    sm_y[y] = sm_own[0:8]
    k_smy = block_of()
    spread("y", sm_y, k_smy)
    ff_sum[...] = pooled(ff_r, k_ffp).astype(BF16)
    hand_across(ff_sum.at[0], lane_block(out_wexp, F), 7)
    hand_rows(ff_sum.at[1], lambda index: out_wred.at[index], 8)

    for j in streams:
        grad_normed = collected(3, j, k_gn[j])
        normal, factor = normalize(u_in[j].astype(F32))
        grad_input = grad[j] + norm_back(grad_normed, normal, factor, gain1)
        dx_low[j] = grad_input.astype(BF16)
        start_if(s == 1, dx_low.at[j], gp_in.at[j], k_gp + j, k_gp + j, sibling)
        dx_buf[j] = grad_input
        sm_last[0:1] += column_sums(grad_normed * normal)
        sm_last[1:2] += column_sums(grad_normed)

    sm_ly[y] = sm_last[...]
    k_smly = block_of()
    spread("y", sm_ly, k_smly)
    start_if(turned, dx_buf, out_dx, k_dx, k_dx, partner)
    wait_dx = local_if(straight, dx_buf, out_dx, 9)

    def around(ref, base):
        start_each(
            NN,
            lambda d: remote(ref.at[c], ref.at[c], base + d, base + c, {"ctx": near_ctx(d)}),
        )

    def total_of(ref):
        rows = ref[0]
        for other in range(1, ref.shape[0]):
            rows = rows + ref[other]
        return rows

    kv_sum[...] = pooled(kv_r, k_kvp).astype(BF16)
    hand_across(kv_sum, lane_block(out_kv, WKV), 12)
    arrived("y", sm_ly, k_smly)
    sm_lc[c] = total_of(sm_ly)
    k_smlc = block_of(NN)
    around(sm_lc, k_smlc)
    arrived("y", sm_y, k_smy)
    sm_c[c, 0:8] = total_of(sm_y)
    sm_c[c, 8:16] = sm_own[8:16]
    k_smc = block_of(NN)
    around(sm_c, k_smc)
    qo_sum[...] = pooled(qo_r, k_qop).astype(BF16)
    hand_across(qo_sum.at[:, 0:WQ], lane_block(out_q, WQ), 10)
    hand_rows(qo_sum.at[:, W:WKV], lambda index: out_out.at[index], 11)

    for ref, base in ((sm_lc, k_smlc), (sm_c, k_smc)):
        @pl.loop(1, NN)
        def _(d):
            landed(ref.at[near_ctx(d)], base + near_ctx(d))

    out_small[0:8] = total_of(sm_lc)
    out_small[8:24] = total_of(sm_c)

    for finish in finals:
        finish()

    @pl.when(turned)
    def _():
        landed(out_y, k_y)
        landed(out_dx, k_dx)

    for wait in [wait_y, wait_dx] + late:
        wait()
    for drain in drains:
        drain()


def bias_at(values, lane, width, first):
    size = values.shape[1]
    row = lax.broadcasted_iota(jnp.int32, (size, width), 0)
    col = lax.broadcasted_iota(jnp.int32, (size, width), 1)
    put = jnp.where(row + first == col + lane, 1.0, 0.0).astype(BF16)
    wide = jnp.broadcast_to(values, (16, size)).astype(BF16)
    return mm(wide, put)[0:1]


def shards(
    tokens, cotangent, block_order, first_gain, first_shift, w_query, b_query, w_key, w_value,
    b_value, w_out, b_out, second_gain, second_shift, w_expand, b_expand, w_reduce, b_reduce,
):
    N = lax.axis_size("fsdp")
    S, R, D = tokens.shape
    F = w_reduce.shape[1]
    DH = D // N
    W = 2 * DH // 3
    WQ, WKV = 2 * W, 3 * W
    J, Q = 2 * S, R // 2
    NN, M = N * N, N * Q
    heads = DH // HEAD
    y = lax.axis_index("fsdp")

    rows = jnp.concatenate(
        [first_gain, first_shift, second_gain, second_shift, b_out, b_reduce, b_query, b_value]
    ).astype(F32)
    rows = jnp.pad(rows, ((0, 8), (0, 0)))

    def shape(dims, dtype):
        return jax.ShapeDtypeStruct(dims, dtype)

    vmem = pl.BlockSpec(memory_space=pltpu.VMEM)
    smem = pl.BlockSpec(memory_space=pltpu.SMEM)
    hbm = pl.BlockSpec(memory_space=pl.ANY)
    V = pltpu.VMEM
    slab = V((J, N, Q, D), BF16)
    rows_low, rows_full = V((J, Q, D), BF16), V((J, Q, D), F32)
    outs = pl.pallas_call(
        functools.partial(kernel, N, J, Q, D, F),
        out_shape=(
            shape((J, Q, D), BF16),
            shape((J, Q, D), F32),
            shape((N, D // NN, N * WKV), BF16),
            shape((N, D // NN, N * WQ), BF16),
            shape((NN, D // NN, WQ), BF16),
            shape((N, D // NN, N * F), BF16),
            shape((NN, F // NN, D), BF16),
            shape((24, D), F32),
        ),
        in_specs=[
            hbm, hbm, smem, vmem, vmem, hbm, hbm, hbm, hbm, hbm, hbm,
        ],
        out_specs=(hbm, hbm, hbm, hbm, hbm, hbm, hbm, vmem),
        scratch_shapes=[
            rows_low, rows_full, rows_low, rows_low, rows_full, rows_low, V((N, 8, D), F32),
            V((1, 2 * N * M), jnp.int32), V((2 * M, 1), jnp.int32),
            V((DH, D), BF16), V((DH, D), BF16), V((DH, D), BF16),
            V((N, DH, WKV + WQ), BF16), V((N, DH, WKV + WQ), BF16), V((N, DH, F), BF16),
            V((F, D), BF16), V((WQ, D), BF16),
            slab, slab, slab, slab,
            V((J, M, F), BF16), V((J, M, F), BF16), V((J, M, F), F32),
            V((J, M, WQ), BF16), V((S, N, 2, M, WKV), BF16),
            V((S * heads, 2 * M, 2 * N * M), F32),
            V((J, M, WQ), BF16), V((J, M, WQ), BF16), V((J, M, WQ), BF16), V((J, M, WKV), BF16),
            V((S, N, 2, M, WKV), BF16), V((S, N, 2, M, WKV), BF16),
            V((4, J, N, Q, D), BF16), V((4, J, N, Q, D), BF16), rows_full, rows_full,
            V((NN, 2, D // NN, D), BF16), V((NN, 2, D // NN, D), BF16), V((2, D // NN, D), BF16),
            V((NN, D // NN, WKV), BF16), V((NN, D // NN, WKV), BF16), V((D // NN, WKV), BF16),
            V((NN, D // NN, WKV), BF16), V((NN, D // NN, WKV), BF16), V((D // NN, WKV), BF16),
            V((N, 8, D), F32), V((NN, 16, D), F32), V((16, D), F32),
            V((N, 8, D), F32), V((NN, 8, D), F32), V((8, D), F32),
            pltpu.SemaphoreType.DMA((SEMS,)),
            pltpu.SemaphoreType.DMA((SEMS,)),
            pltpu.SemaphoreType.DMA((24,)),
            pltpu.SemaphoreType.REGULAR,
        ],
        compiler_params=pltpu.CompilerParams(
            collective_id=0, has_side_effects=True, vmem_limit_bytes=60 * 1024 * 1024
        ),
        name="layers",
    )(
        tokens.reshape(J, Q, D), cotangent.reshape(J, Q, D), block_order, rows, b_expand, w_query[0], w_key[0], w_value[0], w_out[0],
        w_expand[0], w_reduce[0],
    )
    out_y, out_dx, g_kv, g_q, g_out, g_exp, g_red, small = outs
    g_kv = g_kv.reshape(DH, N * WKV)
    g_q = g_q.reshape(DH, N * WQ)

    def whole(parts, width, first):
        pieces = [parts[:, b * width + first : b * width + first + DH] for b in range(N)]
        return jnp.concatenate(pieces, axis=1).astype(F32)[None]

    mine = lax.dynamic_slice(small, (0, y * DH), (16, DH))
    return (
        out_y.reshape(1, S, R, D),
        out_dx.reshape(1, S, R, D),
        mine[0:1],
        mine[1:2],
        whole(g_q, WQ, 0),
        small[16:17, 0:DH],
        whole(g_kv, WKV, 0),
        whole(g_kv, WKV, DH),
        small[17:18, DH:WKV],
        g_out.reshape(D, WQ)[:, WQ - DH :].T.astype(F32)[None],
        mine[12:13],
        mine[10:11],
        mine[11:12],
        g_exp.reshape(1, DH, N * F).astype(F32),
        small[18:19, 0:F],
        g_red.reshape(1, F, D).astype(F32),
        mine[13:14],
    )


def solution(mesh):
    vector = P("section", "fsdp")
    matrix = P("section", "fsdp", None)
    return jax.shard_map(
        shards,
        mesh=mesh,
        in_specs=(
            P("fsdp", "ctx", None), P("fsdp", "ctx", None), P(),
            vector, vector, matrix, vector, matrix, matrix, vector, matrix, vector, vector, vector,
            matrix, vector, matrix, vector,
        ),
        out_specs=(
            P("section", "fsdp", "ctx", None), P("section", "fsdp", "ctx", None),
            vector, vector, matrix, vector, matrix, matrix, vector, matrix, vector, vector, vector,
            matrix, vector, matrix, vector,
        ),
        check_vma=False,
    )
```

```python
import functools

import jax
import jax.numpy as jnp
from jax import lax
from jax.experimental import pallas as pl
from jax.experimental.pallas import tpu as pltpu
from jax.sharding import PartitionSpec as P

HEAD = 64
EPSILON = 1e-05
F32 = jnp.float32
BF16 = jnp.bfloat16
MESH = pl.DeviceIdType.MESH
GELU_SCALE = 0.7978845608028654
GELU_CUBE = 0.044715
SEMS = 80


def mm(left, right):
    return jnp.dot(left, right, preferred_element_type=F32)


def mm_nt(left, right):
    return lax.dot_general(left, right, (((1,), (1,)), ((), ())), preferred_element_type=F32)


def mm_tn(left, right):
    return lax.dot_general(left, right, (((0,), (0,)), ((), ())), preferred_element_type=F32)


def normalize(values):
    average = jnp.mean(values, axis=-1, keepdims=True)
    centered = values - average
    variance = jnp.mean(centered * centered, axis=-1, keepdims=True)
    factor = lax.rsqrt(variance + EPSILON)
    return centered * factor, factor


def norm_back(grad, normal, factor, gain):
    scaled = grad * gain
    return factor * (
        scaled
        - jnp.mean(scaled, axis=-1, keepdims=True)
        - normal * jnp.mean(scaled * normal, axis=-1, keepdims=True)
    )


def column_sums(values):
    return jnp.sum(values.astype(F32), axis=0, keepdims=True)


def kernel(
    N, J, Q, D, F,
    tok, cot, order_in, rows_in, bexp_in, wq_in, wk_in, wv_in, wout_in, wexp_in, wred_in,
    out_y, out_dx, out_kv, out_q, out_out, out_wexp, out_wred, out_small,
    u_in, cot_in, gp_in, y_low, dx_buf, dx_low, vecs, kpos, qpos,
    wq, wk, wv, w_send, w_all, wexp, wred, wout, n1, n2, g_all, ga_all, gb_all, active, slope,
    q_all, kv, probs, mixed, gm_all, dq_all, dkv_all, dkv_send, dkv_recv,
    part_send, part_recv, hidden, grad,
    ff_s, ff_in, ff_r, ff_sum, qo_s, qo_r, qo_sum, kv_s, kv_r, kv_sum,
    sm_y, sm_x, sm_z, sm_own, sm_ly, sm_lx, sm_lz, sm_last,
    ssem, rsem, lsem, go,
):
    NN = N * N
    M = N * Q
    S = J // 2
    DH = D // N
    W = 2 * DH // 3
    WQ, WKV = 2 * W, 3 * W
    heads = DH // HEAD
    s = lax.axis_index("section")
    c = lax.axis_index("ctx")
    y = lax.axis_index("fsdp")
    x = lax.rem(c, N)
    z = lax.div(c, N)
    straight = y == z
    turned = y != z
    order = tuple(sorted(range(1, N), key=lambda d: -min(d, N - d)))
    streams = range(J)
    sibling = {"section": 1 - s}
    partner = {"ctx": y * N + x, "fsdp": z}

    def near(v, d):
        return lax.rem(v + d, N)

    def near_ctx(d):
        return lax.rem(c + d, NN)

    counter = [0]

    def block_of():
        counter[0] += 1
        assert counter[0] <= SEMS
        return counter[0] - 1

    drains = []

    def remote(src, dst, send, recv, device):
        return pltpu.make_async_remote_copy(
            src_ref=src, dst_ref=dst, send_sem=ssem.at[send], recv_sem=rsem.at[recv],
            device_id=device, device_id_type=MESH,
        )

    def start(src, dst, slot, device):
        copy = remote(src, dst, slot, slot, device)
        copy.start()
        drains.append(copy.wait_send)

    def start_if(condition, src, dst, slot, device):
        copy = remote(src, dst, slot, slot, device)
        pl.when(condition)(lambda: copy.start())
        drains.append(lambda: pl.when(condition)(lambda: copy.wait_send()))

    def sent(ref, slot):
        remote(ref, ref, slot, 0, sibling).wait_send()

    def landed(dst, recv):
        remote(dst, dst, 0, recv, sibling).wait_recv()

    def local_if(condition, src, dst, slot):
        copy = pltpu.make_async_copy(src, dst, lsem.at[slot])
        pl.when(condition)(lambda: copy.start())
        return lambda: pl.when(condition)(lambda: copy.wait())

    def local(src, dst, slot):
        copy = pltpu.make_async_copy(src, dst, lsem.at[slot])
        copy.start()
        return copy.wait

    def along(axis, index):
        if axis == "y":
            return {"fsdp": index}
        if axis == "x":
            return {"ctx": z * N + index}
        return {"ctx": index * N + x}

    place = {"x": x, "y": y, "z": z}
    others = pl.ds(0, N - 1)
    rest_ctx = pl.ds(0, NN - 1)

    def spread(axis, ref, slot, *rest):
        me = place[axis]
        for d in order:
            at = ref.at[(me,) + rest]
            remote(at, at, slot, slot, along(axis, near(me, d))).start()
        drains.append(lambda: sent(ref.at[(others,) + rest], slot))

    def arrived(ref, slot, *rest):
        landed(ref.at[(others,) + rest], slot)

    def deal(axis, src, dst, slot):
        me = place[axis]
        for d in order:
            other = near(me, d)
            remote(src.at[other], dst.at[me], slot, slot, along(axis, other)).start()
        drains.append(lambda: sent(src.at[others], slot))

    barrier = pltpu.get_barrier_semaphore()
    everyone = 2 * NN * N

    @pl.loop(1, everyone)
    def _(d):
        index = lax.rem((s * NN + c) * N + y + d, everyone)
        pl.semaphore_signal(
            barrier, inc=1,
            device_id={
                "section": lax.div(index, NN * N),
                "ctx": lax.rem(lax.div(index, N), NN),
                "fsdp": lax.rem(index, N),
            },
            device_id_type=MESH,
        )

    wait_cuts = [local(a, b, 13 + j) for j, (a, b) in enumerate(((wq_in, wq), (wk_in, wk), (wv_in, wv)))]
    wait_wred = local(wred_in, wred, 0)
    wait_wout = local(wout_in, wout.at[pl.ds(WQ - DH, DH)], 1)

    put = (
        lax.broadcasted_iota(jnp.int32, (DH, D), 0) + y * DH
        == lax.broadcasted_iota(jnp.int32, (DH, D), 1)
    )
    vecs[y] = mm(rows_in[...].astype(BF16), jnp.where(put, 1.0, 0.0).astype(BF16))[0:8]

    def picker(width, shift, first):
        row = lax.broadcasted_iota(jnp.int32, (WQ, width), 0)
        col = lax.broadcasted_iota(jnp.int32, (WQ, width), 1)
        inside = jnp.logical_and(col >= first, col < first + DH)
        return jnp.where(
            jnp.logical_and(row - shift == col - first, inside), 1.0, 0.0
        ).astype(BF16)

    for wait in wait_cuts:
        wait()
    for b in range(N):
        lane = b * DH // W * W
        cut = slice(lane, lane + WQ)
        shift = b * DH - lane
        w_send[b, :, 0:WKV] = (
            mm(wk[:, cut], picker(WKV, shift, 0)) + mm(wv[:, cut], picker(WKV, shift, DH))
        ).astype(BF16)
        w_send[b, :, WKV : WKV + WQ] = mm(wq[:, cut], picker(WQ, shift, 0)).astype(BF16)
    w_all[y] = w_send[y]
    pl.semaphore_wait(barrier, everyone - 1)

    k_u = [block_of() for _ in streams]
    k_gp = [block_of() for _ in streams]
    k_cot, k_y, k_dx, k_ff_in, k_ff_pool, k_wexp_out, k_wred_out = (block_of() for _ in range(7))
    k_vecs = block_of()
    spread("y", vecs, k_vecs)
    wait_u = []
    for j in streams:
        start_if(
            jnp.logical_and(s == 0, turned), tok.at[j], u_in.at[j], k_u[j], partner
        )
        wait_u.append(
            local_if(jnp.logical_and(s == 0, straight), tok.at[j], u_in.at[j], 16 + j)
        )

    @pl.when(s == 1)
    def _():
        pl.semaphore_wait(go, 1)

    k_w = block_of()
    deal("y", w_send, w_all, k_w)

    slot = lax.broadcasted_iota(jnp.int32, (1, 2 * N * M), 1)
    found = jnp.zeros_like(slot)
    for b in range(2 * NN):
        stored = 2 * (b % N * N + b // (2 * N)) + b // N % 2
        found = jnp.where(slot >= b * Q, order_in[stored] * Q - b * Q, found)
    kpos[...] = found + slot
    slot = lax.broadcasted_iota(jnp.int32, (2 * M, 1), 0)
    found = jnp.zeros_like(slot)
    for b in range(2 * N):
        found = jnp.where(
            slot >= b * Q, order_in[2 * (b % N * N + x) + b // N] * Q - b * Q, found
        )
    qpos[...] = found + slot

    arrived(vecs, k_vecs)
    params = vecs[0]
    for other in range(1, N):
        params = params + vecs[other]
    gain1, shift1, gain2, shift2, b_out, b_reduce = (params[r : r + 1] for r in range(6))
    lanes = lax.broadcasted_iota(jnp.int32, (1, WQ), 1)

    k_n1 = [block_of() for _ in streams]
    for j in streams:
        @pl.when(jnp.logical_or(s == 1, turned))
        def _():
            landed(u_in.at[j], k_u[j])

        wait_u[j]()
        normal, _ = normalize(u_in[j].astype(F32))
        n1[j, y] = (normal * gain1 + shift1).astype(BF16)
        spread("y", n1.at[j], k_n1[j])

    k_kv = [block_of() for _ in streams]
    arrived(w_all, k_w)
    b_value = bias_at(rows_in[7:8], W, WQ, DH)
    b_query = bias_at(rows_in[6:7], 0, WQ, 0)
    for j in streams:
        arrived(n1.at[j], k_n1[j])
        rows = n1[j].reshape(M, D)
        made = mm(rows, w_all[:, :, 0:WKV].reshape(D, WKV))
        kv[j // 2, x, j % 2, :, 0:W] = made[:, 0:W].astype(BF16)
        kv[j // 2, x, j % 2, :, W:WKV] = (made[:, W:WKV] + b_value).astype(BF16)
        spread("x", kv.at[j // 2], k_kv[j], j % 2)
        query = mm(rows, w_all[:, :, WKV : WKV + WQ].reshape(D, WQ)) + b_query
        q_all[j] = (query * 0.125).astype(BF16)

    @pl.when(s == 0)
    def _():
        pl.semaphore_signal(go, inc=1, device_id=sibling, device_id_type=MESH)

    k_wexp = block_of()

    def wexp_cut(b):
        return wexp_in.at[:, pl.ds(pl.multiple_of(b * F, 128), F)]

    wait_wexp = local(wexp_cut(y), wexp.at[y], 4)
    for d in order:
        other = near(y, d)
        remote(wexp_cut(other), wexp.at[y], k_wexp, k_wexp, along("y", other)).start()
    drains.append(lambda: sent(wexp.at[others], k_wexp))
    start_if(jnp.logical_and(s == 1, turned), cot, cot_in, k_cot, partner)
    wait_cot = local_if(jnp.logical_and(s == 1, straight), cot, cot_in, 5)

    def only(h, values, first):
        inside = jnp.logical_and(lanes >= first + h * HEAD, lanes < first + (h + 1) * HEAD)
        return jnp.where(inside, values.astype(F32), 0.0)

    def scatter(number, j, term, base):
        part_send[number, j] = term.astype(BF16).reshape(N, Q, D)
        deal("y", part_send.at[number, j], part_recv.at[number, j], base)

    def collected(number, j, base):
        total = part_send[number, j, y].astype(F32)
        arrived(part_recv.at[number, j], base)
        for d in order:
            total = total + part_recv[number, j, near(y, d)].astype(F32)
        return total

    def pair(ref, i):
        return ref[2 * i : 2 * i + 2].reshape(2 * M, WQ)

    wout[0 : WQ - DH] = jnp.zeros((WQ - DH, D), BF16)
    wait_wout()
    k_po = [block_of() for _ in streams]
    for i in range(S):
        for side in range(2):
            arrived(kv.at[i], k_kv[2 * i + side], side)
        allowed = kpos[...] <= qpos[...]
        keys = kv[i, :, :, :, 0:WQ].reshape(2 * N * M, WQ)
        values = kv[i, :, :, :, W:WKV].reshape(2 * N * M, WQ)
        total = jnp.zeros((2 * M, WQ), F32)
        for h in range(heads):
            scores = mm_nt(only(h, pair(q_all, i), 0).astype(BF16), keys)
            scores = jnp.where(allowed, scores, -1e30)
            raised = jnp.exp(scores - jnp.max(scores, axis=-1, keepdims=True))
            part = raised / jnp.sum(raised, axis=-1, keepdims=True)
            probs[i * heads + h] = part
            total = total + only(h, mm(part.astype(BF16), values), WQ - DH)
        low = total.astype(BF16)
        mixed[2 * i : 2 * i + 2] = low.reshape(2, M, WQ)
        term = mm(low, wout[...])
        for side in range(2):
            scatter(0, 2 * i + side, term[side * M : (side + 1) * M], k_po[2 * i + side])

    k_n2 = [block_of() for _ in streams]
    for j in streams:
        state = u_in[j].astype(F32) + (collected(0, j, k_po[j]) + b_out)
        hidden[j] = state
        normal, _ = normalize(state)
        n2[j, y] = (normal * gain2 + shift2).astype(BF16)
        spread("y", n2.at[j], k_n2[j])

    wait_wexp()
    wait_wred()
    arrived(wexp, k_wexp)
    k_ff = [block_of() for _ in streams]
    for j in streams:
        arrived(n2.at[j], k_n2[j])
        before = mm(n2[j].reshape(M, D), wexp[...].reshape(D, F)) + bexp_in[...].astype(F32)
        square = before * before
        bent = jnp.tanh(GELU_SCALE * (before + GELU_CUBE * (square * before)))
        side = 0.5 * (1.0 + bent)
        low = (before * side).astype(BF16)
        active[j] = low
        slope[j] = side + 0.5 * before * (1.0 - bent * bent) * (
            GELU_SCALE * (1.0 + 3.0 * GELU_CUBE * square)
        )
        scatter(1, j, mm(low, wred[...]), k_ff[j])

    for j in streams:
        result = hidden[j] + (collected(1, j, k_ff[j]) + b_reduce)
        y_low[j] = result.astype(BF16)
        start_if(s == 0, y_low.at[j], u_in.at[j], k_u[j], sibling)

    def turn(index):
        return lax.rem(lax.rem(index, N) + lax.div(index, N), N)

    def piece(index):
        return turn(index) * N + lax.div(index, N)

    mine = piece(c)
    owner = turn(c)
    home = owner == y

    def pool(src, dst, slot):
        dst[c] = src[mine]

        @pl.loop(1, NN)
        def _(d):
            other = near_ctx(d)
            remote(src.at[piece(other)], dst.at[c], slot, slot, {"ctx": other}).start()

    def pooled(dst, slot):
        landed(dst.at[rest_ctx], slot)
        total = dst[0].astype(F32)
        for other in range(1, NN):
            total = total + dst[other].astype(F32)
        return total.astype(BF16)

    def hand_rows(src, out, slot):
        pltpu.make_async_copy(src, out.at[mine], rsem.at[slot]).start()

        @pl.loop(1, NN)
        def _(d):
            remote(src, out.at[mine], slot, slot, {"ctx": near_ctx(d)}).start()

    def across(out, width):
        return out.at[z, :, pl.ds(pl.multiple_of(y * width, 128), width)]

    def hand_across(src, out, width, slot):
        dst = across(out, width)

        @pl.when(home)
        def _():
            pltpu.make_async_copy(src, dst, rsem.at[slot]).start()

        @pl.when(jnp.logical_not(home))
        def _():
            remote(src, dst, slot, slot, {"fsdp": owner}).start()

        @pl.loop(1, NN)
        def _(d):
            remote(src, dst, slot, slot, {"ctx": near_ctx(d), "fsdp": owner}).start()

    def handed(out, slot, but_one):
        @pl.when(home)
        def _():
            sent(but_one, slot)

        @pl.when(jnp.logical_not(home))
        def _():
            sent(out, slot)

    def reduce_feed():
        landed(ff_in, k_ff_in)
        pool(ff_in, ff_r, k_ff_pool)
        ff_sum[...] = pooled(ff_r, k_ff_pool)

        @pl.loop(0, NN)
        def _(d):
            other = near_ctx(d)
            remote(
                ff_sum.at[0], across(out_wexp, F), k_wexp_out, k_wexp_out,
                {"section": 1 - s, "ctx": other, "fsdp": owner},
            ).start()
            remote(
                ff_sum.at[1], out_wred.at[mine], k_wred_out, k_wred_out,
                {"section": 1 - s, "ctx": other},
            ).start()

    drains.append(lambda: sent(ff_in.at[rest_ctx], k_ff_pool))
    drains.append(lambda: sent(out_wexp, k_wexp_out))
    drains.append(lambda: sent(out_wred, k_wred_out))

    @pl.when(jnp.logical_and(s == 1, turned))
    def _():
        landed(cot_in, k_cot)

    wait_cot()
    pl.when(s == 0)(reduce_feed)
    sm_own[...] = jnp.zeros_like(sm_own)
    sm_last[...] = jnp.zeros_like(sm_last)
    k_g = [block_of() for _ in streams]
    for j in streams:
        @pl.when(s == 1)
        def _():
            grad[j] = cot_in[j]

        @pl.when(s == 0)
        def _():
            landed(gp_in.at[j], k_gp[j])
            grad[j] = gp_in[j].astype(F32)

        low = grad[j].astype(BF16)
        g_all[j, y] = low
        spread("y", g_all.at[j], k_g[j])
        sm_own[5:6] += column_sums(low)

    start_if(turned, y_low, out_y, k_y, partner)
    wait_y = local_if(straight, y_low, out_y, 6)

    k_gf = [block_of() for _ in streams]
    for j in streams:
        arrived(g_all.at[j], k_g[j])
        low = (mm_nt(g_all[j].reshape(M, D), wred[...]) * slope[j]).astype(BF16)
        gb_all[j] = low
        scatter(2, j, mm_nt(low, wexp[...].reshape(D, F)), k_gf[j])

    g_rows = g_all[...].reshape(J * M, D)
    gb_rows = gb_all[...].reshape(J * M, F)
    sm_own[10:11] = column_sums(gb_rows)
    ff_s[:, 1] = mm_tn(active[...].reshape(J * M, F), g_rows).astype(BF16).reshape(NN, F // NN, D)
    ff_s[:, 0] = mm_tn(n2[...].reshape(J * M, D), gb_rows).astype(BF16).reshape(NN, D // NN, F)
    start(ff_s, ff_in, k_ff_in, sibling)

    k_ga = [block_of() for _ in streams]
    for j in streams:
        grad_two = collected(2, j, k_gf[j])
        normal, factor = normalize(hidden[j])
        grad_hidden = grad[j] + norm_back(grad_two, normal, factor, gain2)
        grad[j] = grad_hidden
        low = grad_hidden.astype(BF16)
        ga_all[j, y] = low
        spread("y", ga_all.at[j], k_ga[j])
        sm_own[2:3] += column_sums(grad_two * normal)
        sm_own[3:4] += column_sums(grad_two)
        sm_own[4:5] += column_sums(low)

    k_dkv = [block_of() for _ in range(S)]
    for i in range(S):
        for j in (2 * i, 2 * i + 1):
            arrived(ga_all.at[j], k_ga[j])
            gm_all[j] = mm_nt(ga_all[j].reshape(M, D), wout[...]).astype(BF16)
        keys = kv[i, :, :, :, 0:WQ].reshape(2 * N * M, WQ)
        values = kv[i, :, :, :, W:WKV].reshape(2 * N * M, WQ)
        total = jnp.zeros((2 * M, WQ), F32)
        total_k = jnp.zeros((2 * N * M, WQ), F32)
        total_v = jnp.zeros((2 * N * M, WQ), F32)
        for h in range(heads):
            part = probs[i * heads + h]
            mixed_head = only(h, pair(gm_all, i), WQ - DH).astype(BF16)
            grad_probs = mm_nt(mixed_head, values)
            inner = jnp.sum(part * grad_probs, axis=-1, keepdims=True)
            grad_scores = (part * (grad_probs - inner)).astype(BF16)
            total = total + only(h, mm(grad_scores, keys), 0)
            total_k = total_k + mm_tn(grad_scores, only(h, pair(q_all, i), 0).astype(BF16))
            total_v = total_v + mm_tn(part.astype(BF16), mixed_head)
        shared = total_k[:, W:WQ] + total_v[:, 0:W]
        for lane, terms in ((0, total_k[:, 0:W]), (W, shared), (WQ, total_v[:, W:WQ])):
            dkv_send[i, :, :, :, lane : lane + W] = terms.astype(BF16).reshape(N, 2, M, W)
        deal("x", dkv_send.at[i], dkv_recv.at[i], k_dkv[i])
        low = (total.astype(BF16).astype(F32) * 0.125).astype(BF16)
        dq_all[2 * i : 2 * i + 2] = low.reshape(2, M, WQ)

    n1_rows = n1[...].reshape(J * M, D)
    dq_rows = dq_all[...].reshape(J * M, WQ)
    sm_own[8:9, 0:DH] = column_sums(dq_rows)[:, 0:DH]
    grad_q = mm_tn(n1_rows, dq_rows)
    grad_o = mm_tn(ga_all[...].reshape(J * M, D), mixed[...].reshape(J * M, WQ))
    qo_s[:, :, 0:W] = grad_q[:, 0:W].astype(BF16).reshape(NN, D // NN, W)
    qo_s[:, :, W:WQ] = (grad_q[:, W:WQ] + grad_o[:, 0:W]).astype(BF16).reshape(NN, D // NN, W)
    qo_s[:, :, WQ:WKV] = grad_o[:, W:WQ].astype(BF16).reshape(NN, D // NN, W)
    k_qo, k_kv_pool, k_q_out, k_o_out, k_kv_out = (block_of() for _ in range(5))
    pl.when(s == 0)(lambda: pool(qo_s, qo_r, k_qo))

    def reduce_qo():
        qo_sum[...] = pooled(qo_r, k_qo)
        hand_across(qo_sum.at[:, 0:WQ], out_q, WQ, k_q_out)
        hand_rows(qo_sum.at[:, W:WKV], out_out, k_o_out)


    k_gn = [block_of() for _ in streams]
    for j in streams:
        i, side = j // 2, j % 2
        if side == 0:
            arrived(dkv_recv.at[i], k_dkv[i])
        total = dkv_send[i, x, side].astype(F32)
        for d in order:
            total = total + dkv_recv[i, near(x, d), side].astype(F32)
        low = total.astype(BF16)
        dkv_all[j] = low
        scatter(
            3, j,
            mm_nt(dq_all[j], w_all[:, :, WKV : WKV + WQ].reshape(D, WQ))
            + mm_nt(low, w_all[:, :, 0:WKV].reshape(D, WKV)),
            k_gn[j],
        )

    dkv_rows = dkv_all[...].reshape(J * M, WKV)
    sm_own[9:10, 0:WKV] = column_sums(dkv_rows)
    kv_s[...] = mm_tn(n1_rows, dkv_rows).astype(BF16).reshape(NN, D // NN, WKV)

    @pl.when(s == 0)
    def _():
        pool(kv_s, kv_r, k_kv_pool)
        reduce_qo()

    sm_y[y] = sm_own[0:8]
    k_smy = block_of()
    spread("y", sm_y, k_smy)

    for j in streams:
        grad_normed = collected(3, j, k_gn[j])
        normal, factor = normalize(u_in[j].astype(F32))
        grad_input = grad[j] + norm_back(grad_normed, normal, factor, gain1)
        dx_low[j] = grad_input.astype(BF16)
        start_if(s == 1, dx_low.at[j], gp_in.at[j], k_gp[j], sibling)
        dx_buf[j] = grad_input
        sm_last[0:1] += column_sums(grad_normed * normal)
        sm_last[1:2] += column_sums(grad_normed)

    sm_ly[y] = sm_last[...]
    k_smly = block_of()
    spread("y", sm_ly, k_smly)

    @pl.when(s == 1)
    def _():
        pool(kv_s, kv_r, k_kv_pool)
        pool(qo_s, qo_r, k_qo)

    def total_of(ref):
        rows = ref[0]
        for other in range(1, N):
            rows = rows + ref[other]
        return rows

    arrived(sm_y, k_smy)
    sm_x[x, 0:8] = total_of(sm_y)
    sm_x[x, 8:16] = sm_own[8:16]
    k_smx = block_of()
    spread("x", sm_x, k_smx)
    arrived(sm_ly, k_smly)
    sm_lx[x] = total_of(sm_ly)
    k_smlx = block_of()
    spread("x", sm_lx, k_smlx)
    start_if(turned, dx_buf, out_dx, k_dx, partner)
    wait_dx = local_if(straight, dx_buf, out_dx, 9)
    kv_sum[...] = pooled(kv_r, k_kv_pool)
    hand_across(kv_sum, out_kv, WKV, k_kv_out)
    arrived(sm_x, k_smx)
    sm_z[z] = total_of(sm_x)
    k_smz = block_of()
    spread("z", sm_z, k_smz)
    arrived(sm_lx, k_smlx)
    sm_lz[z] = total_of(sm_lx)
    k_smlz = block_of()
    spread("z", sm_lz, k_smlz)

    @pl.when(s == 1)
    def _():
        reduce_qo()
        reduce_feed()

    arrived(sm_z, k_smz)
    arrived(sm_lz, k_smlz)
    out_small[0:8] = total_of(sm_lz)
    out_small[8:24] = total_of(sm_z)
    drains.append(lambda: sent(qo_s.at[rest_ctx], k_qo))
    drains.append(lambda: sent(kv_s.at[rest_ctx], k_kv_pool))
    drains.append(lambda: handed(out_kv, k_kv_out, kv_r.at[rest_ctx]))
    drains.append(lambda: handed(out_q, k_q_out, qo_r.at[rest_ctx, :, pl.ds(0, WQ)]))
    drains.append(lambda: sent(out_out.at[rest_ctx], k_o_out))

    for ref, slot in (
        (out_kv, k_kv_out), (out_q, k_q_out), (out_out, k_o_out), (out_wexp, k_wexp_out),
        (out_wred, k_wred_out),
    ):
        landed(ref, slot)

    @pl.when(turned)
    def _():
        landed(out_y, k_y)
        landed(out_dx, k_dx)

    for wait in (wait_y, wait_dx):
        wait()
    for drain in drains:
        drain()


def bias_at(values, lane, width, first):
    size = values.shape[1]
    row = lax.broadcasted_iota(jnp.int32, (size, width), 0)
    col = lax.broadcasted_iota(jnp.int32, (size, width), 1)
    put = jnp.where(row + first == col + lane, 1.0, 0.0).astype(BF16)
    wide = jnp.broadcast_to(values, (16, size)).astype(BF16)
    return mm(wide, put)[0:1]


def shards(
    tokens, cotangent, block_order, first_gain, first_shift, w_query, b_query, w_key, w_value,
    b_value, w_out, b_out, second_gain, second_shift, w_expand, b_expand, w_reduce, b_reduce,
):
    N = lax.axis_size("fsdp")
    S, R, D = tokens.shape
    F = w_reduce.shape[1]
    DH = D // N
    W = 2 * DH // 3
    WQ, WKV = 2 * W, 3 * W
    J, Q = 2 * S, R // 2
    NN, M = N * N, N * Q
    heads = DH // HEAD
    y = lax.axis_index("fsdp")

    rows = jnp.concatenate(
        [first_gain, first_shift, second_gain, second_shift, b_out, b_reduce, b_query, b_value]
    ).astype(F32)
    rows = jnp.pad(rows, ((0, 8), (0, 0)))

    def shape(dims, dtype):
        return jax.ShapeDtypeStruct(dims, dtype)

    vmem = pl.BlockSpec(memory_space=pltpu.VMEM)
    smem = pl.BlockSpec(memory_space=pltpu.SMEM)
    hbm = pl.BlockSpec(memory_space=pl.ANY)
    V = pltpu.VMEM
    slab = V((J, N, Q, D), BF16)
    rows_low, rows_full = V((J, Q, D), BF16), V((J, Q, D), F32)
    outs = pl.pallas_call(
        functools.partial(kernel, N, J, Q, D, F),
        out_shape=(
            shape((J, Q, D), BF16),
            shape((J, Q, D), F32),
            shape((N, D // NN, N * WKV), BF16),
            shape((N, D // NN, N * WQ), BF16),
            shape((NN, D // NN, WQ), BF16),
            shape((N, D // NN, N * F), BF16),
            shape((NN, F // NN, D), BF16),
            shape((24, D), F32),
        ),
        in_specs=[
            hbm, hbm, smem, vmem, vmem, hbm, hbm, hbm, hbm, hbm, hbm,
        ],
        out_specs=(hbm, hbm, hbm, hbm, hbm, hbm, hbm, vmem),
        scratch_shapes=[
            rows_low, rows_full, rows_low, rows_low, rows_full, rows_low, V((N, 8, D), F32),
            V((1, 2 * N * M), jnp.int32), V((2 * M, 1), jnp.int32),
            V((DH, D), BF16), V((DH, D), BF16), V((DH, D), BF16),
            V((N, DH, WKV + WQ), BF16), V((N, DH, WKV + WQ), BF16), V((N, DH, F), BF16),
            V((F, D), BF16), V((WQ, D), BF16),
            slab, slab, slab, slab,
            V((J, M, F), BF16), V((J, M, F), BF16), V((J, M, F), F32),
            V((J, M, WQ), BF16), V((S, N, 2, M, WKV), BF16),
            V((S * heads, 2 * M, 2 * N * M), F32),
            V((J, M, WQ), BF16), V((J, M, WQ), BF16), V((J, M, WQ), BF16), V((J, M, WKV), BF16),
            V((S, N, 2, M, WKV), BF16), V((S, N, 2, M, WKV), BF16),
            V((4, J, N, Q, D), BF16), V((4, J, N, Q, D), BF16), rows_full, rows_full,
            V((NN, 2, D // NN, D), BF16), V((NN, 2, D // NN, D), BF16),
            V((NN, 2, D // NN, D), BF16), V((2, D // NN, D), BF16),
            V((NN, D // NN, WKV), BF16), V((NN, D // NN, WKV), BF16), V((D // NN, WKV), BF16),
            V((NN, D // NN, WKV), BF16), V((NN, D // NN, WKV), BF16), V((D // NN, WKV), BF16),
            V((N, 8, D), F32), V((N, 16, D), F32), V((N, 16, D), F32), V((16, D), F32),
            V((N, 8, D), F32), V((N, 8, D), F32), V((N, 8, D), F32), V((8, D), F32),
            pltpu.SemaphoreType.DMA((SEMS,)),
            pltpu.SemaphoreType.DMA((SEMS,)),
            pltpu.SemaphoreType.DMA((24,)),
            pltpu.SemaphoreType.REGULAR,
        ],
        compiler_params=pltpu.CompilerParams(
            collective_id=0, has_side_effects=True, vmem_limit_bytes=60 * 1024 * 1024
        ),
        name="layers",
    )(
        tokens.reshape(J, Q, D), cotangent.reshape(J, Q, D), block_order, rows, b_expand, w_query[0], w_key[0], w_value[0], w_out[0],
        w_expand[0], w_reduce[0],
    )
    out_y, out_dx, g_kv, g_q, g_out, g_exp, g_red, small = outs
    g_kv = g_kv.reshape(DH, N * WKV)
    g_q = g_q.reshape(DH, N * WQ)

    def whole(parts, width, first):
        pieces = [parts[:, b * width + first : b * width + first + DH] for b in range(N)]
        return jnp.concatenate(pieces, axis=1).astype(F32)[None]

    mine = lax.dynamic_slice(small, (0, y * DH), (16, DH))
    return (
        out_y.reshape(1, S, R, D),
        out_dx.reshape(1, S, R, D),
        mine[0:1],
        mine[1:2],
        whole(g_q, WQ, 0),
        small[16:17, 0:DH],
        whole(g_kv, WKV, 0),
        whole(g_kv, WKV, DH),
        small[17:18, DH:WKV],
        g_out.reshape(D, WQ)[:, WQ - DH :].T.astype(F32)[None],
        mine[12:13],
        mine[10:11],
        mine[11:12],
        g_exp.reshape(1, DH, N * F).astype(F32),
        small[18:19, 0:F],
        g_red.reshape(1, F, D).astype(F32),
        mine[13:14],
    )


def solution(mesh):
    vector = P("section", "fsdp")
    matrix = P("section", "fsdp", None)
    return jax.shard_map(
        shards,
        mesh=mesh,
        in_specs=(
            P("fsdp", "ctx", None), P("fsdp", "ctx", None), P(),
            vector, vector, matrix, vector, matrix, matrix, vector, matrix, vector, vector, vector,
            matrix, vector, matrix, vector,
        ),
        out_specs=(
            P("section", "fsdp", "ctx", None), P("section", "fsdp", "ctx", None),
            vector, vector, matrix, vector, matrix, matrix, vector, matrix, vector, vector, vector,
            matrix, vector, matrix, vector,
        ),
        check_vma=False,
    )
```

```python
import functools

import jax
import jax.numpy as jnp
from jax import lax
from jax.experimental import pallas as pl
from jax.experimental.pallas import tpu as pltpu
from jax.sharding import PartitionSpec as P

HEAD = 64
EPSILON = 1e-05
F32 = jnp.float32
BF16 = jnp.bfloat16
MESH = pl.DeviceIdType.MESH
GELU_SCALE = 0.7978845608028654
GELU_CUBE = 0.044715
SEMS = 80


def mm(left, right):
    return jnp.dot(left, right, preferred_element_type=F32)


def mm_nt(left, right):
    return lax.dot_general(left, right, (((1,), (1,)), ((), ())), preferred_element_type=F32)


def mm_tn(left, right):
    return lax.dot_general(left, right, (((0,), (0,)), ((), ())), preferred_element_type=F32)


def normalize(values):
    average = jnp.mean(values, axis=-1, keepdims=True)
    centered = values - average
    variance = jnp.mean(centered * centered, axis=-1, keepdims=True)
    factor = lax.rsqrt(variance + EPSILON)
    return centered * factor, factor


def norm_back(grad, normal, factor, gain):
    scaled = grad * gain
    return factor * (
        scaled
        - jnp.mean(scaled, axis=-1, keepdims=True)
        - normal * jnp.mean(scaled * normal, axis=-1, keepdims=True)
    )


def column_sums(values):
    return jnp.sum(values.astype(F32), axis=0, keepdims=True)


def kernel(
    N, J, Q, D, F,
    tok, cot, order_in, rows_in, bexp_in, wq_in, wk_in, wv_in, wout_in, wexp_in, wred_in,
    out_y, out_dx, out_kv, out_q, out_out, out_wexp, out_wred, out_small,
    u_in, cot_in, gp_in, y_low, dx_buf, dx_low, vecs, kpos, qpos,
    wq, wk, wv, w_send, w_all, wexp, wred, wout, n1, n2, g_all, ga_all, gb_all, active, slope,
    q_all, kv, probs, mixed, gm_all, dq_all, dkv_all, dkv_send, dkv_recv,
    part_send, part_recv, hidden, grad,
    ff_s, ff_in, ff_r, ff_one, ff_two, ff_sum, qo_s, qo_r, qo_sum, kv_s, kv_r, kv_sum,
    sm_y, sm_x, sm_z, sm_own, sm_ly, sm_lx, sm_lz, sm_last,
    ssem, rsem, lsem, go,
):
    NN = N * N
    M = N * Q
    S = J // 2
    DH = D // N
    W = 2 * DH // 3
    WQ, WKV = 2 * W, 3 * W
    heads = DH // HEAD
    s = lax.axis_index("section")
    c = lax.axis_index("ctx")
    y = lax.axis_index("fsdp")
    x = lax.rem(c, N)
    z = lax.div(c, N)
    straight = y == z
    turned = y != z
    order = tuple(sorted(range(1, N), key=lambda d: -min(d, N - d)))
    streams = range(J)
    sibling = {"section": 1 - s}
    partner = {"ctx": y * N + x, "fsdp": z}

    def near(v, d):
        return lax.rem(v + d, N)

    def near_ctx(d):
        return lax.rem(c + d, NN)

    counter = [0]

    def block_of():
        counter[0] += 1
        assert counter[0] <= SEMS
        return counter[0] - 1

    drains = []

    def remote(src, dst, send, recv, device):
        return pltpu.make_async_remote_copy(
            src_ref=src, dst_ref=dst, send_sem=ssem.at[send], recv_sem=rsem.at[recv],
            device_id=device, device_id_type=MESH,
        )

    def start(src, dst, slot, device):
        copy = remote(src, dst, slot, slot, device)
        copy.start()
        drains.append(copy.wait_send)

    def start_if(condition, src, dst, slot, device):
        copy = remote(src, dst, slot, slot, device)
        pl.when(condition)(lambda: copy.start())
        drains.append(lambda: pl.when(condition)(lambda: copy.wait_send()))

    def sent(ref, slot):
        remote(ref, ref, slot, 0, sibling).wait_send()

    def landed(dst, recv):
        remote(dst, dst, 0, recv, sibling).wait_recv()

    def local_if(condition, src, dst, slot):
        copy = pltpu.make_async_copy(src, dst, lsem.at[slot])
        pl.when(condition)(lambda: copy.start())
        return lambda: pl.when(condition)(lambda: copy.wait())

    def local(src, dst, slot):
        copy = pltpu.make_async_copy(src, dst, lsem.at[slot])
        copy.start()
        return copy.wait

    def along(axis, index):
        if axis == "y":
            return {"fsdp": index}
        if axis == "x":
            return {"ctx": z * N + index}
        return {"ctx": index * N + x}

    place = {"x": x, "y": y, "z": z}
    others = pl.ds(0, N - 1)
    rest_ctx = pl.ds(0, NN - 1)

    def send_spread(axis, ref, slot, *rest):
        me = place[axis]
        for d in order:
            at = ref.at[(me,) + rest]
            remote(at, at, slot, slot, along(axis, near(me, d))).start()

    def spread(axis, ref, slot, *rest):
        send_spread(axis, ref, slot, *rest)
        drains.append(lambda: sent(ref.at[(others,) + rest], slot))

    def arrived(ref, slot, *rest):
        landed(ref.at[(others,) + rest], slot)

    def send_deal(axis, src, dst, slot):
        me = place[axis]
        for d in order:
            other = near(me, d)
            remote(src.at[other], dst.at[me], slot, slot, along(axis, other)).start()

    def deal(axis, src, dst, slot):
        send_deal(axis, src, dst, slot)
        drains.append(lambda: sent(src.at[others], slot))

    barrier = pltpu.get_barrier_semaphore()
    everyone = 2 * NN * N

    @pl.loop(1, everyone)
    def _(d):
        index = lax.rem((s * NN + c) * N + y + d, everyone)
        pl.semaphore_signal(
            barrier, inc=1,
            device_id={
                "section": lax.div(index, NN * N),
                "ctx": lax.rem(lax.div(index, N), NN),
                "fsdp": lax.rem(index, N),
            },
            device_id_type=MESH,
        )

    wait_cuts = [local(a, b, 13 + j) for j, (a, b) in enumerate(((wq_in, wq), (wk_in, wk), (wv_in, wv)))]
    wait_wred = local(wred_in, wred, 0)
    wait_wout = local(wout_in, wout.at[pl.ds(WQ - DH, DH)], 1)

    put = (
        lax.broadcasted_iota(jnp.int32, (DH, D), 0) + y * DH
        == lax.broadcasted_iota(jnp.int32, (DH, D), 1)
    )
    vecs[y] = mm(rows_in[...].astype(BF16), jnp.where(put, 1.0, 0.0).astype(BF16))[0:8]

    def picker(width, shift, first):
        row = lax.broadcasted_iota(jnp.int32, (WQ, width), 0)
        col = lax.broadcasted_iota(jnp.int32, (WQ, width), 1)
        inside = jnp.logical_and(col >= first, col < first + DH)
        return jnp.where(
            jnp.logical_and(row - shift == col - first, inside), 1.0, 0.0
        ).astype(BF16)

    for wait in wait_cuts:
        wait()
    for b in range(N):
        lane = b * DH // W * W
        cut = slice(lane, lane + WQ)
        shift = b * DH - lane
        w_send[b, :, 0:WKV] = (
            mm(wk[:, cut], picker(WKV, shift, 0)) + mm(wv[:, cut], picker(WKV, shift, DH))
        ).astype(BF16)
        w_send[b, :, WKV : WKV + WQ] = mm(wq[:, cut], picker(WQ, shift, 0)).astype(BF16)
    w_all[y] = w_send[y]
    pl.semaphore_wait(barrier, everyone - 1)

    k_u = [block_of() for _ in streams]
    k_gp = [block_of() for _ in streams]
    k_cot, k_y, k_dx, k_ff_in, k_wexp_out, k_wred_out = (block_of() for _ in range(6))
    k_first, k_second, k_third = ([block_of(), block_of()] for _ in range(3))
    k_vecs = block_of()
    spread("y", vecs, k_vecs)
    wait_u = []
    for j in streams:
        start_if(
            jnp.logical_and(s == 0, turned), tok.at[j], u_in.at[j], k_u[j], partner
        )
        wait_u.append(
            local_if(jnp.logical_and(s == 0, straight), tok.at[j], u_in.at[j], 16 + j)
        )

    @pl.when(s == 1)
    def _():
        pl.semaphore_wait(go, 1)

    k_w = block_of()
    deal("y", w_send, w_all, k_w)

    slot = lax.broadcasted_iota(jnp.int32, (1, 2 * N * M), 1)
    found = jnp.zeros_like(slot)
    for b in range(2 * NN):
        stored = 2 * (b % N * N + b // (2 * N)) + b // N % 2
        found = jnp.where(slot >= b * Q, order_in[stored] * Q - b * Q, found)
    kpos[...] = found + slot
    slot = lax.broadcasted_iota(jnp.int32, (2 * M, 1), 0)
    found = jnp.zeros_like(slot)
    for b in range(2 * N):
        found = jnp.where(
            slot >= b * Q, order_in[2 * (b % N * N + x) + b // N] * Q - b * Q, found
        )
    qpos[...] = found + slot

    arrived(vecs, k_vecs)
    params = vecs[0]
    for other in range(1, N):
        params = params + vecs[other]
    gain1, shift1, gain2, shift2, b_out, b_reduce = (params[r : r + 1] for r in range(6))
    lanes = lax.broadcasted_iota(jnp.int32, (1, WQ), 1)

    k_n1 = [block_of() for _ in streams]
    for j in streams:
        @pl.when(jnp.logical_or(s == 1, turned))
        def _():
            landed(u_in.at[j], k_u[j])

        wait_u[j]()
        normal, _ = normalize(u_in[j].astype(F32))
        n1[j, y] = (normal * gain1 + shift1).astype(BF16)
        spread("y", n1.at[j], k_n1[j])

    k_kv = [block_of() for _ in streams]
    arrived(w_all, k_w)
    b_value = bias_at(rows_in[7:8], W, WQ, DH)
    b_query = bias_at(rows_in[6:7], 0, WQ, 0)
    for j in streams:
        arrived(n1.at[j], k_n1[j])
        rows = n1[j].reshape(M, D)
        made = mm(rows, w_all[:, :, 0:WKV].reshape(D, WKV))
        kv[j // 2, x, j % 2, :, 0:W] = made[:, 0:W].astype(BF16)
        kv[j // 2, x, j % 2, :, W:WKV] = (made[:, W:WKV] + b_value).astype(BF16)
        spread("x", kv.at[j // 2], k_kv[j], j % 2)
        query = mm(rows, w_all[:, :, WKV : WKV + WQ].reshape(D, WQ)) + b_query
        q_all[j] = (query * 0.125).astype(BF16)

    @pl.when(s == 0)
    def _():
        pl.semaphore_signal(go, inc=1, device_id=sibling, device_id_type=MESH)

    k_wexp = block_of()

    def wexp_cut(b):
        return wexp_in.at[:, pl.ds(pl.multiple_of(b * F, 128), F)]

    wait_wexp = local(wexp_cut(y), wexp.at[y], 4)
    for d in order:
        other = near(y, d)
        remote(wexp_cut(other), wexp.at[y], k_wexp, k_wexp, along("y", other)).start()
    drains.append(lambda: sent(wexp.at[others], k_wexp))
    start_if(jnp.logical_and(s == 1, turned), cot, cot_in, k_cot, partner)
    wait_cot = local_if(jnp.logical_and(s == 1, straight), cot, cot_in, 5)

    def only(h, values, first):
        inside = jnp.logical_and(lanes >= first + h * HEAD, lanes < first + (h + 1) * HEAD)
        return jnp.where(inside, values.astype(F32), 0.0)

    def scatter(number, j, term, base):
        part_send[number, j] = term.astype(BF16).reshape(N, Q, D)
        deal("y", part_send.at[number, j], part_recv.at[number, j], base)

    def collected(number, j, base):
        total = part_send[number, j, y].astype(F32)
        arrived(part_recv.at[number, j], base)
        for d in order:
            total = total + part_recv[number, j, near(y, d)].astype(F32)
        return total

    def pair(ref, i):
        return ref[2 * i : 2 * i + 2].reshape(2 * M, WQ)

    wout[0 : WQ - DH] = jnp.zeros((WQ - DH, D), BF16)
    wait_wout()
    k_po = [block_of() for _ in streams]
    for i in range(S):
        for side in range(2):
            arrived(kv.at[i], k_kv[2 * i + side], side)
        allowed = kpos[...] <= qpos[...]
        keys = kv[i, :, :, :, 0:WQ].reshape(2 * N * M, WQ)
        values = kv[i, :, :, :, W:WKV].reshape(2 * N * M, WQ)
        total = jnp.zeros((2 * M, WQ), F32)
        for h in range(heads):
            scores = mm_nt(only(h, pair(q_all, i), 0).astype(BF16), keys)
            scores = jnp.where(allowed, scores, -1e30)
            raised = jnp.exp(scores - jnp.max(scores, axis=-1, keepdims=True))
            part = raised / jnp.sum(raised, axis=-1, keepdims=True)
            probs[i * heads + h] = part
            total = total + only(h, mm(part.astype(BF16), values), WQ - DH)
        low = total.astype(BF16)
        mixed[2 * i : 2 * i + 2] = low.reshape(2, M, WQ)
        term = mm(low, wout[...])
        for side in range(2):
            scatter(0, 2 * i + side, term[side * M : (side + 1) * M], k_po[2 * i + side])

    k_n2 = [block_of() for _ in streams]
    for j in streams:
        state = u_in[j].astype(F32) + (collected(0, j, k_po[j]) + b_out)
        hidden[j] = state
        normal, _ = normalize(state)
        n2[j, y] = (normal * gain2 + shift2).astype(BF16)
        spread("y", n2.at[j], k_n2[j])

    wait_wexp()
    wait_wred()
    arrived(wexp, k_wexp)
    k_ff = [block_of() for _ in streams]
    for j in streams:
        arrived(n2.at[j], k_n2[j])
        before = mm(n2[j].reshape(M, D), wexp[...].reshape(D, F)) + bexp_in[...].astype(F32)
        square = before * before
        bent = jnp.tanh(GELU_SCALE * (before + GELU_CUBE * (square * before)))
        side = 0.5 * (1.0 + bent)
        low = (before * side).astype(BF16)
        active[j] = low
        slope[j] = side + 0.5 * before * (1.0 - bent * bent) * (
            GELU_SCALE * (1.0 + 3.0 * GELU_CUBE * square)
        )
        scatter(1, j, mm(low, wred[...]), k_ff[j])

    for j in streams:
        result = hidden[j] + (collected(1, j, k_ff[j]) + b_reduce)
        y_low[j] = result.astype(BF16)
        start_if(s == 0, y_low.at[j], u_in.at[j], k_u[j], sibling)

    def turn(index):
        return lax.rem(lax.rem(index, N) + lax.div(index, N), N)

    def piece(index):
        return turn(index) * N + lax.div(index, N)

    mine = piece(c)
    owner = turn(c)
    home = owner == y

    def pool(src, dst, slot):
        dst[c] = src[mine]

        @pl.loop(1, NN)
        def _(d):
            other = near_ctx(d)
            remote(src.at[piece(other)], dst.at[c], slot, slot, {"ctx": other}).start()

    def pooled(dst, slot):
        landed(dst.at[rest_ctx], slot)
        total = dst[0].astype(F32)
        for other in range(1, NN):
            total = total + dst[other].astype(F32)
        return total.astype(BF16)

    def hand_rows(src, out, slot):
        pltpu.make_async_copy(src, out.at[mine], rsem.at[slot]).start()

        @pl.loop(1, NN)
        def _(d):
            remote(src, out.at[mine], slot, slot, {"ctx": near_ctx(d)}).start()

    def across(out, width):
        return out.at[z, :, pl.ds(pl.multiple_of(y * width, 128), width)]

    def hand_across(src, out, width, slot):
        dst = across(out, width)

        @pl.when(home)
        def _():
            pltpu.make_async_copy(src, dst, rsem.at[slot]).start()

        @pl.when(jnp.logical_not(home))
        def _():
            remote(src, dst, slot, slot, {"fsdp": owner}).start()

        @pl.loop(1, NN)
        def _(d):
            remote(src, dst, slot, slot, {"ctx": near_ctx(d), "fsdp": owner}).start()

    def handed(out, slot, but_one):
        @pl.when(home)
        def _():
            sent(but_one, slot)

        @pl.when(jnp.logical_not(home))
        def _():
            sent(out, slot)

    axes = (("x", "z"), ("z", "x"))

    def total_at(axis, own, received):
        total = own.astype(F32)
        for d in order:
            total = total + received[near(place[axis], d)].astype(F32)
        return total.astype(BF16)

    def reduce_feed():
        landed(ff_in, k_ff_in)
        for k in range(2):
            send_deal(axes[k][0], ff_in.at[k], ff_r.at[k], k_first[k])
        for k in range(2):
            first, second = axes[k]
            arrived(ff_r.at[k], k_first[k])
            ff_one[k] = total_at(first, ff_in[k, place[first]], ff_r.at[k])
            send_deal(second, ff_one.at[k], ff_two.at[k], k_second[k])
        for k in range(2):
            second = axes[k][1]
            arrived(ff_two.at[k], k_second[k])
            ff_sum[k, place[second]] = total_at(
                second, ff_one[k, place[second]], ff_two.at[k]
            )
            send_spread(second, ff_sum.at[k], k_third[k])
        arrived(ff_sum.at[0], k_third[0])
        wide = out_wexp.at[:, :, pl.ds(pl.multiple_of(y * F, 128), F)]
        for d in range(N):
            remote(
                ff_sum.at[0], wide, k_wexp_out, k_wexp_out,
                {"section": 1 - s, "ctx": z * N + near(x, d), "fsdp": x},
            ).start()
        arrived(ff_sum.at[1], k_third[1])
        for d in range(N):
            remote(
                ff_sum.at[1], out_wred.at[z], k_wred_out, k_wred_out,
                {"section": 1 - s, "ctx": near(z, d) * N + x},
            ).start()

    for k in range(2):
        drains.append(lambda k=k: sent(ff_in.at[k, others], k_first[k]))
        drains.append(lambda k=k: sent(ff_one.at[k, others], k_second[k]))
        drains.append(lambda k=k: sent(ff_sum.at[k, others], k_third[k]))
    drains.append(lambda: sent(out_wexp, k_wexp_out))
    drains.append(lambda: sent(out_wred, k_wred_out))

    @pl.when(jnp.logical_and(s == 1, turned))
    def _():
        landed(cot_in, k_cot)

    wait_cot()
    pl.when(s == 0)(reduce_feed)
    sm_own[...] = jnp.zeros_like(sm_own)
    sm_last[...] = jnp.zeros_like(sm_last)
    k_g = [block_of() for _ in streams]
    for j in streams:
        @pl.when(s == 1)
        def _():
            grad[j] = cot_in[j]

        @pl.when(s == 0)
        def _():
            landed(gp_in.at[j], k_gp[j])
            grad[j] = gp_in[j].astype(F32)

        low = grad[j].astype(BF16)
        g_all[j, y] = low
        spread("y", g_all.at[j], k_g[j])
        sm_own[5:6] += column_sums(low)

    start_if(turned, y_low, out_y, k_y, partner)
    wait_y = local_if(straight, y_low, out_y, 6)

    k_gf = [block_of() for _ in streams]
    for j in streams:
        arrived(g_all.at[j], k_g[j])
        low = (mm_nt(g_all[j].reshape(M, D), wred[...]) * slope[j]).astype(BF16)
        gb_all[j] = low
        scatter(2, j, mm_nt(low, wexp[...].reshape(D, F)), k_gf[j])

    g_rows = g_all[...].reshape(J * M, D)
    gb_rows = gb_all[...].reshape(J * M, F)
    sm_own[10:11] = column_sums(gb_rows)
    ff_s[1] = (
        mm_tn(active[...].reshape(J * M, F), g_rows).astype(BF16).reshape(N, N, F // NN, D)
    )
    ff_s[0] = mm_tn(n2[...].reshape(J * M, D), gb_rows).astype(BF16).reshape(N, N, D // NN, F)
    start(ff_s, ff_in, k_ff_in, sibling)

    k_ga = [block_of() for _ in streams]
    for j in streams:
        grad_two = collected(2, j, k_gf[j])
        normal, factor = normalize(hidden[j])
        grad_hidden = grad[j] + norm_back(grad_two, normal, factor, gain2)
        grad[j] = grad_hidden
        low = grad_hidden.astype(BF16)
        ga_all[j, y] = low
        spread("y", ga_all.at[j], k_ga[j])
        sm_own[2:3] += column_sums(grad_two * normal)
        sm_own[3:4] += column_sums(grad_two)
        sm_own[4:5] += column_sums(low)

    k_dkv = [block_of() for _ in range(S)]
    for i in range(S):
        for j in (2 * i, 2 * i + 1):
            arrived(ga_all.at[j], k_ga[j])
            gm_all[j] = mm_nt(ga_all[j].reshape(M, D), wout[...]).astype(BF16)
        keys = kv[i, :, :, :, 0:WQ].reshape(2 * N * M, WQ)
        values = kv[i, :, :, :, W:WKV].reshape(2 * N * M, WQ)
        total = jnp.zeros((2 * M, WQ), F32)
        total_k = jnp.zeros((2 * N * M, WQ), F32)
        total_v = jnp.zeros((2 * N * M, WQ), F32)
        for h in range(heads):
            part = probs[i * heads + h]
            mixed_head = only(h, pair(gm_all, i), WQ - DH).astype(BF16)
            grad_probs = mm_nt(mixed_head, values)
            inner = jnp.sum(part * grad_probs, axis=-1, keepdims=True)
            grad_scores = (part * (grad_probs - inner)).astype(BF16)
            total = total + only(h, mm(grad_scores, keys), 0)
            total_k = total_k + mm_tn(grad_scores, only(h, pair(q_all, i), 0).astype(BF16))
            total_v = total_v + mm_tn(part.astype(BF16), mixed_head)
        shared = total_k[:, W:WQ] + total_v[:, 0:W]
        for lane, terms in ((0, total_k[:, 0:W]), (W, shared), (WQ, total_v[:, W:WQ])):
            dkv_send[i, :, :, :, lane : lane + W] = terms.astype(BF16).reshape(N, 2, M, W)
        deal("x", dkv_send.at[i], dkv_recv.at[i], k_dkv[i])
        low = (total.astype(BF16).astype(F32) * 0.125).astype(BF16)
        dq_all[2 * i : 2 * i + 2] = low.reshape(2, M, WQ)

    n1_rows = n1[...].reshape(J * M, D)
    dq_rows = dq_all[...].reshape(J * M, WQ)
    sm_own[8:9, 0:DH] = column_sums(dq_rows)[:, 0:DH]
    grad_q = mm_tn(n1_rows, dq_rows)
    grad_o = mm_tn(ga_all[...].reshape(J * M, D), mixed[...].reshape(J * M, WQ))
    qo_s[:, :, 0:W] = grad_q[:, 0:W].astype(BF16).reshape(NN, D // NN, W)
    qo_s[:, :, W:WQ] = (grad_q[:, W:WQ] + grad_o[:, 0:W]).astype(BF16).reshape(NN, D // NN, W)
    qo_s[:, :, WQ:WKV] = grad_o[:, W:WQ].astype(BF16).reshape(NN, D // NN, W)
    k_qo, k_kv_pool, k_q_out, k_o_out, k_kv_out = (block_of() for _ in range(5))
    pl.when(s == 0)(lambda: pool(qo_s, qo_r, k_qo))

    def reduce_qo():
        qo_sum[...] = pooled(qo_r, k_qo)
        hand_across(qo_sum.at[:, 0:WQ], out_q, WQ, k_q_out)
        hand_rows(qo_sum.at[:, W:WKV], out_out, k_o_out)


    k_gn = [block_of() for _ in streams]
    for j in streams:
        i, side = j // 2, j % 2
        if side == 0:
            arrived(dkv_recv.at[i], k_dkv[i])
        total = dkv_send[i, x, side].astype(F32)
        for d in order:
            total = total + dkv_recv[i, near(x, d), side].astype(F32)
        low = total.astype(BF16)
        dkv_all[j] = low
        scatter(
            3, j,
            mm_nt(dq_all[j], w_all[:, :, WKV : WKV + WQ].reshape(D, WQ))
            + mm_nt(low, w_all[:, :, 0:WKV].reshape(D, WKV)),
            k_gn[j],
        )

    dkv_rows = dkv_all[...].reshape(J * M, WKV)
    sm_own[9:10, 0:WKV] = column_sums(dkv_rows)
    kv_s[...] = mm_tn(n1_rows, dkv_rows).astype(BF16).reshape(NN, D // NN, WKV)

    @pl.when(s == 0)
    def _():
        pool(kv_s, kv_r, k_kv_pool)
        reduce_qo()

    sm_y[y] = sm_own[0:8]
    k_smy = block_of()
    spread("y", sm_y, k_smy)

    for j in streams:
        grad_normed = collected(3, j, k_gn[j])
        normal, factor = normalize(u_in[j].astype(F32))
        grad_input = grad[j] + norm_back(grad_normed, normal, factor, gain1)
        dx_low[j] = grad_input.astype(BF16)
        start_if(s == 1, dx_low.at[j], gp_in.at[j], k_gp[j], sibling)
        dx_buf[j] = grad_input
        sm_last[0:1] += column_sums(grad_normed * normal)
        sm_last[1:2] += column_sums(grad_normed)

    sm_ly[y] = sm_last[...]
    k_smly = block_of()
    spread("y", sm_ly, k_smly)

    @pl.when(s == 1)
    def _():
        pool(kv_s, kv_r, k_kv_pool)
        pool(qo_s, qo_r, k_qo)

    def total_of(ref):
        rows = ref[0]
        for other in range(1, N):
            rows = rows + ref[other]
        return rows

    arrived(sm_y, k_smy)
    sm_x[x, 0:8] = total_of(sm_y)
    sm_x[x, 8:16] = sm_own[8:16]
    k_smx = block_of()
    spread("x", sm_x, k_smx)
    arrived(sm_ly, k_smly)
    sm_lx[x] = total_of(sm_ly)
    k_smlx = block_of()
    spread("x", sm_lx, k_smlx)
    start_if(turned, dx_buf, out_dx, k_dx, partner)
    wait_dx = local_if(straight, dx_buf, out_dx, 9)
    kv_sum[...] = pooled(kv_r, k_kv_pool)
    hand_across(kv_sum, out_kv, WKV, k_kv_out)
    arrived(sm_x, k_smx)
    sm_z[z] = total_of(sm_x)
    k_smz = block_of()
    spread("z", sm_z, k_smz)
    arrived(sm_lx, k_smlx)
    sm_lz[z] = total_of(sm_lx)
    k_smlz = block_of()
    spread("z", sm_lz, k_smlz)

    @pl.when(s == 1)
    def _():
        reduce_qo()
        reduce_feed()

    arrived(sm_z, k_smz)
    arrived(sm_lz, k_smlz)
    out_small[0:8] = total_of(sm_lz)
    out_small[8:24] = total_of(sm_z)
    drains.append(lambda: sent(qo_s.at[rest_ctx], k_qo))
    drains.append(lambda: sent(kv_s.at[rest_ctx], k_kv_pool))
    drains.append(lambda: handed(out_kv, k_kv_out, kv_r.at[rest_ctx]))
    drains.append(lambda: handed(out_q, k_q_out, qo_r.at[rest_ctx, :, pl.ds(0, WQ)]))
    drains.append(lambda: sent(out_out.at[rest_ctx], k_o_out))

    for ref, slot in (
        (out_kv, k_kv_out), (out_q, k_q_out), (out_out, k_o_out), (out_wexp, k_wexp_out),
        (out_wred, k_wred_out),
    ):
        landed(ref, slot)

    @pl.when(turned)
    def _():
        landed(out_y, k_y)
        landed(out_dx, k_dx)

    for wait in (wait_y, wait_dx):
        wait()
    for drain in drains:
        drain()


def bias_at(values, lane, width, first):
    size = values.shape[1]
    row = lax.broadcasted_iota(jnp.int32, (size, width), 0)
    col = lax.broadcasted_iota(jnp.int32, (size, width), 1)
    put = jnp.where(row + first == col + lane, 1.0, 0.0).astype(BF16)
    wide = jnp.broadcast_to(values, (16, size)).astype(BF16)
    return mm(wide, put)[0:1]


def shards(
    tokens, cotangent, block_order, first_gain, first_shift, w_query, b_query, w_key, w_value,
    b_value, w_out, b_out, second_gain, second_shift, w_expand, b_expand, w_reduce, b_reduce,
):
    N = lax.axis_size("fsdp")
    S, R, D = tokens.shape
    F = w_reduce.shape[1]
    DH = D // N
    W = 2 * DH // 3
    WQ, WKV = 2 * W, 3 * W
    J, Q = 2 * S, R // 2
    NN, M = N * N, N * Q
    heads = DH // HEAD
    y = lax.axis_index("fsdp")

    rows = jnp.concatenate(
        [first_gain, first_shift, second_gain, second_shift, b_out, b_reduce, b_query, b_value]
    ).astype(F32)
    rows = jnp.pad(rows, ((0, 8), (0, 0)))

    def shape(dims, dtype):
        return jax.ShapeDtypeStruct(dims, dtype)

    vmem = pl.BlockSpec(memory_space=pltpu.VMEM)
    smem = pl.BlockSpec(memory_space=pltpu.SMEM)
    hbm = pl.BlockSpec(memory_space=pl.ANY)
    V = pltpu.VMEM
    slab = V((J, N, Q, D), BF16)
    whole_sum, part_sum = V((2, N, N, D // NN, D), BF16), V((2, N, D // NN, D), BF16)
    rows_low, rows_full = V((J, Q, D), BF16), V((J, Q, D), F32)
    outs = pl.pallas_call(
        functools.partial(kernel, N, J, Q, D, F),
        out_shape=(
            shape((J, Q, D), BF16),
            shape((J, Q, D), F32),
            shape((N, D // NN, N * WKV), BF16),
            shape((N, D // NN, N * WQ), BF16),
            shape((NN, D // NN, WQ), BF16),
            shape((N, D // NN, N * F), BF16),
            shape((N, N, F // NN, D), BF16),
            shape((24, D), F32),
        ),
        in_specs=[
            hbm, hbm, smem, vmem, vmem, hbm, hbm, hbm, hbm, hbm, hbm,
        ],
        out_specs=(hbm, hbm, hbm, hbm, hbm, hbm, hbm, vmem),
        scratch_shapes=[
            rows_low, rows_full, rows_low, rows_low, rows_full, rows_low, V((N, 8, D), F32),
            V((1, 2 * N * M), jnp.int32), V((2 * M, 1), jnp.int32),
            V((DH, D), BF16), V((DH, D), BF16), V((DH, D), BF16),
            V((N, DH, WKV + WQ), BF16), V((N, DH, WKV + WQ), BF16), V((N, DH, F), BF16),
            V((F, D), BF16), V((WQ, D), BF16),
            slab, slab, slab, slab,
            V((J, M, F), BF16), V((J, M, F), BF16), V((J, M, F), F32),
            V((J, M, WQ), BF16), V((S, N, 2, M, WKV), BF16),
            V((S * heads, 2 * M, 2 * N * M), F32),
            V((J, M, WQ), BF16), V((J, M, WQ), BF16), V((J, M, WQ), BF16), V((J, M, WKV), BF16),
            V((S, N, 2, M, WKV), BF16), V((S, N, 2, M, WKV), BF16),
            V((4, J, N, Q, D), BF16), V((4, J, N, Q, D), BF16), rows_full, rows_full,
            whole_sum, whole_sum, whole_sum, part_sum, part_sum, part_sum,
            V((NN, D // NN, WKV), BF16), V((NN, D // NN, WKV), BF16), V((D // NN, WKV), BF16),
            V((NN, D // NN, WKV), BF16), V((NN, D // NN, WKV), BF16), V((D // NN, WKV), BF16),
            V((N, 8, D), F32), V((N, 16, D), F32), V((N, 16, D), F32), V((16, D), F32),
            V((N, 8, D), F32), V((N, 8, D), F32), V((N, 8, D), F32), V((8, D), F32),
            pltpu.SemaphoreType.DMA((SEMS,)),
            pltpu.SemaphoreType.DMA((SEMS,)),
            pltpu.SemaphoreType.DMA((24,)),
            pltpu.SemaphoreType.REGULAR,
        ],
        compiler_params=pltpu.CompilerParams(
            collective_id=0, has_side_effects=True, vmem_limit_bytes=60 * 1024 * 1024
        ),
        name="layers",
    )(
        tokens.reshape(J, Q, D), cotangent.reshape(J, Q, D), block_order, rows, b_expand, w_query[0], w_key[0], w_value[0], w_out[0],
        w_expand[0], w_reduce[0],
    )
    out_y, out_dx, g_kv, g_q, g_out, g_exp, g_red, small = outs
    g_kv = g_kv.reshape(DH, N * WKV)
    g_q = g_q.reshape(DH, N * WQ)

    def whole(parts, width, first):
        pieces = [parts[:, b * width + first : b * width + first + DH] for b in range(N)]
        return jnp.concatenate(pieces, axis=1).astype(F32)[None]

    mine = lax.dynamic_slice(small, (0, y * DH), (16, DH))
    return (
        out_y.reshape(1, S, R, D),
        out_dx.reshape(1, S, R, D),
        mine[0:1],
        mine[1:2],
        whole(g_q, WQ, 0),
        small[16:17, 0:DH],
        whole(g_kv, WKV, 0),
        whole(g_kv, WKV, DH),
        small[17:18, DH:WKV],
        g_out.reshape(D, WQ)[:, WQ - DH :].T.astype(F32)[None],
        mine[12:13],
        mine[10:11],
        mine[11:12],
        g_exp.reshape(1, DH, N * F).astype(F32),
        small[18:19, 0:F],
        g_red.reshape(1, F, D).astype(F32),
        mine[13:14],
    )


def solution(mesh):
    vector = P("section", "fsdp")
    matrix = P("section", "fsdp", None)
    return jax.shard_map(
        shards,
        mesh=mesh,
        in_specs=(
            P("fsdp", "ctx", None), P("fsdp", "ctx", None), P(),
            vector, vector, matrix, vector, matrix, matrix, vector, matrix, vector, vector, vector,
            matrix, vector, matrix, vector,
        ),
        out_specs=(
            P("section", "fsdp", "ctx", None), P("section", "fsdp", "ctx", None),
            vector, vector, matrix, vector, matrix, matrix, vector, matrix, vector, vector, vector,
            matrix, vector, matrix, vector,
        ),
        check_vma=False,
    )
```

```python
import functools

import jax
import jax.numpy as jnp
from jax import lax
from jax.experimental import pallas as pl
from jax.experimental.pallas import tpu as pltpu
from jax.sharding import PartitionSpec as P

HEAD = 64
EPSILON = 1e-05
F32 = jnp.float32
BF16 = jnp.bfloat16
MESH = pl.DeviceIdType.MESH
GELU_SCALE = 0.7978845608028654
GELU_CUBE = 0.044715
SEMS = 80


def mm(left, right):
    return jnp.dot(left, right, preferred_element_type=F32)


def mm_nt(left, right):
    return lax.dot_general(left, right, (((1,), (1,)), ((), ())), preferred_element_type=F32)


def mm_tn(left, right):
    return lax.dot_general(left, right, (((0,), (0,)), ((), ())), preferred_element_type=F32)


def normalize(values):
    average = jnp.mean(values, axis=-1, keepdims=True)
    centered = values - average
    variance = jnp.mean(centered * centered, axis=-1, keepdims=True)
    factor = lax.rsqrt(variance + EPSILON)
    return centered * factor, factor


def norm_back(grad, normal, factor, gain):
    scaled = grad * gain
    return factor * (
        scaled
        - jnp.mean(scaled, axis=-1, keepdims=True)
        - normal * jnp.mean(scaled * normal, axis=-1, keepdims=True)
    )


def column_sums(values):
    return jnp.sum(values.astype(F32), axis=0, keepdims=True)


def kernel(
    N, J, Q, D, F,
    tok, cot, order_in, rows_in, bexp_in, wq_in, wk_in, wv_in, wout_in, wexp_in, wred_in,
    out_y, out_dx, out_kv, out_q, out_out, out_wexp, out_wred, out_small,
    u_in, cot_in, gp_in, y_low, dx_buf, dx_low, vecs, kpos, qpos,
    wq, wk, wv, w_send, w_all, wexp, wred, wout, n1, n2, g_all, ga_all, gb_all, active, slope,
    q_all, kv, probs, mixed, gm_all, dq_all, dkv_all, dkv_send, dkv_recv,
    part_send, part_recv, hidden, grad,
    ff_s, ff_in, ff_r, ff_one, ff_two, ff_sum, qo_s, qo_r, qo_sum, kv_s, kv_r, kv_sum,
    sm_y, sm_x, sm_z, sm_own, sm_ly, sm_lx, sm_lz, sm_last,
    ssem, rsem, lsem, go,
):
    NN = N * N
    M = N * Q
    S = J // 2
    DH = D // N
    W = 2 * DH // 3
    WQ, WKV = 2 * W, 3 * W
    heads = DH // HEAD
    s = lax.axis_index("section")
    c = lax.axis_index("ctx")
    y = lax.axis_index("fsdp")
    x = lax.rem(c, N)
    z = lax.div(c, N)
    straight = y == z
    turned = y != z
    order = tuple(sorted(range(1, N), key=lambda d: -min(d, N - d)))
    streams = range(J)
    sibling = {"section": 1 - s}
    partner = {"ctx": y * N + x, "fsdp": z}

    def near(v, d):
        return lax.rem(v + d, N)

    def near_ctx(d):
        return lax.rem(c + d, NN)

    counter = [0]

    def block_of():
        counter[0] += 1
        assert counter[0] <= SEMS
        return counter[0] - 1

    drains = []

    def remote(src, dst, send, recv, device):
        return pltpu.make_async_remote_copy(
            src_ref=src, dst_ref=dst, send_sem=ssem.at[send], recv_sem=rsem.at[recv],
            device_id=device, device_id_type=MESH,
        )

    def start(src, dst, slot, device):
        copy = remote(src, dst, slot, slot, device)
        copy.start()
        drains.append(copy.wait_send)

    def start_if(condition, src, dst, slot, device):
        copy = remote(src, dst, slot, slot, device)
        pl.when(condition)(lambda: copy.start())
        drains.append(lambda: pl.when(condition)(lambda: copy.wait_send()))

    def sent(ref, slot):
        remote(ref, ref, slot, 0, sibling).wait_send()

    def landed(dst, recv):
        remote(dst, dst, 0, recv, sibling).wait_recv()

    def local_if(condition, src, dst, slot):
        copy = pltpu.make_async_copy(src, dst, lsem.at[slot])
        pl.when(condition)(lambda: copy.start())
        return lambda: pl.when(condition)(lambda: copy.wait())

    def local(src, dst, slot):
        copy = pltpu.make_async_copy(src, dst, lsem.at[slot])
        copy.start()
        return copy.wait

    def along(axis, index):
        if axis == "y":
            return {"fsdp": index}
        if axis == "x":
            return {"ctx": z * N + index}
        return {"ctx": index * N + x}

    place = {"x": x, "y": y, "z": z}
    others = pl.ds(0, N - 1)
    rest_ctx = pl.ds(0, NN - 1)

    def send_spread(axis, ref, slot, *rest):
        me = place[axis]
        for d in order:
            at = ref.at[(me,) + rest]
            remote(at, at, slot, slot, along(axis, near(me, d))).start()

    def spread(axis, ref, slot, *rest):
        send_spread(axis, ref, slot, *rest)
        drains.append(lambda: sent(ref.at[(others,) + rest], slot))

    def arrived(ref, slot, *rest):
        landed(ref.at[(others,) + rest], slot)

    def send_deal(axis, src, dst, slot):
        me = place[axis]
        for d in order:
            other = near(me, d)
            remote(src.at[other], dst.at[me], slot, slot, along(axis, other)).start()

    def deal(axis, src, dst, slot):
        send_deal(axis, src, dst, slot)
        drains.append(lambda: sent(src.at[others], slot))

    barrier = pltpu.get_barrier_semaphore()

    def greet(device):
        pl.semaphore_signal(barrier, inc=1, device_id=device, device_id_type=MESH)

    @pl.loop(1, NN * N)
    def _(d):
        index = lax.rem(c * N + y + d, NN * N)
        greet({"ctx": lax.div(index, N), "fsdp": lax.rem(index, N)})

    @pl.loop(0, NN)
    def _(d):
        greet({"section": 1 - s, "ctx": z * N + lax.rem(d, N), "fsdp": lax.div(d, N)})

    @pl.loop(1, N)
    def _(d):
        greet({"section": 1 - s, "ctx": near(z, d) * N + x})

    greeted = NN * N - 1 + NN + N - 1
    wait_cuts = [local(a, b, 13 + j) for j, (a, b) in enumerate(((wq_in, wq), (wk_in, wk), (wv_in, wv)))]
    wait_wred = local(wred_in, wred, 0)
    wait_wout = local(wout_in, wout.at[pl.ds(WQ - DH, DH)], 1)

    put = (
        lax.broadcasted_iota(jnp.int32, (DH, D), 0) + y * DH
        == lax.broadcasted_iota(jnp.int32, (DH, D), 1)
    )
    vecs[y] = mm(rows_in[...].astype(BF16), jnp.where(put, 1.0, 0.0).astype(BF16))[0:8]

    def picker(width, shift, first):
        row = lax.broadcasted_iota(jnp.int32, (WQ, width), 0)
        col = lax.broadcasted_iota(jnp.int32, (WQ, width), 1)
        inside = jnp.logical_and(col >= first, col < first + DH)
        return jnp.where(
            jnp.logical_and(row - shift == col - first, inside), 1.0, 0.0
        ).astype(BF16)

    for wait in wait_cuts:
        wait()
    for b in range(N):
        lane = b * DH // W * W
        cut = slice(lane, lane + WQ)
        shift = b * DH - lane
        w_send[b, :, 0:WKV] = (
            mm(wk[:, cut], picker(WKV, shift, 0)) + mm(wv[:, cut], picker(WKV, shift, DH))
        ).astype(BF16)
        w_send[b, :, WKV : WKV + WQ] = mm(wq[:, cut], picker(WQ, shift, 0)).astype(BF16)
    w_all[y] = w_send[y]
    pl.semaphore_wait(barrier, greeted)

    k_u = [block_of() for _ in streams]
    k_gp = [block_of() for _ in streams]
    k_cot, k_y, k_dx, k_wexp_out, k_wred_out = (block_of() for _ in range(5))
    k_ff_in, k_first, k_second, k_third = ([block_of(), block_of()] for _ in range(4))
    k_vecs = block_of()
    spread("y", vecs, k_vecs)
    wait_u = []
    for j in streams:
        start_if(
            jnp.logical_and(s == 0, turned), tok.at[j], u_in.at[j], k_u[j], partner
        )
        wait_u.append(
            local_if(jnp.logical_and(s == 0, straight), tok.at[j], u_in.at[j], 16 + j)
        )

    @pl.when(s == 1)
    def _():
        pl.semaphore_wait(go, 1)

    k_w = block_of()
    deal("y", w_send, w_all, k_w)

    slot = lax.broadcasted_iota(jnp.int32, (1, 2 * N * M), 1)
    found = jnp.zeros_like(slot)
    for b in range(2 * NN):
        stored = 2 * (b % N * N + b // (2 * N)) + b // N % 2
        found = jnp.where(slot >= b * Q, order_in[stored] * Q - b * Q, found)
    kpos[...] = found + slot
    slot = lax.broadcasted_iota(jnp.int32, (2 * M, 1), 0)
    found = jnp.zeros_like(slot)
    for b in range(2 * N):
        found = jnp.where(
            slot >= b * Q, order_in[2 * (b % N * N + x) + b // N] * Q - b * Q, found
        )
    qpos[...] = found + slot

    arrived(vecs, k_vecs)
    params = vecs[0]
    for other in range(1, N):
        params = params + vecs[other]
    gain1, shift1, gain2, shift2, b_out, b_reduce = (params[r : r + 1] for r in range(6))
    lanes = lax.broadcasted_iota(jnp.int32, (1, WQ), 1)

    k_n1 = [block_of() for _ in streams]
    for j in streams:
        @pl.when(jnp.logical_or(s == 1, turned))
        def _():
            landed(u_in.at[j], k_u[j])

        wait_u[j]()
        normal, _ = normalize(u_in[j].astype(F32))
        n1[j, y] = (normal * gain1 + shift1).astype(BF16)
        spread("y", n1.at[j], k_n1[j])

    k_kv = [block_of() for _ in streams]
    arrived(w_all, k_w)
    b_value = bias_at(rows_in[7:8], W, WQ, DH)
    b_query = bias_at(rows_in[6:7], 0, WQ, 0)
    for j in streams:
        arrived(n1.at[j], k_n1[j])
        rows = n1[j].reshape(M, D)
        made = mm(rows, w_all[:, :, 0:WKV].reshape(D, WKV))
        kv[j // 2, x, j % 2, :, 0:W] = made[:, 0:W].astype(BF16)
        kv[j // 2, x, j % 2, :, W:WKV] = (made[:, W:WKV] + b_value).astype(BF16)
        spread("x", kv.at[j // 2], k_kv[j], j % 2)
        query = mm(rows, w_all[:, :, WKV : WKV + WQ].reshape(D, WQ)) + b_query
        q_all[j] = (query * 0.125).astype(BF16)

    @pl.when(s == 0)
    def _():
        pl.semaphore_signal(go, inc=1, device_id=sibling, device_id_type=MESH)

    k_wexp = block_of()

    def wexp_cut(b):
        return wexp_in.at[:, pl.ds(pl.multiple_of(b * F, 128), F)]

    wait_wexp = local(wexp_cut(y), wexp.at[y], 4)
    for d in order:
        other = near(y, d)
        remote(wexp_cut(other), wexp.at[y], k_wexp, k_wexp, along("y", other)).start()
    drains.append(lambda: sent(wexp.at[others], k_wexp))
    start_if(jnp.logical_and(s == 1, turned), cot, cot_in, k_cot, partner)
    wait_cot = local_if(jnp.logical_and(s == 1, straight), cot, cot_in, 5)

    def only(h, values, first):
        inside = jnp.logical_and(lanes >= first + h * HEAD, lanes < first + (h + 1) * HEAD)
        return jnp.where(inside, values.astype(F32), 0.0)

    def scatter(number, j, term, base):
        part_send[number, j] = term.astype(BF16).reshape(N, Q, D)
        deal("y", part_send.at[number, j], part_recv.at[number, j], base)

    def collected(number, j, base):
        total = part_send[number, j, y].astype(F32)
        arrived(part_recv.at[number, j], base)
        for d in order:
            total = total + part_recv[number, j, near(y, d)].astype(F32)
        return total

    def pair(ref, i):
        return ref[2 * i : 2 * i + 2].reshape(2 * M, WQ)

    wout[0 : WQ - DH] = jnp.zeros((WQ - DH, D), BF16)
    wait_wout()
    k_po = [block_of() for _ in streams]
    for i in range(S):
        for side in range(2):
            arrived(kv.at[i], k_kv[2 * i + side], side)
        allowed = kpos[...] <= qpos[...]
        keys = kv[i, :, :, :, 0:WQ].reshape(2 * N * M, WQ)
        values = kv[i, :, :, :, W:WKV].reshape(2 * N * M, WQ)
        total = jnp.zeros((2 * M, WQ), F32)
        for h in range(heads):
            scores = mm_nt(only(h, pair(q_all, i), 0).astype(BF16), keys)
            scores = jnp.where(allowed, scores, -1e30)
            raised = jnp.exp(scores - jnp.max(scores, axis=-1, keepdims=True))
            part = raised * (1.0 / jnp.sum(raised, axis=-1, keepdims=True))
            probs[i * heads + h] = part
            total = total + only(h, mm(part.astype(BF16), values), WQ - DH)
        low = total.astype(BF16)
        mixed[2 * i : 2 * i + 2] = low.reshape(2, M, WQ)
        term = mm(low, wout[...])
        for side in range(2):
            scatter(0, 2 * i + side, term[side * M : (side + 1) * M], k_po[2 * i + side])

    k_n2 = [block_of() for _ in streams]
    for j in streams:
        state = u_in[j].astype(F32) + (collected(0, j, k_po[j]) + b_out)
        hidden[j] = state
        normal, _ = normalize(state)
        n2[j, y] = (normal * gain2 + shift2).astype(BF16)
        spread("y", n2.at[j], k_n2[j])

    wait_wexp()
    wait_wred()
    arrived(wexp, k_wexp)
    k_ff = [block_of() for _ in streams]
    for j in streams:
        arrived(n2.at[j], k_n2[j])
        before = mm(n2[j].reshape(M, D), wexp[...].reshape(D, F)) + bexp_in[...].astype(F32)
        square = before * before
        bent = jnp.tanh(GELU_SCALE * (before + GELU_CUBE * (square * before)))
        side = 0.5 * (1.0 + bent)
        low = (before * side).astype(BF16)
        active[j] = low
        slope[j] = side + 0.5 * before * (1.0 - bent * bent) * (
            GELU_SCALE * (1.0 + 3.0 * GELU_CUBE * square)
        )
        scatter(1, j, mm(low, wred[...]), k_ff[j])

    for j in streams:
        result = hidden[j] + (collected(1, j, k_ff[j]) + b_reduce)
        y_low[j] = result.astype(BF16)
        start_if(s == 0, y_low.at[j], u_in.at[j], k_u[j], sibling)

    def turn(index):
        return lax.rem(lax.rem(index, N) + lax.div(index, N), N)

    def piece(index):
        return turn(index) * N + lax.div(index, N)

    mine = piece(c)
    owner = turn(c)
    home = owner == y

    def pool(src, dst, slot):
        dst[c] = src[mine]

        @pl.loop(1, NN)
        def _(d):
            other = near_ctx(d)
            remote(src.at[piece(other)], dst.at[c], slot, slot, {"ctx": other}).start()

    def pooled(dst, slot):
        landed(dst.at[rest_ctx], slot)
        total = dst[0].astype(F32)
        for other in range(1, NN):
            total = total + dst[other].astype(F32)
        return total.astype(BF16)

    def hand_rows(src, out, slot):
        pltpu.make_async_copy(src, out.at[mine], rsem.at[slot]).start()

        @pl.loop(1, NN)
        def _(d):
            remote(src, out.at[mine], slot, slot, {"ctx": near_ctx(d)}).start()

    def across(out, width):
        return out.at[z, :, pl.ds(pl.multiple_of(y * width, 128), width)]

    def hand_across(src, out, width, slot):
        dst = across(out, width)

        @pl.when(home)
        def _():
            pltpu.make_async_copy(src, dst, rsem.at[slot]).start()

        @pl.when(jnp.logical_not(home))
        def _():
            remote(src, dst, slot, slot, {"fsdp": owner}).start()

        @pl.loop(1, NN)
        def _(d):
            remote(src, dst, slot, slot, {"ctx": near_ctx(d), "fsdp": owner}).start()

    def handed(out, slot, but_one):
        @pl.when(home)
        def _():
            sent(but_one, slot)

        @pl.when(jnp.logical_not(home))
        def _():
            sent(out, slot)

    axes = (("x", "z"), ("z", "x"))

    def total_at(axis, own, received):
        total = own.astype(F32)
        for d in order:
            total = total + received[near(place[axis], d)].astype(F32)
        return total.astype(BF16)

    def reduce_feed():
        for k in (1, 0):
            landed(ff_in.at[k], k_ff_in[k])
            send_deal(axes[k][0], ff_in.at[k], ff_r.at[k], k_first[k])
        for k in (1, 0):
            first, second = axes[k]
            arrived(ff_r.at[k], k_first[k])
            ff_one[k] = total_at(first, ff_in[k, place[first]], ff_r.at[k])
            send_deal(second, ff_one.at[k], ff_two.at[k], k_second[k])
        for k in (1, 0):
            second = axes[k][1]
            arrived(ff_two.at[k], k_second[k])
            ff_sum[k, place[second]] = total_at(
                second, ff_one[k, place[second]], ff_two.at[k]
            )
            send_spread(second, ff_sum.at[k], k_third[k])
        arrived(ff_sum.at[1], k_third[1])
        for d in range(N):
            remote(
                ff_sum.at[1], out_wred.at[z], k_wred_out, k_wred_out,
                {"section": 1 - s, "ctx": near(z, d) * N + x},
            ).start()
        arrived(ff_sum.at[0], k_third[0])
        wide = out_wexp.at[:, :, pl.ds(pl.multiple_of(y * F, 128), F)]
        for d in range(N):
            remote(
                ff_sum.at[0], wide, k_wexp_out, k_wexp_out,
                {"section": 1 - s, "ctx": z * N + near(x, d), "fsdp": x},
            ).start()

    for k in range(2):
        drains.append(lambda k=k: sent(ff_in.at[k, others], k_first[k]))
        drains.append(lambda k=k: sent(ff_one.at[k, others], k_second[k]))
        drains.append(lambda k=k: sent(ff_sum.at[k, others], k_third[k]))
    drains.append(lambda: sent(out_wexp, k_wexp_out))
    drains.append(lambda: sent(out_wred, k_wred_out))

    @pl.when(jnp.logical_and(s == 1, turned))
    def _():
        landed(cot_in, k_cot)

    wait_cot()
    pl.when(s == 0)(reduce_feed)
    sm_own[...] = jnp.zeros_like(sm_own)
    sm_last[...] = jnp.zeros_like(sm_last)
    k_g = [block_of() for _ in streams]
    for j in streams:
        @pl.when(s == 1)
        def _():
            grad[j] = cot_in[j]

        @pl.when(s == 0)
        def _():
            landed(gp_in.at[j], k_gp[j])
            grad[j] = gp_in[j].astype(F32)

        low = grad[j].astype(BF16)
        g_all[j, y] = low
        spread("y", g_all.at[j], k_g[j])
        sm_own[5:6] += column_sums(low)

    start_if(turned, y_low, out_y, k_y, partner)
    wait_y = local_if(straight, y_low, out_y, 6)

    k_gf = [block_of() for _ in streams]
    for j in streams:
        arrived(g_all.at[j], k_g[j])
        low = (mm_nt(g_all[j].reshape(M, D), wred[...]) * slope[j]).astype(BF16)
        gb_all[j] = low
        scatter(2, j, mm_nt(low, wexp[...].reshape(D, F)), k_gf[j])

    g_rows = g_all[...].reshape(J * M, D)
    gb_rows = gb_all[...].reshape(J * M, F)
    ff_s[1] = (
        mm_tn(active[...].reshape(J * M, F), g_rows).astype(BF16).reshape(N, N, F // NN, D)
    )
    start(ff_s.at[1], ff_in.at[1], k_ff_in[1], sibling)
    ff_s[0] = mm_tn(n2[...].reshape(J * M, D), gb_rows).astype(BF16).reshape(N, N, D // NN, F)
    start(ff_s.at[0], ff_in.at[0], k_ff_in[0], sibling)
    sm_own[10:11] = column_sums(gb_rows)

    k_ga = [block_of() for _ in streams]
    for j in streams:
        grad_two = collected(2, j, k_gf[j])
        normal, factor = normalize(hidden[j])
        grad_hidden = grad[j] + norm_back(grad_two, normal, factor, gain2)
        grad[j] = grad_hidden
        low = grad_hidden.astype(BF16)
        ga_all[j, y] = low
        spread("y", ga_all.at[j], k_ga[j])
        sm_own[2:3] += column_sums(grad_two * normal)
        sm_own[3:4] += column_sums(grad_two)
        sm_own[4:5] += column_sums(low)

    k_dkv = [block_of() for _ in range(S)]
    for i in range(S):
        for j in (2 * i, 2 * i + 1):
            arrived(ga_all.at[j], k_ga[j])
            gm_all[j] = mm_nt(ga_all[j].reshape(M, D), wout[...]).astype(BF16)
        keys = kv[i, :, :, :, 0:WQ].reshape(2 * N * M, WQ)
        values = kv[i, :, :, :, W:WKV].reshape(2 * N * M, WQ)
        total = jnp.zeros((2 * M, WQ), F32)
        total_k = jnp.zeros((2 * N * M, WQ), F32)
        total_v = jnp.zeros((2 * N * M, WQ), F32)
        for h in range(heads):
            part = probs[i * heads + h]
            mixed_head = only(h, pair(gm_all, i), WQ - DH).astype(BF16)
            grad_probs = mm_nt(mixed_head, values)
            inner = jnp.sum(part * grad_probs, axis=-1, keepdims=True)
            grad_scores = (part * (grad_probs - inner)).astype(BF16)
            total = total + only(h, mm(grad_scores, keys), 0)
            total_k = total_k + mm_tn(grad_scores, only(h, pair(q_all, i), 0).astype(BF16))
            total_v = total_v + mm_tn(part.astype(BF16), mixed_head)
        shared = total_k[:, W:WQ] + total_v[:, 0:W]
        for lane, terms in ((0, total_k[:, 0:W]), (W, shared), (WQ, total_v[:, W:WQ])):
            dkv_send[i, :, :, :, lane : lane + W] = terms.astype(BF16).reshape(N, 2, M, W)
        deal("x", dkv_send.at[i], dkv_recv.at[i], k_dkv[i])
        low = (total.astype(BF16).astype(F32) * 0.125).astype(BF16)
        dq_all[2 * i : 2 * i + 2] = low.reshape(2, M, WQ)

    n1_rows = n1[...].reshape(J * M, D)
    dq_rows = dq_all[...].reshape(J * M, WQ)
    sm_own[8:9, 0:DH] = column_sums(dq_rows)[:, 0:DH]
    grad_q = mm_tn(n1_rows, dq_rows)
    grad_o = mm_tn(ga_all[...].reshape(J * M, D), mixed[...].reshape(J * M, WQ))
    qo_s[:, :, 0:W] = grad_q[:, 0:W].astype(BF16).reshape(NN, D // NN, W)
    qo_s[:, :, W:WQ] = (grad_q[:, W:WQ] + grad_o[:, 0:W]).astype(BF16).reshape(NN, D // NN, W)
    qo_s[:, :, WQ:WKV] = grad_o[:, W:WQ].astype(BF16).reshape(NN, D // NN, W)
    k_qo, k_kv_pool, k_q_out, k_o_out, k_kv_out = (block_of() for _ in range(5))
    pl.when(s == 0)(lambda: pool(qo_s, qo_r, k_qo))

    def reduce_qo():
        qo_sum[...] = pooled(qo_r, k_qo)
        hand_across(qo_sum.at[:, 0:WQ], out_q, WQ, k_q_out)
        hand_rows(qo_sum.at[:, W:WKV], out_out, k_o_out)


    k_gn = [block_of() for _ in streams]
    for j in streams:
        i, side = j // 2, j % 2
        if side == 0:
            arrived(dkv_recv.at[i], k_dkv[i])
        total = dkv_send[i, x, side].astype(F32)
        for d in order:
            total = total + dkv_recv[i, near(x, d), side].astype(F32)
        low = total.astype(BF16)
        dkv_all[j] = low
        scatter(
            3, j,
            mm_nt(dq_all[j], w_all[:, :, WKV : WKV + WQ].reshape(D, WQ))
            + mm_nt(low, w_all[:, :, 0:WKV].reshape(D, WKV)),
            k_gn[j],
        )

    dkv_rows = dkv_all[...].reshape(J * M, WKV)
    sm_own[9:10, 0:WKV] = column_sums(dkv_rows)
    kv_s[...] = mm_tn(n1_rows, dkv_rows).astype(BF16).reshape(NN, D // NN, WKV)

    @pl.when(s == 0)
    def _():
        pool(kv_s, kv_r, k_kv_pool)
        reduce_qo()

    sm_y[y] = sm_own[0:8]
    k_smy = block_of()
    spread("y", sm_y, k_smy)

    for j in streams:
        grad_normed = collected(3, j, k_gn[j])
        normal, factor = normalize(u_in[j].astype(F32))
        grad_input = grad[j] + norm_back(grad_normed, normal, factor, gain1)
        dx_low[j] = grad_input.astype(BF16)
        start_if(s == 1, dx_low.at[j], gp_in.at[j], k_gp[j], sibling)
        dx_buf[j] = grad_input
        sm_last[0:1] += column_sums(grad_normed * normal)
        sm_last[1:2] += column_sums(grad_normed)

    sm_ly[y] = sm_last[...]
    k_smly = block_of()
    spread("y", sm_ly, k_smly)

    @pl.when(s == 1)
    def _():
        pool(kv_s, kv_r, k_kv_pool)
        pool(qo_s, qo_r, k_qo)

    def total_of(ref):
        rows = ref[0]
        for other in range(1, N):
            rows = rows + ref[other]
        return rows

    arrived(sm_y, k_smy)
    sm_x[x, 0:8] = total_of(sm_y)
    sm_x[x, 8:16] = sm_own[8:16]
    k_smx = block_of()
    spread("x", sm_x, k_smx)
    kv_sum[...] = pooled(kv_r, k_kv_pool)
    hand_across(kv_sum, out_kv, WKV, k_kv_out)
    arrived(sm_ly, k_smly)
    sm_lx[x] = total_of(sm_ly)
    k_smlx = block_of()
    spread("x", sm_lx, k_smlx)
    start_if(turned, dx_buf, out_dx, k_dx, partner)
    wait_dx = local_if(straight, dx_buf, out_dx, 9)
    arrived(sm_x, k_smx)
    sm_z[z] = total_of(sm_x)
    k_smz = block_of()
    spread("z", sm_z, k_smz)
    arrived(sm_lx, k_smlx)
    sm_lz[z] = total_of(sm_lx)
    k_smlz = block_of()
    spread("z", sm_lz, k_smlz)

    @pl.when(s == 1)
    def _():
        reduce_qo()
        reduce_feed()

    arrived(sm_z, k_smz)
    arrived(sm_lz, k_smlz)
    out_small[0:8] = total_of(sm_lz)
    out_small[8:24] = total_of(sm_z)
    drains.append(lambda: sent(qo_s.at[rest_ctx], k_qo))
    drains.append(lambda: sent(kv_s.at[rest_ctx], k_kv_pool))
    drains.append(lambda: handed(out_kv, k_kv_out, kv_r.at[rest_ctx]))
    drains.append(lambda: handed(out_q, k_q_out, qo_r.at[rest_ctx, :, pl.ds(0, WQ)]))
    drains.append(lambda: sent(out_out.at[rest_ctx], k_o_out))

    for ref, slot in (
        (out_kv, k_kv_out), (out_q, k_q_out), (out_out, k_o_out), (out_wexp, k_wexp_out),
        (out_wred, k_wred_out),
    ):
        landed(ref, slot)

    @pl.when(turned)
    def _():
        landed(out_y, k_y)
        landed(out_dx, k_dx)

    for wait in (wait_y, wait_dx):
        wait()
    for drain in drains:
        drain()


def bias_at(values, lane, width, first):
    size = values.shape[1]
    row = lax.broadcasted_iota(jnp.int32, (size, width), 0)
    col = lax.broadcasted_iota(jnp.int32, (size, width), 1)
    put = jnp.where(row + first == col + lane, 1.0, 0.0).astype(BF16)
    wide = jnp.broadcast_to(values, (16, size)).astype(BF16)
    return mm(wide, put)[0:1]


def shards(
    tokens, cotangent, block_order, first_gain, first_shift, w_query, b_query, w_key, w_value,
    b_value, w_out, b_out, second_gain, second_shift, w_expand, b_expand, w_reduce, b_reduce,
):
    N = lax.axis_size("fsdp")
    S, R, D = tokens.shape
    F = w_reduce.shape[1]
    DH = D // N
    W = 2 * DH // 3
    WQ, WKV = 2 * W, 3 * W
    J, Q = 2 * S, R // 2
    NN, M = N * N, N * Q
    heads = DH // HEAD
    y = lax.axis_index("fsdp")

    rows = jnp.concatenate(
        [first_gain, first_shift, second_gain, second_shift, b_out, b_reduce, b_query, b_value]
    ).astype(F32)
    rows = jnp.pad(rows, ((0, 8), (0, 0)))

    def shape(dims, dtype):
        return jax.ShapeDtypeStruct(dims, dtype)

    vmem = pl.BlockSpec(memory_space=pltpu.VMEM)
    smem = pl.BlockSpec(memory_space=pltpu.SMEM)
    hbm = pl.BlockSpec(memory_space=pl.ANY)
    V = pltpu.VMEM
    slab = V((J, N, Q, D), BF16)
    whole_sum, part_sum = V((2, N, N, D // NN, D), BF16), V((2, N, D // NN, D), BF16)
    rows_low, rows_full = V((J, Q, D), BF16), V((J, Q, D), F32)
    outs = pl.pallas_call(
        functools.partial(kernel, N, J, Q, D, F),
        out_shape=(
            shape((J, Q, D), BF16),
            shape((J, Q, D), F32),
            shape((N, D // NN, N * WKV), BF16),
            shape((N, D // NN, N * WQ), BF16),
            shape((NN, D // NN, WQ), BF16),
            shape((N, D // NN, N * F), BF16),
            shape((N, N, F // NN, D), BF16),
            shape((24, D), F32),
        ),
        in_specs=[
            hbm, hbm, smem, vmem, vmem, hbm, hbm, hbm, hbm, hbm, hbm,
        ],
        out_specs=(hbm, hbm, hbm, hbm, hbm, hbm, hbm, vmem),
        scratch_shapes=[
            rows_low, rows_full, rows_low, rows_low, rows_full, rows_low, V((N, 8, D), F32),
            V((1, 2 * N * M), jnp.int32), V((2 * M, 1), jnp.int32),
            V((DH, D), BF16), V((DH, D), BF16), V((DH, D), BF16),
            V((N, DH, WKV + WQ), BF16), V((N, DH, WKV + WQ), BF16), V((N, DH, F), BF16),
            V((F, D), BF16), V((WQ, D), BF16),
            slab, slab, slab, slab,
            V((J, M, F), BF16), V((J, M, F), BF16), V((J, M, F), F32),
            V((J, M, WQ), BF16), V((S, N, 2, M, WKV), BF16),
            V((S * heads, 2 * M, 2 * N * M), F32),
            V((J, M, WQ), BF16), V((J, M, WQ), BF16), V((J, M, WQ), BF16), V((J, M, WKV), BF16),
            V((S, N, 2, M, WKV), BF16), V((S, N, 2, M, WKV), BF16),
            V((4, J, N, Q, D), BF16), V((4, J, N, Q, D), BF16), rows_full, rows_full,
            whole_sum, whole_sum, whole_sum, part_sum, part_sum, part_sum,
            V((NN, D // NN, WKV), BF16), V((NN, D // NN, WKV), BF16), V((D // NN, WKV), BF16),
            V((NN, D // NN, WKV), BF16), V((NN, D // NN, WKV), BF16), V((D // NN, WKV), BF16),
            V((N, 8, D), F32), V((N, 16, D), F32), V((N, 16, D), F32), V((16, D), F32),
            V((N, 8, D), F32), V((N, 8, D), F32), V((N, 8, D), F32), V((8, D), F32),
            pltpu.SemaphoreType.DMA((SEMS,)),
            pltpu.SemaphoreType.DMA((SEMS,)),
            pltpu.SemaphoreType.DMA((24,)),
            pltpu.SemaphoreType.REGULAR,
        ],
        compiler_params=pltpu.CompilerParams(
            collective_id=0, has_side_effects=True, vmem_limit_bytes=60 * 1024 * 1024
        ),
        name="layers",
    )(
        tokens.reshape(J, Q, D), cotangent.reshape(J, Q, D), block_order, rows, b_expand, w_query[0], w_key[0], w_value[0], w_out[0],
        w_expand[0], w_reduce[0],
    )
    out_y, out_dx, g_kv, g_q, g_out, g_exp, g_red, small = outs
    g_kv = g_kv.reshape(DH, N * WKV)
    g_q = g_q.reshape(DH, N * WQ)

    def whole(parts, width, first):
        pieces = [parts[:, b * width + first : b * width + first + DH] for b in range(N)]
        return jnp.concatenate(pieces, axis=1).astype(F32)[None]

    mine = lax.dynamic_slice(small, (0, y * DH), (16, DH))
    return (
        out_y.reshape(1, S, R, D),
        out_dx.reshape(1, S, R, D),
        mine[0:1],
        mine[1:2],
        whole(g_q, WQ, 0),
        small[16:17, 0:DH],
        whole(g_kv, WKV, 0),
        whole(g_kv, WKV, DH),
        small[17:18, DH:WKV],
        g_out.reshape(D, WQ)[:, WQ - DH :].T.astype(F32)[None],
        mine[12:13],
        mine[10:11],
        mine[11:12],
        g_exp.reshape(1, DH, N * F).astype(F32),
        small[18:19, 0:F],
        g_red.reshape(1, F, D).astype(F32),
        mine[13:14],
    )


def solution(mesh):
    vector = P("section", "fsdp")
    matrix = P("section", "fsdp", None)
    return jax.shard_map(
        shards,
        mesh=mesh,
        in_specs=(
            P("fsdp", "ctx", None), P("fsdp", "ctx", None), P(),
            vector, vector, matrix, vector, matrix, matrix, vector, matrix, vector, vector, vector,
            matrix, vector, matrix, vector,
        ),
        out_specs=(
            P("section", "fsdp", "ctx", None), P("section", "fsdp", "ctx", None),
            vector, vector, matrix, vector, matrix, matrix, vector, matrix, vector, vector, vector,
            matrix, vector, matrix, vector,
        ),
        check_vma=False,
    )
```

```python
import functools

import jax
import jax.numpy as jnp
from jax import lax
from jax.experimental import pallas as pl
from jax.experimental.pallas import tpu as pltpu
from jax.sharding import PartitionSpec as P

HEAD = 64
EPSILON = 1e-05
F32 = jnp.float32
BF16 = jnp.bfloat16
MESH = pl.DeviceIdType.MESH
GELU_SCALE = 0.7978845608028654
GELU_CUBE = 0.044715
SEMS = 80


def mm(left, right):
    return jnp.dot(left, right, preferred_element_type=F32)


def mm_nt(left, right):
    return lax.dot_general(left, right, (((1,), (1,)), ((), ())), preferred_element_type=F32)


def mm_tn(left, right):
    return lax.dot_general(left, right, (((0,), (0,)), ((), ())), preferred_element_type=F32)


def normalize(values):
    average = jnp.mean(values, axis=-1, keepdims=True)
    centered = values - average
    variance = jnp.mean(centered * centered, axis=-1, keepdims=True)
    factor = lax.rsqrt(variance + EPSILON)
    return centered * factor, factor


def norm_back(grad, normal, factor, gain):
    scaled = grad * gain
    return factor * (
        scaled
        - jnp.mean(scaled, axis=-1, keepdims=True)
        - normal * jnp.mean(scaled * normal, axis=-1, keepdims=True)
    )


def column_sums(values):
    return jnp.sum(values.astype(F32), axis=0, keepdims=True)


def kernel(
    N, J, Q, D, F,
    tok, cot, order_in, rows_in, bexp_in, wq_in, wk_in, wv_in, wout_in, wexp_in, wred_in,
    out_y, out_dx, out_kv, out_q, out_out, out_wexp, out_wred, out_small,
    u_in, cot_in, gp_in, y_low, dx_buf, dx_low, vecs, kpos, qpos,
    wq, wk, wv, w_send, w_all, wexp, wred, wout, n1, n2, g_all, ga_all, gb_all, active, slope,
    q_all, kv, probs, mixed, gm_all, dq_all, dkv_all, dkv_send, dkv_recv,
    part_send, part_recv, hidden, grad,
    ff_s, ff_in, ff_r, ff_one, ff_two, ff_sum, qo_s, qo_r, qo_sum, kv_s, kv_r, kv_sum,
    sm_y, sm_x, sm_z, sm_own, sm_ly, sm_lx, sm_lz, sm_last,
    ssem, rsem, lsem, go,
):
    NN = N * N
    M = N * Q
    S = J // 2
    DH = D // N
    W = 2 * DH // 3
    WQ, WKV = 2 * W, 3 * W
    heads = DH // HEAD
    s = lax.axis_index("section")
    c = lax.axis_index("ctx")
    y = lax.axis_index("fsdp")
    x = lax.rem(c, N)
    z = lax.div(c, N)
    straight = y == z
    turned = y != z
    order = tuple(sorted(range(1, N), key=lambda d: -min(d, N - d)))
    streams = range(J)
    sibling = {"section": 1 - s}
    partner = {"ctx": y * N + x, "fsdp": z}

    def near(v, d):
        return lax.rem(v + d, N)

    def near_ctx(d):
        return lax.rem(c + d, NN)

    counter = [0]

    def block_of():
        counter[0] += 1
        assert counter[0] <= SEMS
        return counter[0] - 1

    drains = []

    def remote(src, dst, send, recv, device):
        return pltpu.make_async_remote_copy(
            src_ref=src, dst_ref=dst, send_sem=ssem.at[send], recv_sem=rsem.at[recv],
            device_id=device, device_id_type=MESH,
        )

    def start(src, dst, slot, device):
        copy = remote(src, dst, slot, slot, device)
        copy.start()
        drains.append(copy.wait_send)

    def start_if(condition, src, dst, slot, device):
        copy = remote(src, dst, slot, slot, device)
        pl.when(condition)(lambda: copy.start())
        drains.append(lambda: pl.when(condition)(lambda: copy.wait_send()))

    def sent(ref, slot):
        remote(ref, ref, slot, 0, sibling).wait_send()

    def landed(dst, recv):
        remote(dst, dst, 0, recv, sibling).wait_recv()

    def local_if(condition, src, dst, slot):
        copy = pltpu.make_async_copy(src, dst, lsem.at[slot])
        pl.when(condition)(lambda: copy.start())
        return lambda: pl.when(condition)(lambda: copy.wait())

    def local(src, dst, slot):
        copy = pltpu.make_async_copy(src, dst, lsem.at[slot])
        copy.start()
        return copy.wait

    def along(axis, index):
        if axis == "y":
            return {"fsdp": index}
        if axis == "x":
            return {"ctx": z * N + index}
        return {"ctx": index * N + x}

    place = {"x": x, "y": y, "z": z}
    others = pl.ds(0, N - 1)
    rest_ctx = pl.ds(0, NN - 1)

    def send_spread(axis, ref, slot, *rest):
        me = place[axis]
        for d in order:
            at = ref.at[(me,) + rest]
            remote(at, at, slot, slot, along(axis, near(me, d))).start()

    def spread(axis, ref, slot, *rest):
        send_spread(axis, ref, slot, *rest)
        drains.append(lambda: sent(ref.at[(others,) + rest], slot))

    def arrived(ref, slot, *rest):
        landed(ref.at[(others,) + rest], slot)

    def send_deal(axis, src, dst, slot):
        me = place[axis]
        for d in order:
            other = near(me, d)
            remote(src.at[other], dst.at[me], slot, slot, along(axis, other)).start()

    def deal(axis, src, dst, slot):
        send_deal(axis, src, dst, slot)
        drains.append(lambda: sent(src.at[others], slot))

    barrier = pltpu.get_barrier_semaphore()

    def greet(device):
        pl.semaphore_signal(barrier, inc=1, device_id=device, device_id_type=MESH)

    @pl.loop(1, NN * N)
    def _(d):
        index = lax.rem(c * N + y + d, NN * N)
        greet({"ctx": lax.div(index, N), "fsdp": lax.rem(index, N)})

    @pl.loop(0, NN)
    def _(d):
        greet({"section": 1 - s, "ctx": z * N + lax.rem(d, N), "fsdp": lax.div(d, N)})

    @pl.loop(1, N)
    def _(d):
        greet({"section": 1 - s, "ctx": near(z, d) * N + x})

    greeted = NN * N - 1 + NN + N - 1
    wait_cuts = [local(a, b, 13 + j) for j, (a, b) in enumerate(((wq_in, wq), (wk_in, wk), (wv_in, wv)))]
    wait_wred = local(wred_in, wred, 0)
    wait_wout = local(wout_in, wout.at[pl.ds(WQ - DH, DH)], 1)

    put = (
        lax.broadcasted_iota(jnp.int32, (DH, D), 0) + y * DH
        == lax.broadcasted_iota(jnp.int32, (DH, D), 1)
    )
    vecs[y] = mm(rows_in[...].astype(BF16), jnp.where(put, 1.0, 0.0).astype(BF16))[0:8]

    def picker(width, shift, first):
        row = lax.broadcasted_iota(jnp.int32, (WQ, width), 0)
        col = lax.broadcasted_iota(jnp.int32, (WQ, width), 1)
        inside = jnp.logical_and(col >= first, col < first + DH)
        return jnp.where(
            jnp.logical_and(row - shift == col - first, inside), 1.0, 0.0
        ).astype(BF16)

    for wait in wait_cuts:
        wait()
    for b in range(N):
        lane = b * DH // W * W
        cut = slice(lane, lane + WQ)
        shift = b * DH - lane
        w_send[b, :, 0:WKV] = (
            mm(wk[:, cut], picker(WKV, shift, 0)) + mm(wv[:, cut], picker(WKV, shift, DH))
        ).astype(BF16)
        w_send[b, :, WKV : WKV + WQ] = mm(wq[:, cut], picker(WQ, shift, 0)).astype(BF16)
    w_all[y] = w_send[y]
    pl.semaphore_wait(barrier, greeted)

    k_u = [block_of() for _ in streams]
    k_gp = [block_of() for _ in streams]
    k_cot, k_y, k_dx, k_wexp_out, k_wred_out = (block_of() for _ in range(5))
    k_ff_in, k_first, k_second, k_third = ([block_of(), block_of()] for _ in range(4))
    k_vecs = block_of()
    spread("y", vecs, k_vecs)
    wait_u = []
    for j in streams:
        start_if(
            jnp.logical_and(s == 0, turned), tok.at[j], u_in.at[j], k_u[j], partner
        )
        wait_u.append(
            local_if(jnp.logical_and(s == 0, straight), tok.at[j], u_in.at[j], 16 + j)
        )

    @pl.when(s == 1)
    def _():
        pl.semaphore_wait(go, 1)

    k_w = block_of()
    deal("y", w_send, w_all, k_w)

    slot = lax.broadcasted_iota(jnp.int32, (1, 2 * N * M), 1)
    found = jnp.zeros_like(slot)
    for b in range(2 * NN):
        stored = 2 * (b % N * N + b // (2 * N)) + b // N % 2
        found = jnp.where(slot >= b * Q, order_in[stored] * Q - b * Q, found)
    kpos[...] = found + slot
    slot = lax.broadcasted_iota(jnp.int32, (2 * M, 1), 0)
    found = jnp.zeros_like(slot)
    for b in range(2 * N):
        found = jnp.where(
            slot >= b * Q, order_in[2 * (b % N * N + x) + b // N] * Q - b * Q, found
        )
    qpos[...] = found + slot

    arrived(vecs, k_vecs)
    params = vecs[0]
    for other in range(1, N):
        params = params + vecs[other]
    gain1, shift1, gain2, shift2, b_out, b_reduce = (params[r : r + 1] for r in range(6))
    lanes = lax.broadcasted_iota(jnp.int32, (1, WQ), 1)

    k_n1 = [block_of() for _ in streams]
    for j in streams:
        @pl.when(jnp.logical_or(s == 1, turned))
        def _():
            landed(u_in.at[j], k_u[j])

        wait_u[j]()
        normal, _ = normalize(u_in[j].astype(F32))
        n1[j, y] = (normal * gain1 + shift1).astype(BF16)
        spread("y", n1.at[j], k_n1[j])

    k_kv = [block_of() for _ in streams]
    arrived(w_all, k_w)
    b_value = bias_at(rows_in[7:8], W, WQ, DH)
    b_query = bias_at(rows_in[6:7], 0, WQ, 0)
    for j in streams:
        arrived(n1.at[j], k_n1[j])
        rows = n1[j].reshape(M, D)
        made = mm(rows, w_all[:, :, 0:WKV].reshape(D, WKV))
        kv[j // 2, x, j % 2, :, 0:W] = made[:, 0:W].astype(BF16)
        kv[j // 2, x, j % 2, :, W:WKV] = (made[:, W:WKV] + b_value).astype(BF16)
        spread("x", kv.at[j // 2], k_kv[j], j % 2)
        query = mm(rows, w_all[:, :, WKV : WKV + WQ].reshape(D, WQ)) + b_query
        q_all[j] = (query * 0.125).astype(BF16)

    k_wexp = block_of()

    def wexp_cut(b):
        return wexp_in.at[:, pl.ds(pl.multiple_of(b * F, 128), F)]

    wait_wexp = local(wexp_cut(y), wexp.at[y], 4)
    for d in order:
        other = near(y, d)
        remote(wexp_cut(other), wexp.at[y], k_wexp, k_wexp, along("y", other)).start()
    drains.append(lambda: sent(wexp.at[others], k_wexp))
    start_if(jnp.logical_and(s == 1, turned), cot, cot_in, k_cot, partner)
    wait_cot = local_if(jnp.logical_and(s == 1, straight), cot, cot_in, 5)

    def only(h, values, first):
        inside = jnp.logical_and(lanes >= first + h * HEAD, lanes < first + (h + 1) * HEAD)
        return jnp.where(inside, values.astype(F32), 0.0)

    def scatter(number, j, term, base):
        part_send[number, j] = term.astype(BF16).reshape(N, Q, D)
        deal("y", part_send.at[number, j], part_recv.at[number, j], base)

    def collected(number, j, base):
        total = part_send[number, j, y].astype(F32)
        arrived(part_recv.at[number, j], base)
        for d in order:
            total = total + part_recv[number, j, near(y, d)].astype(F32)
        return total

    def pair(ref, i):
        return ref[2 * i : 2 * i + 2].reshape(2 * M, WQ)

    wout[0 : WQ - DH] = jnp.zeros((WQ - DH, D), BF16)
    wait_wout()
    k_po = [block_of() for _ in streams]
    for i in range(S):
        for side in range(2):
            arrived(kv.at[i], k_kv[2 * i + side], side)
        allowed = kpos[...] <= qpos[...]
        keys = kv[i, :, :, :, 0:WQ].reshape(2 * N * M, WQ)
        values = kv[i, :, :, :, W:WKV].reshape(2 * N * M, WQ)
        total = jnp.zeros((2 * M, WQ), F32)
        for h in range(heads):
            scores = mm_nt(only(h, pair(q_all, i), 0).astype(BF16), keys)
            scores = jnp.where(allowed, scores, -1e30)
            raised = jnp.exp(scores - jnp.max(scores, axis=-1, keepdims=True))
            part = raised * (1.0 / jnp.sum(raised, axis=-1, keepdims=True))
            probs[i * heads + h] = part
            total = total + only(h, mm(part.astype(BF16), values), WQ - DH)
        low = total.astype(BF16)
        mixed[2 * i : 2 * i + 2] = low.reshape(2, M, WQ)
        term = mm(low, wout[...])
        for side in range(2):
            scatter(0, 2 * i + side, term[side * M : (side + 1) * M], k_po[2 * i + side])

    @pl.when(s == 0)
    def _():
        pl.semaphore_signal(go, inc=1, device_id=sibling, device_id_type=MESH)

    k_n2 = [block_of() for _ in streams]
    for j in streams:
        state = u_in[j].astype(F32) + (collected(0, j, k_po[j]) + b_out)
        hidden[j] = state
        normal, _ = normalize(state)
        n2[j, y] = (normal * gain2 + shift2).astype(BF16)
        spread("y", n2.at[j], k_n2[j])

    wait_wexp()
    wait_wred()
    arrived(wexp, k_wexp)
    k_ff = [block_of() for _ in streams]
    for j in streams:
        arrived(n2.at[j], k_n2[j])
        before = mm(n2[j].reshape(M, D), wexp[...].reshape(D, F)) + bexp_in[...].astype(F32)
        square = before * before
        bent = jnp.tanh(GELU_SCALE * (before + GELU_CUBE * (square * before)))
        side = 0.5 * (1.0 + bent)
        low = (before * side).astype(BF16)
        active[j] = low
        slope[j] = side + 0.5 * before * (1.0 - bent * bent) * (
            GELU_SCALE * (1.0 + 3.0 * GELU_CUBE * square)
        )
        scatter(1, j, mm(low, wred[...]), k_ff[j])

    for j in streams:
        result = hidden[j] + (collected(1, j, k_ff[j]) + b_reduce)
        y_low[j] = result.astype(BF16)
        start_if(s == 0, y_low.at[j], u_in.at[j], k_u[j], sibling)

    def turn(index):
        return lax.rem(lax.rem(index, N) + lax.div(index, N), N)

    def piece(index):
        return turn(index) * N + lax.div(index, N)

    mine = piece(c)
    owner = turn(c)
    home = owner == y

    def pool(src, dst, slot):
        dst[c] = src[mine]

        @pl.loop(1, NN)
        def _(d):
            other = near_ctx(d)
            remote(src.at[piece(other)], dst.at[c], slot, slot, {"ctx": other}).start()

    def pooled(dst, slot):
        landed(dst.at[rest_ctx], slot)
        total = dst[0].astype(F32)
        for other in range(1, NN):
            total = total + dst[other].astype(F32)
        return total.astype(BF16)

    def hand_rows(src, out, slot):
        pltpu.make_async_copy(src, out.at[mine], rsem.at[slot]).start()

        @pl.loop(1, NN)
        def _(d):
            remote(src, out.at[mine], slot, slot, {"ctx": near_ctx(d)}).start()

    def across(out, width):
        return out.at[z, :, pl.ds(pl.multiple_of(y * width, 128), width)]

    def hand_across(src, out, width, slot):
        dst = across(out, width)

        @pl.when(home)
        def _():
            pltpu.make_async_copy(src, dst, rsem.at[slot]).start()

        @pl.when(jnp.logical_not(home))
        def _():
            remote(src, dst, slot, slot, {"fsdp": owner}).start()

        @pl.loop(1, NN)
        def _(d):
            remote(src, dst, slot, slot, {"ctx": near_ctx(d), "fsdp": owner}).start()

    def handed(out, slot, but_one):
        @pl.when(home)
        def _():
            sent(but_one, slot)

        @pl.when(jnp.logical_not(home))
        def _():
            sent(out, slot)

    axes = (("x", "z"), ("z", "x"))

    def total_at(axis, own, received):
        total = own.astype(F32)
        for d in order:
            total = total + received[near(place[axis], d)].astype(F32)
        return total.astype(BF16)

    def reduce_feed():
        for k in (1, 0):
            landed(ff_in.at[k], k_ff_in[k])
            send_deal(axes[k][0], ff_in.at[k], ff_r.at[k], k_first[k])
        for k in (1, 0):
            first, second = axes[k]
            arrived(ff_r.at[k], k_first[k])
            ff_one[k] = total_at(first, ff_in[k, place[first]], ff_r.at[k])
            send_deal(second, ff_one.at[k], ff_two.at[k], k_second[k])
        for k in (1, 0):
            second = axes[k][1]
            arrived(ff_two.at[k], k_second[k])
            ff_sum[k, place[second]] = total_at(
                second, ff_one[k, place[second]], ff_two.at[k]
            )
            send_spread(second, ff_sum.at[k], k_third[k])
        arrived(ff_sum.at[1], k_third[1])
        for d in range(N):
            remote(
                ff_sum.at[1], out_wred.at[z], k_wred_out, k_wred_out,
                {"section": 1 - s, "ctx": near(z, d) * N + x},
            ).start()
        arrived(ff_sum.at[0], k_third[0])
        wide = out_wexp.at[:, :, pl.ds(pl.multiple_of(y * F, 128), F)]
        for d in range(N):
            remote(
                ff_sum.at[0], wide, k_wexp_out, k_wexp_out,
                {"section": 1 - s, "ctx": z * N + near(x, d), "fsdp": x},
            ).start()

    for k in range(2):
        drains.append(lambda k=k: sent(ff_in.at[k, others], k_first[k]))
        drains.append(lambda k=k: sent(ff_one.at[k, others], k_second[k]))
        drains.append(lambda k=k: sent(ff_sum.at[k, others], k_third[k]))
    drains.append(lambda: sent(out_wexp, k_wexp_out))
    drains.append(lambda: sent(out_wred, k_wred_out))

    @pl.when(jnp.logical_and(s == 1, turned))
    def _():
        landed(cot_in, k_cot)

    wait_cot()
    pl.when(s == 0)(reduce_feed)
    sm_own[...] = jnp.zeros_like(sm_own)
    sm_last[...] = jnp.zeros_like(sm_last)
    k_g = [block_of() for _ in streams]
    for j in streams:
        @pl.when(s == 1)
        def _():
            grad[j] = cot_in[j]

        @pl.when(s == 0)
        def _():
            landed(gp_in.at[j], k_gp[j])
            grad[j] = gp_in[j].astype(F32)

        low = grad[j].astype(BF16)
        g_all[j, y] = low
        spread("y", g_all.at[j], k_g[j])
        sm_own[5:6] += column_sums(low)

    start_if(turned, y_low, out_y, k_y, partner)
    wait_y = local_if(straight, y_low, out_y, 6)

    k_gf = [block_of() for _ in streams]
    for j in streams:
        arrived(g_all.at[j], k_g[j])
        low = (mm_nt(g_all[j].reshape(M, D), wred[...]) * slope[j]).astype(BF16)
        gb_all[j] = low
        scatter(2, j, mm_nt(low, wexp[...].reshape(D, F)), k_gf[j])

    g_rows = g_all[...].reshape(J * M, D)
    gb_rows = gb_all[...].reshape(J * M, F)
    ff_s[1] = (
        mm_tn(active[...].reshape(J * M, F), g_rows).astype(BF16).reshape(N, N, F // NN, D)
    )
    start(ff_s.at[1], ff_in.at[1], k_ff_in[1], sibling)
    ff_s[0] = mm_tn(n2[...].reshape(J * M, D), gb_rows).astype(BF16).reshape(N, N, D // NN, F)
    start(ff_s.at[0], ff_in.at[0], k_ff_in[0], sibling)
    sm_own[10:11] = column_sums(gb_rows)

    k_ga = [block_of() for _ in streams]
    for j in streams:
        grad_two = collected(2, j, k_gf[j])
        normal, factor = normalize(hidden[j])
        grad_hidden = grad[j] + norm_back(grad_two, normal, factor, gain2)
        grad[j] = grad_hidden
        low = grad_hidden.astype(BF16)
        ga_all[j, y] = low
        spread("y", ga_all.at[j], k_ga[j])
        sm_own[2:3] += column_sums(grad_two * normal)
        sm_own[3:4] += column_sums(grad_two)
        sm_own[4:5] += column_sums(low)

    k_dkv = [block_of() for _ in range(S)]
    for i in range(S):
        for j in (2 * i, 2 * i + 1):
            arrived(ga_all.at[j], k_ga[j])
            gm_all[j] = mm_nt(ga_all[j].reshape(M, D), wout[...]).astype(BF16)
        keys = kv[i, :, :, :, 0:WQ].reshape(2 * N * M, WQ)
        values = kv[i, :, :, :, W:WKV].reshape(2 * N * M, WQ)
        total = jnp.zeros((2 * M, WQ), F32)
        total_k = jnp.zeros((2 * N * M, WQ), F32)
        total_v = jnp.zeros((2 * N * M, WQ), F32)
        for h in range(heads):
            part = probs[i * heads + h]
            mixed_head = only(h, pair(gm_all, i), WQ - DH).astype(BF16)
            grad_probs = mm_nt(mixed_head, values)
            inner = jnp.sum(part * grad_probs, axis=-1, keepdims=True)
            grad_scores = (part * (grad_probs - inner)).astype(BF16)
            total = total + only(h, mm(grad_scores, keys), 0)
            total_k = total_k + mm_tn(grad_scores, only(h, pair(q_all, i), 0).astype(BF16))
            total_v = total_v + mm_tn(part.astype(BF16), mixed_head)
        shared = total_k[:, W:WQ] + total_v[:, 0:W]
        for lane, terms in ((0, total_k[:, 0:W]), (W, shared), (WQ, total_v[:, W:WQ])):
            dkv_send[i, :, :, :, lane : lane + W] = terms.astype(BF16).reshape(N, 2, M, W)
        deal("x", dkv_send.at[i], dkv_recv.at[i], k_dkv[i])
        low = (total.astype(BF16).astype(F32) * 0.125).astype(BF16)
        dq_all[2 * i : 2 * i + 2] = low.reshape(2, M, WQ)

    n1_rows = n1[...].reshape(J * M, D)
    dq_rows = dq_all[...].reshape(J * M, WQ)
    sm_own[8:9, 0:DH] = column_sums(dq_rows)[:, 0:DH]
    grad_q = mm_tn(n1_rows, dq_rows)
    grad_o = mm_tn(ga_all[...].reshape(J * M, D), mixed[...].reshape(J * M, WQ))
    qo_s[:, :, 0:W] = grad_q[:, 0:W].astype(BF16).reshape(NN, D // NN, W)
    qo_s[:, :, W:WQ] = (grad_q[:, W:WQ] + grad_o[:, 0:W]).astype(BF16).reshape(NN, D // NN, W)
    qo_s[:, :, WQ:WKV] = grad_o[:, W:WQ].astype(BF16).reshape(NN, D // NN, W)
    k_qo, k_kv_pool, k_q_out, k_o_out, k_kv_out = (block_of() for _ in range(5))
    pl.when(s == 0)(lambda: pool(qo_s, qo_r, k_qo))

    def reduce_qo():
        qo_sum[...] = pooled(qo_r, k_qo)
        hand_across(qo_sum.at[:, 0:WQ], out_q, WQ, k_q_out)
        hand_rows(qo_sum.at[:, W:WKV], out_out, k_o_out)


    k_gn = [block_of() for _ in streams]
    for j in streams:
        i, side = j // 2, j % 2
        if side == 0:
            arrived(dkv_recv.at[i], k_dkv[i])
        total = dkv_send[i, x, side].astype(F32)
        for d in order:
            total = total + dkv_recv[i, near(x, d), side].astype(F32)
        low = total.astype(BF16)
        dkv_all[j] = low
        scatter(
            3, j,
            mm_nt(dq_all[j], w_all[:, :, WKV : WKV + WQ].reshape(D, WQ))
            + mm_nt(low, w_all[:, :, 0:WKV].reshape(D, WKV)),
            k_gn[j],
        )

    dkv_rows = dkv_all[...].reshape(J * M, WKV)
    sm_own[9:10, 0:WKV] = column_sums(dkv_rows)
    kv_s[...] = mm_tn(n1_rows, dkv_rows).astype(BF16).reshape(NN, D // NN, WKV)

    @pl.when(s == 0)
    def _():
        pool(kv_s, kv_r, k_kv_pool)

    sm_y[y] = sm_own[0:8]
    k_smy = block_of()
    spread("y", sm_y, k_smy)

    for j in streams:
        grad_normed = collected(3, j, k_gn[j])
        normal, factor = normalize(u_in[j].astype(F32))
        grad_input = grad[j] + norm_back(grad_normed, normal, factor, gain1)
        dx_low[j] = grad_input.astype(BF16)
        start_if(s == 1, dx_low.at[j], gp_in.at[j], k_gp[j], sibling)
        dx_buf[j] = grad_input
        sm_last[0:1] += column_sums(grad_normed * normal)
        sm_last[1:2] += column_sums(grad_normed)

    sm_ly[y] = sm_last[...]
    k_smly = block_of()
    spread("y", sm_ly, k_smly)

    @pl.when(s == 1)
    def _():
        pool(kv_s, kv_r, k_kv_pool)
        pool(qo_s, qo_r, k_qo)

    def total_of(ref):
        rows = ref[0]
        for other in range(1, N):
            rows = rows + ref[other]
        return rows

    arrived(sm_y, k_smy)
    sm_x[x, 0:8] = total_of(sm_y)
    sm_x[x, 8:16] = sm_own[8:16]
    k_smx = block_of()
    spread("x", sm_x, k_smx)
    kv_sum[...] = pooled(kv_r, k_kv_pool)
    hand_across(kv_sum, out_kv, WKV, k_kv_out)
    arrived(sm_ly, k_smly)
    sm_lx[x] = total_of(sm_ly)
    k_smlx = block_of()
    spread("x", sm_lx, k_smlx)
    start_if(turned, dx_buf, out_dx, k_dx, partner)
    wait_dx = local_if(straight, dx_buf, out_dx, 9)
    arrived(sm_x, k_smx)
    sm_z[z] = total_of(sm_x)
    k_smz = block_of()
    spread("z", sm_z, k_smz)
    arrived(sm_lx, k_smlx)
    sm_lz[z] = total_of(sm_lx)
    k_smlz = block_of()
    spread("z", sm_lz, k_smlz)

    reduce_qo()
    pl.when(s == 1)(reduce_feed)

    arrived(sm_z, k_smz)
    arrived(sm_lz, k_smlz)
    out_small[0:8] = total_of(sm_lz)
    out_small[8:24] = total_of(sm_z)
    drains.append(lambda: sent(qo_s.at[rest_ctx], k_qo))
    drains.append(lambda: sent(kv_s.at[rest_ctx], k_kv_pool))
    drains.append(lambda: handed(out_kv, k_kv_out, kv_r.at[rest_ctx]))
    drains.append(lambda: handed(out_q, k_q_out, qo_r.at[rest_ctx, :, pl.ds(0, WQ)]))
    drains.append(lambda: sent(out_out.at[rest_ctx], k_o_out))

    for ref, slot in (
        (out_kv, k_kv_out), (out_q, k_q_out), (out_out, k_o_out), (out_wexp, k_wexp_out),
        (out_wred, k_wred_out),
    ):
        landed(ref, slot)

    @pl.when(turned)
    def _():
        landed(out_y, k_y)
        landed(out_dx, k_dx)

    for wait in (wait_y, wait_dx):
        wait()
    for drain in drains:
        drain()


def bias_at(values, lane, width, first):
    size = values.shape[1]
    row = lax.broadcasted_iota(jnp.int32, (size, width), 0)
    col = lax.broadcasted_iota(jnp.int32, (size, width), 1)
    put = jnp.where(row + first == col + lane, 1.0, 0.0).astype(BF16)
    wide = jnp.broadcast_to(values, (16, size)).astype(BF16)
    return mm(wide, put)[0:1]


def shards(
    tokens, cotangent, block_order, first_gain, first_shift, w_query, b_query, w_key, w_value,
    b_value, w_out, b_out, second_gain, second_shift, w_expand, b_expand, w_reduce, b_reduce,
):
    N = lax.axis_size("fsdp")
    S, R, D = tokens.shape
    F = w_reduce.shape[1]
    DH = D // N
    W = 2 * DH // 3
    WQ, WKV = 2 * W, 3 * W
    J, Q = 2 * S, R // 2
    NN, M = N * N, N * Q
    heads = DH // HEAD
    y = lax.axis_index("fsdp")

    rows = jnp.concatenate(
        [first_gain, first_shift, second_gain, second_shift, b_out, b_reduce, b_query, b_value]
    ).astype(F32)
    rows = jnp.pad(rows, ((0, 8), (0, 0)))

    def shape(dims, dtype):
        return jax.ShapeDtypeStruct(dims, dtype)

    vmem = pl.BlockSpec(memory_space=pltpu.VMEM)
    smem = pl.BlockSpec(memory_space=pltpu.SMEM)
    hbm = pl.BlockSpec(memory_space=pl.ANY)
    V = pltpu.VMEM
    slab = V((J, N, Q, D), BF16)
    whole_sum, part_sum = V((2, N, N, D // NN, D), BF16), V((2, N, D // NN, D), BF16)
    rows_low, rows_full = V((J, Q, D), BF16), V((J, Q, D), F32)
    outs = pl.pallas_call(
        functools.partial(kernel, N, J, Q, D, F),
        out_shape=(
            shape((J, Q, D), BF16),
            shape((J, Q, D), F32),
            shape((N, D // NN, N * WKV), BF16),
            shape((N, D // NN, N * WQ), BF16),
            shape((NN, D // NN, WQ), BF16),
            shape((N, D // NN, N * F), BF16),
            shape((N, N, F // NN, D), BF16),
            shape((24, D), F32),
        ),
        in_specs=[
            hbm, hbm, smem, vmem, vmem, hbm, hbm, hbm, hbm, hbm, hbm,
        ],
        out_specs=(hbm, hbm, hbm, hbm, hbm, hbm, hbm, vmem),
        scratch_shapes=[
            rows_low, rows_full, rows_low, rows_low, rows_full, rows_low, V((N, 8, D), F32),
            V((1, 2 * N * M), jnp.int32), V((2 * M, 1), jnp.int32),
            V((DH, D), BF16), V((DH, D), BF16), V((DH, D), BF16),
            V((N, DH, WKV + WQ), BF16), V((N, DH, WKV + WQ), BF16), V((N, DH, F), BF16),
            V((F, D), BF16), V((WQ, D), BF16),
            slab, slab, slab, slab,
            V((J, M, F), BF16), V((J, M, F), BF16), V((J, M, F), F32),
            V((J, M, WQ), BF16), V((S, N, 2, M, WKV), BF16),
            V((S * heads, 2 * M, 2 * N * M), F32),
            V((J, M, WQ), BF16), V((J, M, WQ), BF16), V((J, M, WQ), BF16), V((J, M, WKV), BF16),
            V((S, N, 2, M, WKV), BF16), V((S, N, 2, M, WKV), BF16),
            V((4, J, N, Q, D), BF16), V((4, J, N, Q, D), BF16), rows_full, rows_full,
            whole_sum, whole_sum, whole_sum, part_sum, part_sum, part_sum,
            V((NN, D // NN, WKV), BF16), V((NN, D // NN, WKV), BF16), V((D // NN, WKV), BF16),
            V((NN, D // NN, WKV), BF16), V((NN, D // NN, WKV), BF16), V((D // NN, WKV), BF16),
            V((N, 8, D), F32), V((N, 16, D), F32), V((N, 16, D), F32), V((16, D), F32),
            V((N, 8, D), F32), V((N, 8, D), F32), V((N, 8, D), F32), V((8, D), F32),
            pltpu.SemaphoreType.DMA((SEMS,)),
            pltpu.SemaphoreType.DMA((SEMS,)),
            pltpu.SemaphoreType.DMA((24,)),
            pltpu.SemaphoreType.REGULAR,
        ],
        compiler_params=pltpu.CompilerParams(
            collective_id=0, has_side_effects=True, vmem_limit_bytes=60 * 1024 * 1024
        ),
        name="layers",
    )(
        tokens.reshape(J, Q, D), cotangent.reshape(J, Q, D), block_order, rows, b_expand, w_query[0], w_key[0], w_value[0], w_out[0],
        w_expand[0], w_reduce[0],
    )
    out_y, out_dx, g_kv, g_q, g_out, g_exp, g_red, small = outs
    g_kv = g_kv.reshape(DH, N * WKV)
    g_q = g_q.reshape(DH, N * WQ)

    def whole(parts, width, first):
        pieces = [parts[:, b * width + first : b * width + first + DH] for b in range(N)]
        return jnp.concatenate(pieces, axis=1).astype(F32)[None]

    mine = lax.dynamic_slice(small, (0, y * DH), (16, DH))
    return (
        out_y.reshape(1, S, R, D),
        out_dx.reshape(1, S, R, D),
        mine[0:1],
        mine[1:2],
        whole(g_q, WQ, 0),
        small[16:17, 0:DH],
        whole(g_kv, WKV, 0),
        whole(g_kv, WKV, DH),
        small[17:18, DH:WKV],
        g_out.reshape(D, WQ)[:, WQ - DH :].T.astype(F32)[None],
        mine[12:13],
        mine[10:11],
        mine[11:12],
        g_exp.reshape(1, DH, N * F).astype(F32),
        small[18:19, 0:F],
        g_red.reshape(1, F, D).astype(F32),
        mine[13:14],
    )


def solution(mesh):
    vector = P("section", "fsdp")
    matrix = P("section", "fsdp", None)
    return jax.shard_map(
        shards,
        mesh=mesh,
        in_specs=(
            P("fsdp", "ctx", None), P("fsdp", "ctx", None), P(),
            vector, vector, matrix, vector, matrix, matrix, vector, matrix, vector, vector, vector,
            matrix, vector, matrix, vector,
        ),
        out_specs=(
            P("section", "fsdp", "ctx", None), P("section", "fsdp", "ctx", None),
            vector, vector, matrix, vector, matrix, matrix, vector, matrix, vector, vector, vector,
            matrix, vector, matrix, vector,
        ),
        check_vma=False,
    )
```
